32 devices in a mesh: px: 4 (over z), py: 4 (over y, core), ch: 2 (over x).
Axes of the slice: x: 2, y: 2, z: 4, core: 2. Of those that a mesh axis runs over, the one named last changes fastest.
Arguments:
- features: bfloat16 [128, 12, 4, 4, 1024], P('ch', None, 'py', 'px'), may hold values from -6 to 6
- cotangent: bfloat16 [128, 12, 4, 4, 1024], P('ch', None, 'py', 'px'), may hold values from -6 to 6
- weight: bfloat16 [3, 3, 128, 128], replicated, may hold values from -0.1875 to 0.1875
- edge_table: int32 [12, 4, 3], replicated, may hold values from 0 to 11, as said below
- corner_table: int32 [12, 4, 2], replicated, may hold values from 0 to 11, as said below
Outputs:
- activation: bfloat16 [128, 12, 4, 4, 1024], P('ch', None, 'py', 'px')
- input_grad: bfloat16 [128, 12, 4, 4, 1024], P('ch', None, 'py', 'px')
The draws below stay inside these ranges and needn't reach their ends.
Inputs may be any that keep to these rules, and one draw needn't show every extreme that they name: edge_table[f, e] = (g, s, r): beyond edge e of face f lie the pixels of side s of face g, in reverse order if r = 1; every side of every face is named exactly once, and if (f, e) names (g, s) then (g, s) names (f, e) with the same r. corner_table[f, c] = (h, q): corner c of face f takes corner pixel q of face h; in each corner column every face appears once, and each q appears 12 times.
All inputs are finite; a program needn't handle non-finite values.
Results may differ from the reference program's by a relative error of at most 0.0049.
Values may be sent and summed in bfloat16 or wider, within the bound.
No kernel may reach another device: no remote copies, remote signals or barrier semaphores. Data moves between devices by JAX's collectives and lax.ppermute only.
A program may use at most 192 MiB of HBM per device.

```python
import jax
import jax.numpy as jnp
from jax import lax

C = 128
FACES = 12
RB = 32
RA = 32
TILE = 1024
N_PX = 4
N_PY = 4


def draw_edge_table(key, part):
    order = jax.random.permutation(jax.random.fold_in(key, 11), FACES * 4)
    firsts = order[0::2]
    seconds = order[1::2]
    partner = jnp.zeros((FACES * 4,), jnp.int32).at[firsts].set(seconds).at[seconds].set(firsts)
    pair_flip = jax.random.randint(jax.random.fold_in(key, 12), (FACES * 2,), 0, 2)
    flips = jnp.zeros((FACES * 4,), jnp.int32).at[firsts].set(pair_flip).at[seconds].set(pair_flip)
    table = jnp.stack([partner // 4, partner % 4, flips], axis=1).reshape(FACES, 4, 3)
    return table.astype(jnp.int32)


def draw_corner_table(key, part):
    sources = jnp.stack([jax.random.permutation(jax.random.fold_in(key, 20 + corner_num), FACES) for corner_num in range(4)], axis=1)
    pixels = (jax.random.permutation(jax.random.fold_in(key, 30), FACES * 4) % 4).reshape(FACES, 4)
    return jnp.stack([sources, pixels], axis=2).astype(jnp.int32)


def levels(stream_key, shape, pieces, smallest, high):
    gain, own = 1.0, jax.random.fold_in(stream_key, 6)
    for dim, blocks in pieces:
        draws = jnp.exp(jax.random.uniform(jax.random.fold_in(own, dim), (blocks,), jnp.float32, smallest / len(pieces), high / len(pieces)))
        gain = gain * jnp.repeat(draws, shape[dim] // blocks).reshape([-1 if axis == dim else 1 for axis in range(len(shape))])
    return gain


def bell_draw(own_key, extent, deviation, bound, pieces=(), held_as=jnp.bfloat16):
    gain = levels(own_key, extent, pieces, -0.22, 0.18) if pieces else 1.0
    array = jax.random.normal(own_key, extent, jnp.float32) * deviation * gain
    return jnp.minimum(jnp.maximum(array, -bound), bound).astype(held_as)


def setup_inputs(seed: int = 0) -> dict:
    key_of = jax.random.split(jax.random.key(seed), 6)
    return {
        "features": bell_draw(key_of[0], (C, FACES, N_PY, N_PX, TILE), 1.0, 6.0, ((0, 2), (2, 4), (3, 4))),
        "cotangent": bell_draw(key_of[1], (C, FACES, N_PY, N_PX, TILE), 1.0, 6.0, ((0, 2), (2, 4), (3, 4))),
        "weight": bell_draw(key_of[2], (3, 3, C, C), (9 * C) ** -0.5, 0.1875),
        "edge_table": draw_edge_table(jax.random.fold_in(key_of[5], 71), 0),
        "corner_table": draw_corner_table(jax.random.fold_in(key_of[5], 71), 0),
    }


def to_grid(blocked):
    chan_count = blocked.shape[0]
    face_count = blocked.shape[1]
    tiles_col = blocked.shape[2]
    tiles_row = blocked.shape[3]
    shaped = blocked.reshape(chan_count, face_count, tiles_col, tiles_row, RA, RB)
    shaped = jnp.transpose(shaped, (0, 1, 2, 4, 3, 5))
    return shaped.reshape(chan_count, face_count, tiles_col * RA, tiles_row * RB)


def to_blocked(grid):
    chan_count = grid.shape[0]
    face_count = grid.shape[1]
    tiles_col = grid.shape[2] // RA
    tiles_row = grid.shape[3] // RB
    shaped = grid.reshape(chan_count, face_count, tiles_col, RA, tiles_row, RB)
    shaped = jnp.transpose(shaped, (0, 1, 2, 4, 3, 5))
    return shaped.reshape(chan_count, face_count, tiles_col, tiles_row, RA * RB)


def edge_strips(lines, edge_table, corner_table):
    chan_count = lines.shape[0]
    face_count = lines.shape[1]
    side_len = lines.shape[3]
    flat_lines = lines.reshape(chan_count, face_count * 4, side_len)
    pixels = jnp.stack([lines[:, :, 0, 0], lines[:, :, 0, -1], lines[:, :, 1, 0], lines[:, :, 1, -1]], axis=2).reshape(chan_count, face_count * 4)
    corner_index = (corner_table[:, :, 0] * 4 + corner_table[:, :, 1]).astype(jnp.int32)
    corner_vals = jnp.take(pixels, corner_index, axis=1)
    strips = []
    for edge_num, start_corner, end_corner in ((0, 0, 1), (1, 2, 3), (2, 0, 2), (3, 1, 3)):
        source_row = (edge_table[:, edge_num, 0] * 4 + edge_table[:, edge_num, 1]).astype(jnp.int32)
        strip_line = jnp.take(flat_lines, source_row, axis=1)
        flipped = (edge_table[:, edge_num, 2] == 1)[None, :, None]
        strip_line = jnp.where(flipped, strip_line[:, :, ::-1], strip_line)
        strips.append(jnp.concatenate([corner_vals[:, :, start_corner:start_corner + 1], strip_line, corner_vals[:, :, end_corner:end_corner + 1]], axis=2))
    return strips


def pad_whole(field, edge_table, corner_table):
    lines = jnp.stack([field[:, :, 0, :], field[:, :, -1, :], field[:, :, :, 0], field[:, :, :, -1]], axis=2)
    strips = edge_strips(lines, edge_table, corner_table)
    padded = jnp.pad(field, ((0, 0), (0, 0), (1, 1), (1, 1)))
    padded = padded.at[:, :, 0, :].set(strips[0])
    padded = padded.at[:, :, -1, :].set(strips[1])
    padded = padded.at[:, :, :, 0].set(strips[2])
    padded = padded.at[:, :, :, -1].set(strips[3])
    return padded


def gate_outputs(preact, cotangent):
    sigmoid_val = jax.nn.sigmoid(preact)
    activation = (preact * sigmoid_val).astype(jnp.bfloat16)
    gated = (cotangent.astype(jnp.float32) * sigmoid_val * (1.0 + preact * (1.0 - sigmoid_val))).astype(jnp.bfloat16)
    return activation, gated


def reference(features, cotangent, weight, edge_table, corner_table):
    taps = weight.astype(jnp.float32)
    features = to_grid(features)
    cotangent = to_grid(cotangent)
    side_len = features.shape[2]
    feat_pad = pad_whole(features, edge_table, corner_table)

    def forward_face(operands):
        face_pad, face_cot = operands
        summed = jnp.zeros((taps.shape[2], side_len, side_len), jnp.float32)
        for tap_row in range(3):
            for tap_col in range(3):
                window = face_pad[:, tap_row:tap_row + side_len, tap_col:tap_col + side_len].astype(jnp.float32)
                summed = summed + jnp.einsum("oc,cab->oab", taps[tap_row, tap_col], window, precision=lax.Precision.HIGHEST)
        return gate_outputs(summed, face_cot)

    act_faces, gated_faces = lax.map(forward_face, (jnp.moveaxis(feat_pad, 1, 0), jnp.moveaxis(cotangent, 1, 0)))
    activation = jnp.moveaxis(act_faces, 0, 1)
    gated = jnp.moveaxis(gated_faces, 0, 1)
    grad_pad = pad_whole(gated, edge_table, corner_table)

    def backward_face(face_pad):
        summed = jnp.zeros((taps.shape[3], side_len, side_len), jnp.float32)
        for tap_row in range(3):
            for tap_col in range(3):
                window = face_pad[:, 2 - tap_row:2 - tap_row + side_len, 2 - tap_col:2 - tap_col + side_len].astype(jnp.float32)
                summed = summed + jnp.einsum("oc,oab->cab", taps[tap_row, tap_col], window, precision=lax.Precision.HIGHEST)
        return summed.astype(jnp.bfloat16)

    grad_faces = lax.map(backward_face, jnp.moveaxis(grad_pad, 1, 0))
    input_grad = jnp.moveaxis(grad_faces, 0, 1)
    return to_blocked(activation), to_blocked(input_grad)
```

```python
import jax
import jax.numpy as jnp
import numpy as np
from jax import lax
from jax.experimental import pallas as pl
from jax.experimental.pallas import tpu as pltpu
from jax.sharding import PartitionSpec as P

RB = 32
GROUP = 4
LANES = 128
VMEM_LIMIT = 48 * 1024 * 1024
STRIP_LANE = (96, 0, 32, 64)


def ring_matrix(col_len):
    mat = np.zeros((col_len * RB, LANES), np.float32)
    for b in range(RB):
        mat[b, b] = 1
        mat[(col_len - 1) * RB + b, 32 + b] = 1
    for a in range(col_len):
        mat[a * RB, 64 + a] = 1
        mat[a * RB + RB - 1, 96 + a] = 1
    return mat


def corner_matrix():
    mat = np.zeros((LANES, LANES), np.float32)
    for q, lane in enumerate((0, RB - 1, 32, 32 + RB - 1)):
        mat[lane, q] = 1
    return mat


def reverse_matrix(unit):
    mat = np.zeros((LANES, LANES), np.float32)
    for lane in range(LANES):
        mat[lane, (lane // unit) * unit + unit - 1 - lane % unit] = 1
    return mat


def spread_matrix(col_len):
    width = col_len * RB + LANES
    mat = np.zeros((LANES, width), np.float32)
    top, bottom = (col_len + 3) * RB, col_len * RB
    mat[0, top] = 1
    mat[1, top + RB - 1] = 1
    mat[2, bottom] = 1
    mat[3, bottom + RB - 1] = 1
    for a in range(col_len):
        mat[STRIP_LANE[2] + a, a * RB] = 1
        mat[STRIP_LANE[3] + a, a * RB + RB - 1] = 1
    return mat


def lane_iota(shape):
    return lax.broadcasted_iota(jnp.int32, shape, len(shape) - 1)


def emit_rings(step, steps, fields, pos_ref, ring_ref, cornsel_ref, packs_ref, shard_ref, corner_acc):
    chan = fields[0].shape[0]
    lane = lane_iota((chan, LANES))
    rings = [
        jnp.dot(field, ring_ref[...], preferred_element_type=jnp.float32) for field in fields
    ]
    for side in range(4):
        tile = jnp.zeros((chan, LANES), jnp.float32)
        for g, ring in enumerate(rings):
            moved = pltpu.roll(ring, ((g - side) * 32) % LANES, 1) if g != side else ring
            tile = jnp.where(lane // 32 == g, moved, tile)
        packs_ref[side * steps + step] = tile.astype(jnp.bfloat16)

    @pl.when(step == 0)
    def _():
        corner_acc[...] = jnp.zeros_like(corner_acc)

    for g, ring in enumerate(rings):
        picked = jnp.dot(
            ring.astype(jnp.bfloat16), cornsel_ref[...], preferred_element_type=jnp.float32
        )
        corner_acc[...] += pltpu.roll(picked, (step * GROUP + g) * 4, 1)

    @pl.when(step == steps - 1)
    def _():
        row_first = pos_ref[0] == 1
        col_first = pos_ref[1] == 1
        for q in range(steps):
            shard_ref[q] = jnp.where(row_first, packs_ref[q], packs_ref[steps + q])
            shard_ref[steps + q] = jnp.where(
                col_first, packs_ref[2 * steps + q], packs_ref[3 * steps + q]
            )
        shard_ref[2 * steps] = corner_acc[...].astype(jnp.bfloat16)


def rings_kernel(steps, pos_ref, field_ref, ring_ref, cornsel_ref, packs_ref, shard_ref, corner_acc):
    step = pl.program_id(0)
    fields = [field_ref[g] for g in range(GROUP)]
    emit_rings(step, steps, fields, pos_ref, ring_ref, cornsel_ref, packs_ref, shard_ref, corner_acc)


def whole_spec(array):
    zeros = (0,) * array.ndim
    return pl.BlockSpec(array.shape, lambda *_: zeros)


def rings_of(field, pos, ring, cornsel):
    faces, chan, tile = field.shape
    steps = faces // GROUP
    packs = jax.ShapeDtypeStruct((4 * steps, chan, LANES), jnp.bfloat16)
    shard = jax.ShapeDtypeStruct((2 * steps + 1, chan, LANES), jnp.bfloat16)
    return pl.pallas_call(
        lambda *refs: rings_kernel(steps, *refs),
        grid=(steps,),
        in_specs=[
            pl.BlockSpec(memory_space=pltpu.SMEM),
            pl.BlockSpec((GROUP, chan, tile), lambda i: (i, 0, 0)),
            whole_spec(ring),
            whole_spec(cornsel),
        ],
        out_specs=[whole_spec(packs), whole_spec(shard)],
        out_shape=[packs, shard],
        scratch_shapes=[pltpu.VMEM((chan, LANES), jnp.float32)],
        compiler_params=pltpu.CompilerParams(vmem_limit_bytes=VMEM_LIMIT),
        name="rings",
    )(pos, field, ring, cornsel)


def halo_kernel(faces, units, unit, meta_ref, lines_ref, n0, n1, n2, n3, rev_ref, halo_ref, rev_acc):
    steps = faces // GROUP
    near = (n0, n1, n2, n3)
    chan = halo_ref.shape[1]
    lane = lane_iota((chan, LANES))
    per_face = sum(units) * 3 + 8
    corner_tile = jnp.zeros((chan, LANES), jnp.float32)
    plain = []
    for f in range(faces):
        tile = jnp.zeros((chan, LANES), jnp.float32)
        flipped = jnp.zeros((chan, LANES), jnp.float32)
        at = f * per_face
        for e in range(4):
            for un in range(units[e]):
                index, shift, mode = (meta_ref[at], meta_ref[at + 1], meta_ref[at + 2])
                at += 3
                base = STRIP_LANE[e] + un * unit
                span = (lane >= base) & (lane < base + unit)
                source = jnp.where(mode == 0, near[e][f // GROUP], lines_ref[index])
                moved = pltpu.roll(source.astype(jnp.float32), shift, 1)
                tile = jnp.where(span & (mode != 2), moved, tile)
                flipped = jnp.where(span & (mode == 2), moved, flipped)
        rev_acc[f] = flipped.astype(jnp.bfloat16)
        plain.append(tile)
        for c in range(4):
            index, shift = (meta_ref[at], meta_ref[at + 1])
            at += 2
            moved = pltpu.roll(lines_ref[index].astype(jnp.float32), shift, 1)
            corner_tile = jnp.where(lane == f * 4 + c, moved, corner_tile)
    turned = jnp.dot(
        rev_acc[...].reshape(faces * chan, LANES), rev_ref[...], preferred_element_type=jnp.float32
    ).reshape(faces, chan, LANES)
    for f in range(faces):
        halo_ref[f] = (plain[f] + turned[f]).astype(jnp.bfloat16)
    halo_ref[faces] = corner_tile.astype(jnp.bfloat16)


def assemble_halo(meta, lines, near, rev, units, unit):
    chan = lines.shape[1]
    faces = near[0].shape[0] * GROUP
    halo = jax.ShapeDtypeStruct((faces + 1, chan, LANES), jnp.bfloat16)
    vmem = pl.BlockSpec(memory_space=pltpu.VMEM)
    return pl.pallas_call(
        lambda *refs: halo_kernel(faces, units, unit, *refs),
        in_specs=[pl.BlockSpec(memory_space=pltpu.SMEM)] + [vmem] * 6,
        out_specs=vmem,
        out_shape=halo,
        scratch_shapes=[pltpu.VMEM((faces, chan, LANES), jnp.bfloat16)],
        compiler_params=pltpu.CompilerParams(vmem_limit_bytes=VMEM_LIMIT),
        name="halo",
    )(meta, lines, *near, rev)


def conv_face(g, step, field_refs, halo_refs, corner_refs, taps_ref, spread_ref, stack_ref):
    chan, tile = field_refs[0].shape[1:]
    pieces = len(field_refs)
    total = chan * pieces
    width = tile + LANES
    for k in range(pieces):
        stack_ref[total + k * chan : total + (k + 1) * chan, :tile] = field_refs[k][g]
        stack_ref[total + k * chan : total + (k + 1) * chan, tile:] = halo_refs[k][g]
    halo = stack_ref[total : 2 * total, tile:].astype(jnp.float32)
    corners = jnp.concatenate([ref[0].astype(jnp.float32) for ref in corner_refs], axis=0)
    corners = pltpu.roll(corners, (LANES - (step * GROUP + g) * 4) % LANES, 1)
    lane = lane_iota((total, LANES))
    sides = jnp.where(lane < 4, corners, halo).astype(jnp.bfloat16)
    beside = jnp.dot(sides, spread_ref[...], preferred_element_type=jnp.float32)
    middle = stack_ref[total : 2 * total].astype(jnp.float32)
    col = lane_iota((total, width)) % RB
    stack_ref[:total] = jnp.where(col == 0, beside, pltpu.roll(middle, 1, 1)).astype(jnp.bfloat16)
    stack_ref[2 * total :] = jnp.where(
        col == RB - 1, beside, pltpu.roll(middle, width - 1, 1)
    ).astype(jnp.bfloat16)
    sums = jnp.dot(taps_ref[...], stack_ref[...], preferred_element_type=jnp.float32)
    above = pltpu.roll(sums[:chan], RB, 1)
    below = pltpu.roll(sums[2 * chan :], width - RB, 1)
    return (above + sums[chan : 2 * chan] + below)[:, :tile]


def forward_kernel(steps, pieces, pos_ref, *refs):
    field_refs, refs = (refs[:pieces], refs[pieces:])
    halo_refs, refs = (refs[:pieces], refs[pieces:])
    corner_refs, refs = (refs[:pieces], refs[pieces:])
    (cot_ref, taps_ref, spread_ref, ring_ref, cornsel_ref) = refs[:5]
    (act_ref, gated_ref, packs_ref, shard_ref, stack_ref, corner_acc) = refs[5:]
    step = pl.program_id(0)
    fields = []
    for g in range(GROUP):
        pre = conv_face(g, step, field_refs, halo_refs, corner_refs, taps_ref, spread_ref, stack_ref)
        sig = 1.0 / (1.0 + jnp.exp(-pre))
        act_ref[g] = (pre * sig).astype(jnp.bfloat16)
        gated = cot_ref[g].astype(jnp.float32) * sig * (1.0 + pre * (1.0 - sig))
        gated_ref[g] = gated.astype(jnp.bfloat16)
        fields.append(gated.astype(jnp.bfloat16))
    emit_rings(step, steps, fields, pos_ref, ring_ref, cornsel_ref, packs_ref, shard_ref, corner_acc)


def backward_kernel(steps, pieces, *refs):
    field_refs, refs = (refs[:pieces], refs[pieces:])
    halo_refs, refs = (refs[:pieces], refs[pieces:])
    corner_refs, refs = (refs[:pieces], refs[pieces:])
    (taps_ref, spread_ref, grad_ref, stack_ref) = refs
    step = pl.program_id(0)
    for g in range(GROUP):
        total = conv_face(
            g, step, field_refs, halo_refs, corner_refs, taps_ref, spread_ref, stack_ref
        )
        grad_ref[g] = total.astype(jnp.bfloat16)


def conv_specs(fields, halos):
    faces, chan, tile = fields[0].shape
    group = lambda i: (i, 0, 0)
    return (
        [pl.BlockSpec((GROUP, chan, tile), group) for _ in fields]
        + [pl.BlockSpec((GROUP, chan, LANES), group) for _ in halos]
        + [pl.BlockSpec((1, chan, LANES), lambda i: (faces, 0, 0)) for _ in halos]
    )


def forward(pos, fields, halos, cot, taps, spread, ring, cornsel):
    faces, chan, tile = fields[0].shape
    steps = faces // GROUP
    pieces = len(fields)
    packs = jax.ShapeDtypeStruct((4 * steps, chan, LANES), jnp.bfloat16)
    shard = jax.ShapeDtypeStruct((2 * steps + 1, chan, LANES), jnp.bfloat16)
    out = jax.ShapeDtypeStruct((faces, chan, tile), jnp.bfloat16)
    block = pl.BlockSpec((GROUP, chan, tile), lambda i: (i, 0, 0))
    return pl.pallas_call(
        lambda *refs: forward_kernel(steps, pieces, *refs),
        grid=(steps,),
        in_specs=[pl.BlockSpec(memory_space=pltpu.SMEM)]
        + conv_specs(fields, halos)
        + [block, whole_spec(taps), whole_spec(spread), whole_spec(ring), whole_spec(cornsel)],
        out_specs=[block, block, whole_spec(packs), whole_spec(shard)],
        out_shape=[out, out, packs, shard],
        scratch_shapes=[
            pltpu.VMEM((3 * chan * pieces, tile + LANES), jnp.bfloat16),
            pltpu.VMEM((chan, LANES), jnp.float32),
        ],
        compiler_params=pltpu.CompilerParams(vmem_limit_bytes=VMEM_LIMIT),
        name="forward",
    )(pos, *fields, *halos, *halos, cot, taps, spread, ring, cornsel)


def backward(fields, halos, taps, spread):
    faces, chan, tile = fields[0].shape
    steps = faces // GROUP
    pieces = len(fields)
    return pl.pallas_call(
        lambda *refs: backward_kernel(steps, pieces, *refs),
        grid=(steps,),
        in_specs=conv_specs(fields, halos) + [whole_spec(taps), whole_spec(spread)],
        out_specs=pl.BlockSpec((GROUP, chan, tile), lambda i: (i, 0, 0)),
        out_shape=jax.ShapeDtypeStruct((faces, chan, tile), jnp.bfloat16),
        scratch_shapes=[pltpu.VMEM((3 * chan * pieces, tile + LANES), jnp.bfloat16)],
        compiler_params=pltpu.CompilerParams(vmem_limit_bytes=VMEM_LIMIT),
        name="backward",
    )(*fields, *halos, *halos, taps, spread)


def halo_meta(edge_table, corner_table, row_pos, col_pos, px_count, py_count, col_len, unit):
    faces = edge_table.shape[0]
    steps = faces // GROUP
    tiles = 2 * steps + 1
    side_len = px_count * RB
    face = jnp.arange(faces)
    on_border = (col_pos == 0, col_pos == py_count - 1, row_pos == 0, row_pos == px_count - 1)

    def line_cell(g, s, at):
        along_px = s < 2
        length = jnp.where(along_px, RB, col_len)
        seg = at // length
        px_of = jnp.where(along_px, seg, jnp.where(s == 2, 0, px_count - 1))
        py_of = jnp.where(along_px, jnp.where(s == 0, 0, py_count - 1), seg)
        tile = (px_of * py_count + py_of) * tiles + jnp.where(along_px, 0, steps) + g // GROUP
        return (tile, (g % GROUP) * 32 + at % length)

    def linked(e, at):
        g, s, r = (edge_table[:, e, 0], edge_table[:, e, 1], edge_table[:, e, 2])
        return (g, s, r, jnp.where(r == 1, side_len - 1 - at, at))

    columns = []
    for e in range(4):
        start = row_pos * RB if e < 2 else col_pos * col_len
        for un in range((RB if e < 2 else col_len) // unit):
            g, s, r, at = linked(e, start + un * unit)
            tile, lane = line_cell(g, s, at - jnp.where(r == 1, unit - 1, 0))
            near_lane = (face % GROUP) * 32 + un * unit
            lane = jnp.where(on_border[e], lane, near_lane)
            tile = jnp.where(on_border[e], tile, 0)
            mode = jnp.where(on_border[e], 1 + r, 0)
            columns += [tile, (STRIP_LANE[e] + un * unit - lane) % LANES, mode]
    for c in range(4):
        down, right = (c // 2, c % 2)
        row_edge, col_edge = (down, 2 + right)
        along_row = row_pos * RB + (RB if right else -1)
        along_col = col_pos * col_len + (col_len if down else -1)
        g, s, _, at = linked(row_edge, jnp.clip(along_row, 0, side_len - 1))
        row_tile, row_lane = line_cell(g, s, at)
        g, s, _, at = linked(col_edge, jnp.clip(along_col, 0, side_len - 1))
        col_tile, col_lane = line_cell(g, s, at)
        h, q = (corner_table[:, c, 0], corner_table[:, c, 1])
        face_tile, face_lane = line_cell(h, q // 2, (q % 2) * (side_len - 1))
        diag_px = jnp.clip(row_pos + (1 if right else -1), 0, px_count - 1)
        diag_py = jnp.clip(col_pos + (1 if down else -1), 0, py_count - 1)
        diag_tile = (diag_px * py_count + diag_py) * tiles + 2 * steps
        diag_lane = face * 4 + 3 - c
        row_on, col_on = (on_border[row_edge], on_border[col_edge])
        pick = lambda both, row, col, diag: jnp.where(
            row_on & col_on, both, jnp.where(row_on, row, jnp.where(col_on, col, diag))
        )
        tile = pick(face_tile, row_tile, col_tile, diag_tile)
        lane = pick(face_lane, row_lane, col_lane, diag_lane)
        columns += [tile, (face * 4 + c - lane) % LANES]
    return jnp.stack([jnp.broadcast_to(col, (faces,)) for col in columns], axis=1).reshape(-1)


def from_others(array, ch_count):
    return [array] + [
        lax.ppermute(array, "ch", [(i, (i + k) % ch_count) for i in range(ch_count)])
        for k in range(1, ch_count)
    ]


def exchange_halo(packs, shard, meta, rev, units, unit, px_count, py_count):
    steps = packs.shape[0] // 4
    top, bottom, left, right = [packs[s * steps : (s + 1) * steps] for s in range(4)]
    up = lambda n: [(i, i + 1) for i in range(n - 1)]
    down = lambda n: [(i + 1, i) for i in range(n - 1)]
    near = (
        lax.ppermute(bottom, "py", up(py_count)),
        lax.ppermute(top, "py", down(py_count)),
        lax.ppermute(right, "px", up(px_count)),
        lax.ppermute(left, "px", down(px_count)),
    )
    lines = lax.all_gather(shard, ("px", "py"), axis=0, tiled=True)
    return assemble_halo(meta, lines, near, rev, units, unit)


def local(features, cotangent, weight, edge_table, corner_table):
    chan, faces = features.shape[:2]
    tile = features.shape[4]
    col_len = tile // RB
    unit = min(RB, col_len)
    units = (RB // unit, RB // unit, col_len // unit, col_len // unit)
    px_count, py_count, ch_count = [lax.axis_size(name) for name in ("px", "py", "ch")]
    row_pos, col_pos, ch_pos = [lax.axis_index(name) for name in ("px", "py", "ch")]
    ring = jnp.asarray(ring_matrix(col_len), jnp.bfloat16)
    cornsel = jnp.asarray(corner_matrix(), jnp.bfloat16)
    spread = jnp.asarray(spread_matrix(col_len), jnp.bfloat16)
    rev = jnp.asarray(reverse_matrix(unit), jnp.bfloat16)
    pos = jnp.stack([col_pos == 0, row_pos == 0]).astype(jnp.int32)
    meta = halo_meta(
        edge_table, corner_table, row_pos, col_pos, px_count, py_count, col_len, unit
    )

    feats = jnp.transpose(features.reshape(chan, faces, tile), (1, 0, 2))
    cot = jnp.transpose(cotangent.reshape(chan, faces, tile), (1, 0, 2))

    def blocks(array, axis):
        order = [(ch_pos - k) % ch_count for k in range(ch_count)]
        return jnp.concatenate(
            [lax.dynamic_slice_in_dim(array, at * chan, chan, axis) for at in order], axis
        )

    own_out = lax.dynamic_slice_in_dim(weight, ch_pos * chan, chan, 2)
    taps = blocks(own_out, 3).transpose(0, 2, 1, 3).reshape(3 * chan, -1)
    own_in = lax.dynamic_slice_in_dim(weight, ch_pos * chan, chan, 3)
    back_taps = blocks(own_in, 2)[::-1, ::-1].transpose(0, 3, 1, 2).reshape(3 * chan, -1)

    packs, shard = rings_of(feats, pos, ring, cornsel)
    fields = from_others(feats, ch_count)
    halo = exchange_halo(packs, shard, meta, rev, units, unit, px_count, py_count)
    halos = from_others(halo, ch_count)
    act, gated, packs, shard = forward(pos, fields, halos, cot, taps, spread, ring, cornsel)

    fields = from_others(gated, ch_count)
    halo = exchange_halo(packs, shard, meta, rev, units, unit, px_count, py_count)
    halos = from_others(halo, ch_count)
    grad = backward(fields, halos, back_taps, spread)

    shape = (chan, faces, 1, 1, tile)
    return (
        jnp.transpose(act, (1, 0, 2)).reshape(shape),
        jnp.transpose(grad, (1, 0, 2)).reshape(shape),
    )


def solution(mesh):
    spec = P("ch", None, "py", "px", None)
    return jax.shard_map(
        local,
        mesh=mesh,
        in_specs=(spec, spec, P(), P(), P()),
        out_specs=(spec, spec),
        check_vma=False,
    )
```

```python
import jax
import jax.numpy as jnp
import numpy as np
from jax import lax
from jax.experimental import pallas as pl
from jax.experimental.pallas import tpu as pltpu
from jax.sharding import PartitionSpec as P

RB = 32
GROUP = 4
LANES = 128
VMEM_LIMIT = 48 * 1024 * 1024
STRIP_LANE = (96, 0, 32, 64)


def ring_matrix(col_len):
    mat = np.zeros((col_len * RB, LANES), np.float32)
    for b in range(RB):
        mat[b, b] = 1
        mat[(col_len - 1) * RB + b, 32 + b] = 1
    for a in range(col_len):
        mat[a * RB, 64 + a] = 1
        mat[a * RB + RB - 1, 96 + a] = 1
    return mat


def corner_matrix():
    mat = np.zeros((LANES, LANES), np.float32)
    for q, lane in enumerate((0, RB - 1, 32, 32 + RB - 1)):
        mat[lane, q] = 1
    return mat


def reverse_matrix(unit):
    mat = np.zeros((LANES, LANES), np.float32)
    for lane in range(LANES):
        mat[lane, (lane // unit) * unit + unit - 1 - lane % unit] = 1
    return mat


def spread_matrix(col_len):
    width = col_len * RB + LANES
    mat = np.zeros((LANES, width), np.float32)
    top, bottom = (col_len + 3) * RB, col_len * RB
    mat[0, top] = 1
    mat[1, top + RB - 1] = 1
    mat[2, bottom] = 1
    mat[3, bottom + RB - 1] = 1
    for a in range(col_len):
        mat[STRIP_LANE[2] + a, a * RB] = 1
        mat[STRIP_LANE[3] + a, a * RB + RB - 1] = 1
    return mat


def lane_iota(shape):
    return lax.broadcasted_iota(jnp.int32, shape, len(shape) - 1)


def emit_rings(step, steps, fields, sel_ref, ring_ref, cornsel_ref, outs, packs_acc, corner_acc):
    chan = fields[0].shape[0]
    lane = lane_iota((chan, LANES))
    rings = [
        jnp.dot(field, ring_ref[...], preferred_element_type=jnp.float32) for field in fields
    ]
    for side in range(4):
        tile = jnp.zeros((chan, LANES), jnp.float32)
        for g, ring in enumerate(rings):
            moved = pltpu.roll(ring, ((g - side) * 32) % LANES, 1) if g != side else ring
            tile = jnp.where(lane // 32 == g, moved, tile)
        packs_acc[side * steps + step] = tile.astype(jnp.bfloat16)

    @pl.when(step == 0)
    def _():
        corner_acc[...] = jnp.zeros_like(corner_acc)

    for g, ring in enumerate(rings):
        picked = jnp.dot(
            ring.astype(jnp.bfloat16), cornsel_ref[...], preferred_element_type=jnp.float32
        )
        corner_acc[...] += pltpu.roll(picked, (step * GROUP + g) * 4, 1)

    @pl.when(step == steps - 1)
    def _():
        pack = 0
        for out in outs[:-1]:
            for at in range(0, out.shape[0], steps):
                base = sel_ref[pack] * steps
                for q in range(steps):
                    out[at + q] = packs_acc[base + q]
                pack += 1
        outs[-1][0] = corner_acc[...].astype(jnp.bfloat16)


def ring_outs(faces, chan, counts):
    steps = faces // GROUP
    tiles = [count * steps for count in counts] + [1]
    return [jax.ShapeDtypeStruct((n, chan, LANES), jnp.bfloat16) for n in tiles]


def ring_scratch(faces, chan):
    steps = faces // GROUP
    return [
        pltpu.VMEM((4 * steps, chan, LANES), jnp.bfloat16),
        pltpu.VMEM((chan, LANES), jnp.float32),
    ]


def rings_kernel(steps, sel_ref, field_ref, ring_ref, cornsel_ref, *refs):
    fields = [field_ref[g] for g in range(GROUP)]
    emit_rings(
        pl.program_id(0), steps, fields, sel_ref, ring_ref, cornsel_ref, refs[:-2], *refs[-2:]
    )


def whole_spec(array):
    zeros = (0,) * array.ndim
    return pl.BlockSpec(array.shape, lambda *_: zeros)


def rings_of(field, sel, ring, cornsel, counts):
    faces, chan, tile = field.shape
    steps = faces // GROUP
    outs = ring_outs(faces, chan, counts)
    return pl.pallas_call(
        lambda *refs: rings_kernel(steps, *refs),
        grid=(steps,),
        in_specs=[
            pl.BlockSpec(memory_space=pltpu.SMEM),
            pl.BlockSpec((GROUP, chan, tile), lambda i: (i, 0, 0)),
            whole_spec(ring),
            whole_spec(cornsel),
        ],
        out_specs=[whole_spec(out) for out in outs],
        out_shape=outs,
        scratch_shapes=ring_scratch(faces, chan),
        name="rings",
    )(sel, field, ring, cornsel)


def halo_kernel(faces, units, unit, *refs):
    (strip_tile, strip_shift, strip_rev, corner_at, corner_shift), refs = (refs[:5], refs[5:])
    tile_refs, (rev_ref, halo_ref, pool, turn_acc) = (refs[:-4], refs[-4:])
    chan = halo_ref.shape[1]
    lane = lane_iota((chan, LANES))
    at = 0
    for ref in tile_refs:
        pool[at : at + ref.shape[0]] = ref[...]
        at += ref.shape[0]
    corner_tile = jnp.zeros((chan, LANES), jnp.float32)
    most = max(units)
    for f in range(faces):
        tile = jnp.zeros((chan, LANES), jnp.float32)
        turned = jnp.zeros((chan, LANES), jnp.float32)
        for e in range(4):
            for un in range(units[e]):
                base = STRIP_LANE[e] + un * unit
                span = (lane >= base) & (lane < base + unit)
                entry = e * most + un
                moved = pltpu.roll(
                    pool[strip_tile[f, entry]].astype(jnp.float32), strip_shift[f, entry], 1
                )
                flip = strip_rev[f, entry] == 1
                tile = jnp.where(span & jnp.logical_not(flip), moved, tile)
                turned = jnp.where(span & flip, moved, turned)
        halo_ref[f] = tile.astype(jnp.bfloat16)
        turn_acc[f] = turned.astype(jnp.bfloat16)
        for c in range(4):
            moved = pltpu.roll(pool[corner_at[f, c]].astype(jnp.float32), corner_shift[f, c], 1)
            corner_tile = jnp.where(lane == f * 4 + c, moved, corner_tile)
    turned = jnp.dot(
        turn_acc[...].reshape(faces * chan, LANES), rev_ref[...], preferred_element_type=jnp.float32
    ).reshape(faces, chan, LANES)
    for f in range(faces):
        halo_ref[f] += turned[f].astype(jnp.bfloat16)
    halo_ref[faces] = corner_tile.astype(jnp.bfloat16)


def assemble_halo(tables, tiles, rev, faces, units, unit):
    chan = tiles[0].shape[1]
    halo = jax.ShapeDtypeStruct((faces + 1, chan, LANES), jnp.bfloat16)
    vmem = pl.BlockSpec(memory_space=pltpu.VMEM)
    smem = pl.BlockSpec(memory_space=pltpu.SMEM)
    return pl.pallas_call(
        lambda *refs: halo_kernel(faces, units, unit, *refs),
        in_specs=[smem] * len(tables) + [vmem] * (len(tiles) + 1),
        out_specs=vmem,
        out_shape=halo,
        scratch_shapes=[
            pltpu.VMEM((sum(t.shape[0] for t in tiles), chan, LANES), jnp.bfloat16),
            pltpu.VMEM((faces, chan, LANES), jnp.bfloat16),
        ],
        name="halo",
    )(*tables, *tiles, rev)


def conv_face(g, step, field_refs, halo_refs, corner_refs, taps_ref, spread_ref, stack_ref):
    chan, tile = field_refs[0].shape[1:]
    pieces = len(field_refs)
    total = chan * pieces
    width = tile + LANES
    for k in range(pieces):
        stack_ref[total + k * chan : total + (k + 1) * chan, :tile] = field_refs[k][g]
        stack_ref[total + k * chan : total + (k + 1) * chan, tile:] = halo_refs[k][g]
    halo = stack_ref[total : 2 * total, tile:].astype(jnp.float32)
    corners = jnp.concatenate([ref[0].astype(jnp.float32) for ref in corner_refs], axis=0)
    corners = pltpu.roll(corners, (LANES - (step * GROUP + g) * 4) % LANES, 1)
    lane = lane_iota((total, LANES))
    sides = jnp.where(lane < 4, corners, halo).astype(jnp.bfloat16)
    beside = jnp.dot(sides, spread_ref[...], preferred_element_type=jnp.float32)
    middle = stack_ref[total : 2 * total].astype(jnp.float32)
    col = lane_iota((total, width)) % RB
    stack_ref[:total] = jnp.where(col == 0, beside, pltpu.roll(middle, 1, 1)).astype(jnp.bfloat16)
    stack_ref[2 * total :] = jnp.where(
        col == RB - 1, beside, pltpu.roll(middle, width - 1, 1)
    ).astype(jnp.bfloat16)
    sums = jnp.dot(taps_ref[...], stack_ref[...], preferred_element_type=jnp.float32)
    above = pltpu.roll(sums[:chan], RB, 1)
    below = pltpu.roll(sums[2 * chan :], width - RB, 1)
    return (above + sums[chan : 2 * chan] + below)[:, :tile]


def forward_kernel(steps, pieces, sel_ref, *refs):
    field_refs, refs = (refs[:pieces], refs[pieces:])
    halo_refs, refs = (refs[:pieces], refs[pieces:])
    corner_refs, refs = (refs[:pieces], refs[pieces:])
    (cot_ref, taps_ref, spread_ref, ring_ref, cornsel_ref, act_ref, gated_ref) = refs[:7]
    outs, (stack_ref, packs_acc, corner_acc) = (refs[7:-3], refs[-3:])
    step = pl.program_id(0)
    fields = []
    for g in range(GROUP):
        pre = conv_face(g, step, field_refs, halo_refs, corner_refs, taps_ref, spread_ref, stack_ref)
        sig = 1.0 / (1.0 + jnp.exp(-pre))
        act_ref[g] = (pre * sig).astype(jnp.bfloat16)
        gated = cot_ref[g].astype(jnp.float32) * sig * (1.0 + pre * (1.0 - sig))
        gated_ref[g] = gated.astype(jnp.bfloat16)
        fields.append(gated.astype(jnp.bfloat16))
    emit_rings(step, steps, fields, sel_ref, ring_ref, cornsel_ref, outs, packs_acc, corner_acc)


def backward_kernel(steps, pieces, *refs):
    field_refs, refs = (refs[:pieces], refs[pieces:])
    halo_refs, refs = (refs[:pieces], refs[pieces:])
    corner_refs, refs = (refs[:pieces], refs[pieces:])
    (taps_ref, spread_ref, grad_ref, stack_ref) = refs
    step = pl.program_id(0)
    for g in range(GROUP):
        total = conv_face(
            g, step, field_refs, halo_refs, corner_refs, taps_ref, spread_ref, stack_ref
        )
        grad_ref[g] = total.astype(jnp.bfloat16)


def conv_specs(fields, halos):
    faces, chan, tile = fields[0].shape
    group = lambda i: (i, 0, 0)
    return (
        [pl.BlockSpec((GROUP, chan, tile), group) for _ in fields]
        + [pl.BlockSpec((GROUP, chan, LANES), group) for _ in halos]
        + [pl.BlockSpec((1, chan, LANES), lambda i: (faces, 0, 0)) for _ in halos]
    )


def forward(sel, fields, halos, cot, taps, spread, ring, cornsel, counts):
    faces, chan, tile = fields[0].shape
    steps = faces // GROUP
    pieces = len(fields)
    outs = ring_outs(faces, chan, counts)
    out = jax.ShapeDtypeStruct((faces, chan, tile), jnp.bfloat16)
    block = pl.BlockSpec((GROUP, chan, tile), lambda i: (i, 0, 0))
    return pl.pallas_call(
        lambda *refs: forward_kernel(steps, pieces, *refs),
        grid=(steps,),
        in_specs=[pl.BlockSpec(memory_space=pltpu.SMEM)]
        + conv_specs(fields, halos)
        + [block, whole_spec(taps), whole_spec(spread), whole_spec(ring), whole_spec(cornsel)],
        out_specs=[block, block] + [whole_spec(o) for o in outs],
        out_shape=[out, out] + outs,
        scratch_shapes=[pltpu.VMEM((3 * chan * pieces, tile + LANES), jnp.bfloat16)]
        + ring_scratch(faces, chan),
        compiler_params=pltpu.CompilerParams(vmem_limit_bytes=VMEM_LIMIT),
        name="forward",
    )(sel, *fields, *halos, *halos, cot, taps, spread, ring, cornsel)


def backward(fields, halos, taps, spread):
    faces, chan, tile = fields[0].shape
    steps = faces // GROUP
    pieces = len(fields)
    return pl.pallas_call(
        lambda *refs: backward_kernel(steps, pieces, *refs),
        grid=(steps,),
        in_specs=conv_specs(fields, halos) + [whole_spec(taps), whole_spec(spread)],
        out_specs=pl.BlockSpec((GROUP, chan, tile), lambda i: (i, 0, 0)),
        out_shape=jax.ShapeDtypeStruct((faces, chan, tile), jnp.bfloat16),
        scratch_shapes=[pltpu.VMEM((3 * chan * pieces, tile + LANES), jnp.bfloat16)],
        compiler_params=pltpu.CompilerParams(vmem_limit_bytes=VMEM_LIMIT),
        name="backward",
    )(*fields, *halos, *halos, taps, spread)


def halo_tables(edge_table, corner_table, place, counts, col_len, unit, strip_cell, near_cell, corner_cell):
    row_pos, col_pos = place
    px_count, py_count = counts
    faces = edge_table.shape[0]
    side_len = px_count * RB
    most = RB // unit
    shape = (faces, 4, most)
    face = lax.broadcasted_iota(jnp.int32, shape, 0)
    edge = lax.broadcasted_iota(jnp.int32, shape, 1)
    un = lax.broadcasted_iota(jnp.int32, shape, 2)
    g, s, r = [edge_table[:, :, i, None] for i in range(3)]
    along_row = edge < 2
    border = ((edge == 0) & (col_pos == 0)) | ((edge == 1) & (col_pos == py_count - 1))
    border |= ((edge == 2) & (row_pos == 0)) | ((edge == 3) & (row_pos == px_count - 1))
    at = jnp.where(along_row, row_pos * RB, col_pos * col_len) + un * unit
    at = jnp.clip(at, 0, side_len - unit)
    at = jnp.where(r == 1, side_len - unit - at, at)
    line_tile, line_lane = strip_cell(g, s, at)
    tile = jnp.where(border, line_tile, near_cell(edge, face))
    lane = jnp.where(border, line_lane, (face % GROUP) * 32 + un * unit)
    first = jnp.where(edge == 0, STRIP_LANE[0], jnp.where(edge == 1, STRIP_LANE[1], edge * 32 - 32))
    shift = (first + un * unit - lane + LANES) % LANES
    flip = jnp.where(border & (r == 1), 1, 0)
    strips = [jnp.broadcast_to(v, shape).reshape(faces, 4 * most) for v in (tile, shift, flip)]

    shape = (faces, 2, 2)
    face = lax.broadcasted_iota(jnp.int32, shape, 0)
    down = lax.broadcasted_iota(jnp.int32, shape, 1)
    right = lax.broadcasted_iota(jnp.int32, shape, 2)
    row_on = ((down == 0) & (col_pos == 0)) | ((down == 1) & (col_pos == py_count - 1))
    col_on = ((right == 0) & (row_pos == 0)) | ((right == 1) & (row_pos == px_count - 1))
    row_at = row_pos * RB + jnp.where(right == 1, RB, -1)
    col_at = col_pos * col_len + jnp.where(down == 1, col_len, -1)
    row_edge = [edge_table[:, :2, None, i] for i in range(3)]
    col_edge = [edge_table[:, None, 2:, i] for i in range(3)]
    g, s, r = [jnp.where(row_on, row, col) for row, col in zip(row_edge, col_edge)]
    at = jnp.clip(jnp.where(row_on, row_at, col_at), 0, side_len - 1)
    at = jnp.where(r == 1, side_len - 1 - at, at)
    h, q = [corner_table[:, :, i].reshape(shape) for i in range(2)]
    both = row_on & col_on
    g, s, at = (
        jnp.where(both, h, g),
        jnp.where(both, q // 2, s),
        jnp.where(both, (q % 2) * (side_len - 1), at),
    )
    line_tile, line_lane = corner_cell(g, s, at, None, None)
    diag_px = jnp.clip(row_pos + 2 * right - 1, 0, px_count - 1)
    diag_py = jnp.clip(col_pos + 2 * down - 1, 0, py_count - 1)
    diag_tile, diag_lane = corner_cell(face, None, 3 - 2 * down - right, diag_px, diag_py)
    on = row_on | col_on
    corner_at = jnp.where(on, line_tile, diag_tile)
    corner_lane = jnp.where(on, line_lane, diag_lane)
    corner_shift = (face * 4 + 2 * down + right - corner_lane + LANES) % LANES
    return (
        *strips,
        corner_at.reshape(faces, 4),
        corner_shift.reshape(faces, 4),
    )


def from_others(array, ch_count):
    return [array] + [
        lax.ppermute(array, "ch", [(i, (i + k) % ch_count) for i in range(ch_count)])
        for k in range(1, ch_count)
    ]


class SquareHalo:
    counts = (1, 1, 2, 2)

    def __init__(self, row_pos, col_pos):
        self.place = (row_pos, col_pos)
        self.row_edge = (row_pos == 0) | (row_pos == 3)
        self.col_edge = (col_pos == 0) | (col_pos == 3)
        self.corner = self.row_edge & self.col_edge
        self.middle = self.row_edge != self.col_edge
        self.side = jnp.where(
            self.col_edge, jnp.where(col_pos == 0, 0, 1), jnp.where(row_pos == 0, 2, 3)
        )
        self.seg = jnp.where(self.col_edge, row_pos, col_pos)
        row_line = jnp.where(col_pos == 0, 0, 1)
        col_line = jnp.where(row_pos == 0, 2, 3)
        to_px, to_py = (jnp.where(row_pos == 1, 3, 2), jnp.where(col_pos == 1, 1, 0))
        self.sel = jnp.stack(
            [
                jnp.where(row_pos % 2 == 0, 3, 2),
                jnp.where(col_pos % 2 == 0, 1, 0),
                self.side,
                jnp.where(self.row_edge, to_py, to_px),
                jnp.where(self.corner, row_line, jnp.where(self.middle, self.side, to_py)),
                jnp.where(self.corner, col_line, self.side),
            ]
        ).astype(jnp.int32)

    def exchange(self, col_side, row_side, pair, lines, corner):
        every = [(x, y) for x in range(4) for y in range(4)]
        number = lambda x, y: x * 4 + y
        axes = ("px", "py")
        swap = lambda array, pairs: lax.ppermute(
            array, axes, [(number(*a), number(*b)) for a, b in pairs]
        )
        ends = (0, 3)
        corners = [(x, y) for x in ends for y in ends]
        spot = lambda side, seg: ((seg, 0), (seg, 3), (0, seg), (3, seg))[side]
        near_col = swap(col_side, [((x, y), (x ^ 1, y)) for x, y in every])
        near_row = swap(row_side, [((x, y), (x, y ^ 1)) for x, y in every])
        beside = [(spot(side, k), spot(side, 3 - k)) for side in range(4) for k in (1, 2)]
        beside += [((x, y), (3 - x, y)) for x in (1, 2) for y in (1, 2)]
        paired = swap(pair, beside)
        slot = lax.broadcasted_iota(jnp.int32, lines.shape, 0) // (lines.shape[0] // 2)
        theirs = self.middle & (slot != self.seg - 1)
        half = paired[: lines.shape[0] // 2]
        lines = jnp.where(theirs, jnp.concatenate([half, half], axis=0), lines)
        across = []
        for j in (1, 2, 3):
            pairs = [(spot(side, k), spot(side ^ j, k)) for side in range(4) for k in (1, 2)]
            pairs += [(corners[c], corners[c ^ j]) for c in range(4)]
            if j == 1:
                pairs += [((x, y), (x, 3 - y)) for x in (1, 2) for y in (1, 2)]
            across.append(swap(lines, pairs))
        ends_of = jnp.broadcast_to(corner, (16,) + corner.shape[1:])
        ends_of = lax.all_to_all(ends_of, axes, 0, 0, tiled=True)
        return [lines, *across, paired, near_col, near_row, ends_of]

    def tables(self, edge_table, corner_table, col_len, unit):
        row_pos, col_pos = self.place
        quads = edge_table.shape[0] // GROUP
        slot = 2 * quads

        def strip_cell(g, s, at):
            k = at // RB
            lane = (g % GROUP) * 32
            me = jnp.where(row_pos > 0, 2, 0) + jnp.where(col_pos > 0, 1, 0)
            far = jnp.where(k > 0, 1, 0)
            owner = jnp.where(s < 2, 2 * far + s, 2 * (s - 2) + far)
            corner = (me ^ owner) * slot + (s // 2) * quads
            middle = (self.side ^ s) * slot + (k - 1) * quads
            return (jnp.where(self.corner, corner, middle) + g // GROUP, lane)

        def near_cell(edge, face):
            paired, near_col, near_row = (4 * slot + quads, 5 * slot, 5 * slot + quads)
            by_col = jnp.where(row_pos % 2 == 3 - edge, near_col, paired)
            rest = jnp.where(self.row_edge, paired, slot)
            by_row = jnp.where(col_pos % 2 == 1 - edge, near_row, rest)
            return jnp.where(edge < 2, by_row, by_col) + face // GROUP

        def corner_cell(g, s, at, px, py):
            base = 5 * slot + 2 * quads
            if s is None:
                return (base + px * 4 + py, g * 4 + at)
            seg, hi = (at // RB, jnp.where(at % RB == 0, 0, 1))
            owner = jnp.where(s < 2, seg * 4 + 3 * s, 12 * (s - 2) + seg)
            q = jnp.where(s < 2, 2 * s + hi, s - 2 + 2 * hi)
            return (base + owner, g * 4 + q)

        return halo_tables(
            edge_table, corner_table, self.place, (4, 4), col_len, unit,
            strip_cell, near_cell, corner_cell,
        )


class GatheredHalo:
    counts = (1, 1, 1, 1, 2)

    def __init__(self, row_pos, col_pos, px_count, py_count):
        self.place = (row_pos, col_pos)
        self.size = (px_count, py_count)
        lines = [jnp.where(col_pos == 0, 0, 1), jnp.where(row_pos == 0, 2, 3)]
        self.sel = jnp.stack([jnp.int32(side) for side in range(4)] + lines).astype(jnp.int32)

    def exchange(self, top, bottom, left, right, lines, corner):
        px_count, py_count = self.size
        up = lambda n: [(i, i + 1) for i in range(n - 1)]
        down = lambda n: [(i + 1, i) for i in range(n - 1)]
        return [
            lax.ppermute(bottom, "py", up(py_count)),
            lax.ppermute(top, "py", down(py_count)),
            lax.ppermute(right, "px", up(px_count)),
            lax.ppermute(left, "px", down(px_count)),
            lax.all_gather(lines, ("px", "py"), axis=0, tiled=True),
            lax.all_gather(corner, ("px", "py"), axis=0, tiled=True),
        ]

    def tables(self, edge_table, corner_table, col_len, unit):
        px_count, py_count = self.size
        quads = edge_table.shape[0] // GROUP
        line_base = 4 * quads
        corner_base = line_base + px_count * py_count * 2 * quads

        def strip_cell(g, s, at):
            length = jnp.where(s < 2, RB, col_len)
            seg = at // length
            px = jnp.where(s < 2, seg, (s - 2) * (px_count - 1))
            py = jnp.where(s < 2, s * (py_count - 1), seg)
            tile = line_base + ((px * py_count + py) * 2 + s // 2) * quads + g // GROUP
            return (tile, (g % GROUP) * 32 + at % length)

        def near_cell(edge, face):
            return edge * quads + face // GROUP

        def corner_cell(g, s, at, px, py):
            if s is None:
                return (corner_base + px * py_count + py, g * 4 + at)
            return strip_cell(g, s, at)

        return halo_tables(
            edge_table, corner_table, self.place, self.size, col_len, unit,
            strip_cell, near_cell, corner_cell,
        )


def local(features, cotangent, weight, edge_table, corner_table):
    chan, faces = features.shape[:2]
    tile = features.shape[4]
    col_len = tile // RB
    unit = min(RB, col_len)
    units = (RB // unit, RB // unit, col_len // unit, col_len // unit)
    px_count, py_count, ch_count = [lax.axis_size(name) for name in ("px", "py", "ch")]
    row_pos, col_pos, ch_pos = [lax.axis_index(name) for name in ("px", "py", "ch")]
    ring = jnp.asarray(ring_matrix(col_len), jnp.bfloat16)
    cornsel = jnp.asarray(corner_matrix(), jnp.bfloat16)
    spread = jnp.asarray(spread_matrix(col_len), jnp.bfloat16)
    rev = jnp.asarray(reverse_matrix(unit), jnp.bfloat16)
    if px_count == py_count == 4 and col_len == RB:
        halo_plan = SquareHalo(row_pos, col_pos)
    else:
        halo_plan = GatheredHalo(row_pos, col_pos, px_count, py_count)
    counts, sel = (halo_plan.counts, halo_plan.sel)

    feats = jnp.transpose(features.reshape(chan, faces, tile), (1, 0, 2))
    cot = jnp.transpose(cotangent.reshape(chan, faces, tile), (1, 0, 2))
    fields = from_others(feats, ch_count)

    def blocks(array, axis):
        order = [(ch_pos - k) % ch_count for k in range(ch_count)]
        return jnp.concatenate(
            [lax.dynamic_slice_in_dim(array, at * chan, chan, axis) for at in order], axis
        )

    own_out = lax.dynamic_slice_in_dim(weight, ch_pos * chan, chan, 2)
    taps = blocks(own_out, 3).transpose(0, 2, 1, 3).reshape(3 * chan, -1)
    own_in = lax.dynamic_slice_in_dim(weight, ch_pos * chan, chan, 3)
    back_taps = blocks(own_in, 2)[::-1, ::-1].transpose(0, 3, 1, 2).reshape(3 * chan, -1)
    tables = halo_plan.tables(edge_table, corner_table, col_len, unit)

    parts = rings_of(feats, sel, ring, cornsel, counts)
    tiles = halo_plan.exchange(*parts)
    halo = assemble_halo(tables, tiles, rev, faces, units, unit)
    halo, taps, back_taps = lax.optimization_barrier((halo, taps, back_taps))
    halos = from_others(halo, ch_count)
    act, gated, *parts = forward(sel, fields, halos, cot, taps, spread, ring, cornsel, counts)

    fields = from_others(gated, ch_count)
    tiles = halo_plan.exchange(*parts)
    halo = assemble_halo(tables, tiles, rev, faces, units, unit)
    halos = from_others(halo, ch_count)
    grad = backward(fields, halos, back_taps, spread)

    shape = (chan, faces, 1, 1, tile)
    return (
        jnp.transpose(act, (1, 0, 2)).reshape(shape),
        jnp.transpose(grad, (1, 0, 2)).reshape(shape),
    )


def solution(mesh):
    spec = P("ch", None, "py", "px", None)
    return jax.shard_map(
        local,
        mesh=mesh,
        in_specs=(spec, spec, P(), P(), P()),
        out_specs=(spec, spec),
        check_vma=False,
    )
```

```python
import jax
import jax.numpy as jnp
import numpy as np
from jax import lax
from jax.experimental import pallas as pl
from jax.experimental.pallas import tpu as pltpu
from jax.sharding import PartitionSpec as P

RB = 32
GROUP = 4
LANES = 128
VMEM_LIMIT = 24 * 1024 * 1024
STRIP_LANE = (96, 0, 32, 64)


def ring_matrix(col_len):
    mat = np.zeros((col_len * RB, LANES), np.float32)
    for b in range(RB):
        mat[b, b] = 1
        mat[(col_len - 1) * RB + b, 32 + b] = 1
    for a in range(col_len):
        mat[a * RB, 64 + a] = 1
        mat[a * RB + RB - 1, 96 + a] = 1
    return mat


def corner_matrix():
    mat = np.zeros((LANES, LANES), np.float32)
    for q, lane in enumerate((0, RB - 1, 32, 32 + RB - 1)):
        mat[lane, q] = 1
    return mat


def reverse_matrix(unit):
    mat = np.zeros((LANES, LANES), np.float32)
    for lane in range(LANES):
        mat[lane, (lane // unit) * unit + unit - 1 - lane % unit] = 1
    return mat


def spread_matrix(col_len):
    width = col_len * RB + LANES
    mat = np.zeros((LANES, width), np.float32)
    top, bottom = (col_len + 3) * RB, col_len * RB
    mat[0, top] = 1
    mat[1, top + RB - 1] = 1
    mat[2, bottom] = 1
    mat[3, bottom + RB - 1] = 1
    for a in range(col_len):
        mat[STRIP_LANE[2] + a, a * RB] = 1
        mat[STRIP_LANE[3] + a, a * RB + RB - 1] = 1
    return mat


def lane_iota(shape):
    return lax.broadcasted_iota(jnp.int32, shape, len(shape) - 1)


def emit_rings(step, steps, fields, plan, ring_ref, cornsel_ref, outs, packs_acc, corner_acc):
    chan = fields[0].shape[0]
    lane = lane_iota((chan, LANES))
    rings = [
        jnp.dot(field, ring_ref[...], preferred_element_type=jnp.float32) for field in fields
    ]
    for side in range(4):
        tile = jnp.zeros((chan, LANES), jnp.float32)
        for g, ring in enumerate(rings):
            moved = pltpu.roll(ring, ((g - side) * 32) % LANES, 1) if g != side else ring
            tile = jnp.where(lane // 32 == g, moved, tile)
        packs_acc[side * steps + step] = tile.astype(jnp.bfloat16)

    @pl.when(step == 0)
    def _():
        corner_acc[...] = jnp.zeros_like(corner_acc)

    for g, ring in enumerate(rings):
        picked = jnp.dot(
            ring.astype(jnp.bfloat16), cornsel_ref[...], preferred_element_type=jnp.float32
        )
        corner_acc[...] += pltpu.roll(picked, (step * GROUP + g) * 4, 1)

    @pl.when(step == steps - 1)
    def _():
        chosen = iter(plan.chosen_sides())
        for out in outs[:-1]:
            for at in range(0, out.shape[0], steps):
                base = next(chosen) * steps
                for q in range(steps):
                    out[at + q] = packs_acc[base + q]
        outs[-1][0] = corner_acc[...].astype(jnp.bfloat16)


def ring_outs(faces, chan, counts):
    steps = faces // GROUP
    tiles = [count * steps for count in counts] + [1]
    return [jax.ShapeDtypeStruct((n, chan, LANES), jnp.bfloat16) for n in tiles]


def ring_scratch(faces, chan):
    steps = faces // GROUP
    return [
        pltpu.VMEM((4 * steps, chan, LANES), jnp.bfloat16),
        pltpu.VMEM((chan, LANES), jnp.float32),
    ]


def rings_kernel(steps, plan, field_ref, ring_ref, cornsel_ref, *refs):
    fields = [field_ref[g] for g in range(GROUP)]
    emit_rings(pl.program_id(0), steps, fields, plan, ring_ref, cornsel_ref, refs[:-2], *refs[-2:])


def whole_spec(array):
    zeros = (0,) * array.ndim
    return pl.BlockSpec(array.shape, lambda *_: zeros)


def rings_of(field, plan, ring, cornsel):
    faces, chan, tile = field.shape
    steps = faces // GROUP
    outs = ring_outs(faces, chan, plan.counts)
    return pl.pallas_call(
        lambda *refs: rings_kernel(steps, plan, *refs),
        grid=(steps,),
        in_specs=[
            pl.BlockSpec((GROUP, chan, tile), lambda i: (i, 0, 0)),
            whole_spec(ring),
            whole_spec(cornsel),
        ],
        out_specs=[whole_spec(out) for out in outs],
        out_shape=outs,
        scratch_shapes=ring_scratch(faces, chan),
        compiler_params=pltpu.CompilerParams(vmem_limit_bytes=VMEM_LIMIT),
        name="rings",
    )(field, ring, cornsel)


def halo_kernel(faces, units, unit, *refs):
    table, tile_refs, (rev_ref, halo_ref, pool, turn_acc) = (refs[0], refs[1:-4], refs[-4:])
    chan = halo_ref.shape[1]
    lane = lane_iota((chan, LANES))
    at = 0
    for ref in tile_refs:
        pool[at : at + ref.shape[0]] = ref[...]
        at += ref.shape[0]
    corner_tile = jnp.zeros((chan, LANES), jnp.float32)
    most = max(units)
    rows = 4 * most
    for f in range(faces):
        tile = jnp.zeros((chan, LANES), jnp.float32)
        turned = jnp.zeros((chan, LANES), jnp.float32)
        for e in range(4):
            for un in range(units[e]):
                base = STRIP_LANE[e] + un * unit
                span = (lane >= base) & (lane < base + unit)
                entry = e * most + un
                source = pool[table[entry, f]].astype(jnp.float32)
                moved = pltpu.roll(source, table[rows + entry, f], 1)
                flip = table[2 * rows + entry, f] == 1
                tile = jnp.where(span & jnp.logical_not(flip), moved, tile)
                turned = jnp.where(span & flip, moved, turned)
        halo_ref[f] = tile.astype(jnp.bfloat16)
        turn_acc[f] = turned.astype(jnp.bfloat16)
        for c in range(4):
            source = pool[table[3 * rows + c, f]].astype(jnp.float32)
            moved = pltpu.roll(source, table[3 * rows + 4 + c, f], 1)
            corner_tile = jnp.where(lane == f * 4 + c, moved, corner_tile)
    turned = jnp.dot(
        turn_acc[...].reshape(faces * chan, LANES), rev_ref[...], preferred_element_type=jnp.float32
    ).reshape(faces, chan, LANES)
    for f in range(faces):
        halo_ref[f] += turned[f].astype(jnp.bfloat16)
    halo_ref[faces] = corner_tile.astype(jnp.bfloat16)


def assemble_halo(table, tiles, rev, faces, units, unit):
    chan = tiles[0].shape[1]
    halo = jax.ShapeDtypeStruct((faces + 1, chan, LANES), jnp.bfloat16)
    vmem = pl.BlockSpec(memory_space=pltpu.VMEM)
    smem = pl.BlockSpec(memory_space=pltpu.SMEM)
    return pl.pallas_call(
        lambda *refs: halo_kernel(faces, units, unit, *refs),
        in_specs=[smem] + [vmem] * (len(tiles) + 1),
        out_specs=vmem,
        out_shape=halo,
        scratch_shapes=[
            pltpu.VMEM((sum(t.shape[0] for t in tiles), chan, LANES), jnp.bfloat16),
            pltpu.VMEM((faces, chan, LANES), jnp.bfloat16),
        ],
        compiler_params=pltpu.CompilerParams(vmem_limit_bytes=VMEM_LIMIT),
        name="halo",
    )(table, *tiles, rev)


def conv_face(g, step, field_refs, halo_refs, corner_refs, taps_ref, spread_ref, stack_ref):
    chan, tile = field_refs[0].shape[1:]
    pieces = len(field_refs)
    total = chan * pieces
    width = tile + LANES
    for k in range(pieces):
        stack_ref[total + k * chan : total + (k + 1) * chan, :tile] = field_refs[k][g]
        stack_ref[total + k * chan : total + (k + 1) * chan, tile:] = halo_refs[k][g]
    halo = stack_ref[total : 2 * total, tile:].astype(jnp.float32)
    corners = jnp.concatenate([ref[0].astype(jnp.float32) for ref in corner_refs], axis=0)
    corners = pltpu.roll(corners, (LANES - (step * GROUP + g) * 4) % LANES, 1)
    lane = lane_iota((total, LANES))
    sides = jnp.where(lane < 4, corners, halo).astype(jnp.bfloat16)
    beside = jnp.dot(sides, spread_ref[...], preferred_element_type=jnp.float32)
    middle = stack_ref[total : 2 * total].astype(jnp.float32)
    col = lane_iota((total, width)) % RB
    stack_ref[:total] = jnp.where(col == 0, beside, pltpu.roll(middle, 1, 1)).astype(jnp.bfloat16)
    stack_ref[2 * total :] = jnp.where(
        col == RB - 1, beside, pltpu.roll(middle, width - 1, 1)
    ).astype(jnp.bfloat16)
    sums = jnp.dot(taps_ref[...], stack_ref[...], preferred_element_type=jnp.float32)
    above = pltpu.roll(sums[:chan], RB, 1)
    below = pltpu.roll(sums[2 * chan :], width - RB, 1)
    return (above + sums[chan : 2 * chan] + below)[:, :tile]


def forward_kernel(steps, pieces, plan, *refs):
    field_refs, refs = (refs[:pieces], refs[pieces:])
    halo_refs, refs = (refs[:pieces], refs[pieces:])
    corner_refs, refs = (refs[:pieces], refs[pieces:])
    (cot_ref, taps_ref, spread_ref, ring_ref, cornsel_ref, act_ref, gated_ref) = refs[:7]
    outs, (stack_ref, packs_acc, corner_acc) = (refs[7:-3], refs[-3:])
    step = pl.program_id(0)
    fields = []
    for g in range(GROUP):
        pre = conv_face(g, step, field_refs, halo_refs, corner_refs, taps_ref, spread_ref, stack_ref)
        sig = 1.0 / (1.0 + jnp.exp(-pre))
        act_ref[g] = (pre * sig).astype(jnp.bfloat16)
        gated = cot_ref[g].astype(jnp.float32) * sig * (1.0 + pre * (1.0 - sig))
        gated_ref[g] = gated.astype(jnp.bfloat16)
        fields.append(gated.astype(jnp.bfloat16))
    emit_rings(step, steps, fields, plan, ring_ref, cornsel_ref, outs, packs_acc, corner_acc)


def backward_kernel(steps, pieces, *refs):
    field_refs, refs = (refs[:pieces], refs[pieces:])
    halo_refs, refs = (refs[:pieces], refs[pieces:])
    corner_refs, refs = (refs[:pieces], refs[pieces:])
    (taps_ref, spread_ref, grad_ref, stack_ref) = refs
    step = pl.program_id(0)
    for g in range(GROUP):
        total = conv_face(
            g, step, field_refs, halo_refs, corner_refs, taps_ref, spread_ref, stack_ref
        )
        grad_ref[g] = total.astype(jnp.bfloat16)


def conv_specs(fields, halos):
    faces, chan, tile = fields[0].shape
    group = lambda i: (i, 0, 0)
    return (
        [pl.BlockSpec((GROUP, chan, tile), group) for _ in fields]
        + [pl.BlockSpec((GROUP, chan, LANES), group) for _ in halos]
        + [pl.BlockSpec((1, chan, LANES), lambda i: (faces, 0, 0)) for _ in halos]
    )


def forward(plan, fields, halos, cot, taps, spread, ring, cornsel):
    faces, chan, tile = fields[0].shape
    steps = faces // GROUP
    pieces = len(fields)
    outs = ring_outs(faces, chan, plan.counts)
    out = jax.ShapeDtypeStruct((faces, chan, tile), jnp.bfloat16)
    block = pl.BlockSpec((GROUP, chan, tile), lambda i: (i, 0, 0))
    return pl.pallas_call(
        lambda *refs: forward_kernel(steps, pieces, plan, *refs),
        grid=(steps,),
        in_specs=conv_specs(fields, halos)
        + [block, whole_spec(taps), whole_spec(spread), whole_spec(ring), whole_spec(cornsel)],
        out_specs=[block, block] + [whole_spec(o) for o in outs],
        out_shape=[out, out] + outs,
        scratch_shapes=[pltpu.VMEM((3 * chan * pieces, tile + LANES), jnp.bfloat16)]
        + ring_scratch(faces, chan),
        compiler_params=pltpu.CompilerParams(vmem_limit_bytes=VMEM_LIMIT),
        name="forward",
    )(*fields, *halos, *halos, cot, taps, spread, ring, cornsel)


def backward(fields, halos, taps, spread):
    faces, chan, tile = fields[0].shape
    steps = faces // GROUP
    pieces = len(fields)
    return pl.pallas_call(
        lambda *refs: backward_kernel(steps, pieces, *refs),
        grid=(steps,),
        in_specs=conv_specs(fields, halos) + [whole_spec(taps), whole_spec(spread)],
        out_specs=pl.BlockSpec((GROUP, chan, tile), lambda i: (i, 0, 0)),
        out_shape=jax.ShapeDtypeStruct((faces, chan, tile), jnp.bfloat16),
        scratch_shapes=[pltpu.VMEM((3 * chan * pieces, tile + LANES), jnp.bfloat16)],
        compiler_params=pltpu.CompilerParams(vmem_limit_bytes=VMEM_LIMIT),
        name="backward",
    )(*fields, *halos, *halos, taps, spread)


def rows_of(*parts):
    return jnp.concatenate(parts, axis=0)


def halo_table(plan, edge_ref, corner_ref, px_count, py_count, col_len, unit):
    row_pos, col_pos = plan.place()
    faces = edge_ref.shape[2]
    side_len = px_count * RB
    most = RB // unit
    shape = (4 * most, faces)
    face = lane_iota(shape)
    row = lax.broadcasted_iota(jnp.int32, shape, 0)
    edge, un = (row // most, row % most)
    g, s, r = [
        rows_of(*[edge_ref[i, e : e + 1] for e in range(4) for _ in range(most)]) for i in range(3)
    ]
    border = ((edge == 0) & (col_pos == 0)) | ((edge == 1) & (col_pos == py_count - 1))
    border |= ((edge == 2) & (row_pos == 0)) | ((edge == 3) & (row_pos == px_count - 1))
    at = jnp.where(edge < 2, row_pos * RB, col_pos * col_len) + un * unit
    at = jnp.clip(at, 0, side_len - unit)
    at = jnp.where(r == 1, side_len - unit - at, at)
    line_tile, line_lane = plan.strip_cell(g, s, at)
    tile = jnp.where(border, line_tile, plan.near_cell(edge, face))
    lane = jnp.where(border, line_lane, (face % GROUP) * 32 + un * unit)
    first = jnp.where(edge == 0, STRIP_LANE[0], jnp.where(edge == 1, STRIP_LANE[1], edge * 32 - 32))
    shift = (first + un * unit - lane + LANES) % LANES
    flip = jnp.where(border & (r == 1), 1, 0)

    shape = (4, faces)
    face = lane_iota(shape)
    c = lax.broadcasted_iota(jnp.int32, shape, 0)
    down, right = (c // 2, c % 2)
    row_on = ((down == 0) & (col_pos == 0)) | ((down == 1) & (col_pos == py_count - 1))
    col_on = ((right == 0) & (row_pos == 0)) | ((right == 1) & (row_pos == px_count - 1))
    row_at = row_pos * RB + jnp.where(right == 1, RB, -1)
    col_at = col_pos * col_len + jnp.where(down == 1, col_len, -1)
    edge_of = lambda i, edges: rows_of(*[edge_ref[i, e : e + 1] for e in edges])
    g, s, r = [
        jnp.where(row_on, edge_of(i, (0, 0, 1, 1)), edge_of(i, (2, 3, 2, 3))) for i in range(3)
    ]
    at = jnp.clip(jnp.where(row_on, row_at, col_at), 0, side_len - 1)
    at = jnp.where(r == 1, side_len - 1 - at, at)
    h, q = [rows_of(*[corner_ref[k, i : i + 1] for k in range(4)]) for i in range(2)]
    both = row_on & col_on
    g = jnp.where(both, h, g)
    s = jnp.where(both, q // 2, s)
    at = jnp.where(both, (q % 2) * (side_len - 1), at)
    line_tile, line_lane = plan.corner_cell(g, s, at)
    diag_px = jnp.clip(row_pos + 2 * right - 1, 0, px_count - 1)
    diag_py = jnp.clip(col_pos + 2 * down - 1, 0, py_count - 1)
    diag_tile, diag_lane = plan.diagonal_cell(face, 3 - c, diag_px, diag_py)
    on = row_on | col_on
    corner_at = jnp.where(on, line_tile, diag_tile)
    corner_lane = jnp.where(on, line_lane, diag_lane)
    corner_shift = (face * 4 + c - corner_lane + LANES) % LANES
    return rows_of(tile, shift, flip, corner_at, corner_shift)


def setup_kernel(plan, chan, shape, edge_ref, corner_ref, weight_ref, table_ref, taps_ref, back_ref, turn):
    table_ref[...] = halo_table(plan, edge_ref, corner_ref, *shape)
    total = weight_ref.shape[2]
    own = lax.axis_index("ch") * chan
    shift = (total - own) % total
    for i in range(3):
        for j in range(3):
            turn[...] = weight_ref[i, j].astype(jnp.float32)
            rows = pltpu.roll(turn[pl.ds(pl.multiple_of(own, chan), chan)], shift, 1)
            cols = slice(j * total, (j + 1) * total)
            taps_ref[i * chan : (i + 1) * chan, cols] = rows.astype(jnp.bfloat16)
            turn[...] = turn[...].T
            rows = pltpu.roll(turn[pl.ds(pl.multiple_of(own, chan), chan)], shift, 1)
            cols = slice((2 - j) * total, (3 - j) * total)
            back_ref[(2 - i) * chan : (3 - i) * chan, cols] = rows.astype(jnp.bfloat16)


def setup(plan, edge_table, corner_table, weight, chan, counts, col_len, unit):
    edges = jnp.transpose(edge_table, (2, 1, 0))
    corners = jnp.transpose(corner_table, (1, 2, 0))
    total = weight.shape[2]
    vmem = pl.BlockSpec(memory_space=pltpu.VMEM)
    taps = jax.ShapeDtypeStruct((3 * chan, 3 * total), jnp.bfloat16)
    table = jax.ShapeDtypeStruct((12 * (RB // unit) + 8, edges.shape[2]), jnp.int32)
    return pl.pallas_call(
        lambda *refs: setup_kernel(plan, chan, (*counts, col_len, unit), *refs),
        in_specs=[vmem] * 3,
        out_specs=[vmem] * 3,
        out_shape=[table, taps, taps],
        scratch_shapes=[pltpu.VMEM((total, total), jnp.float32)],
        compiler_params=pltpu.CompilerParams(vmem_limit_bytes=VMEM_LIMIT),
        name="setup",
    )(edges, corners, weight)


def from_others(array, ch_count):
    return [array] + [
        lax.ppermute(array, "ch", [((i + k) % ch_count, i) for i in range(ch_count)])
        for k in range(1, ch_count)
    ]


class Place:
    @staticmethod
    def place():
        return (lax.axis_index("px"), lax.axis_index("py"))


class SquareHalo(Place):
    counts = (2, 1, 1, 2)

    def __init__(self, quads):
        self.quads = quads

    def roles(self):
        row_pos, col_pos = self.place()
        px_end = (row_pos == 0) | (row_pos == 3)
        py_end = (col_pos == 0) | (col_pos == 3)
        side = jnp.where(
            py_end, jnp.where(col_pos == 0, 0, 1), jnp.where(row_pos == 0, 2, 3)
        )
        corner = px_end & py_end
        middle = (px_end | py_end) & jnp.logical_not(corner)
        return (px_end, corner, middle, side, jnp.where(px_end, col_pos, row_pos))

    def chosen_sides(self):
        row_pos, col_pos = self.place()
        px_end, corner, middle, side, seg = self.roles()
        row_line = jnp.where(col_pos == 0, 0, 1)
        col_line = jnp.where(row_pos == 0, 2, 3)
        to_px, to_py = (jnp.where(row_pos == 1, 3, 2), jnp.where(col_pos == 1, 1, 0))
        facing = jnp.where(px_end, to_py, to_px)
        return [
            jnp.where(seg == 1, side, facing),
            jnp.where(seg == 1, facing, side),
            jnp.where(row_pos % 2 == 0, 3, 2),
            jnp.where(col_pos % 2 == 0, 1, 0),
            jnp.where(corner, row_line, jnp.where(middle, side, to_py)),
            jnp.where(corner, col_line, side),
        ]

    def exchange(self, pair, col_side, row_side, lines, corner):
        every = [(x, y) for x in range(4) for y in range(4)]
        axes = ("px", "py")
        swap = lambda array, pairs: lax.ppermute(
            array, axes, [(a[0] * 4 + a[1], b[0] * 4 + b[1]) for a, b in pairs]
        )
        ends = (0, 3)
        corners = [(x, y) for x in ends for y in ends]
        spot = lambda side, seg: ((seg, 0), (seg, 3), (0, seg), (3, seg))[side]
        beside = [(spot(side, k), spot(side, 3 - k)) for side in range(4) for k in (1, 2)]
        beside += [((x, y), (3 - x, y)) for x in (1, 2) for y in (1, 2)]
        paired = swap(pair, beside)
        near_col = swap(col_side, [((x, y), (x ^ 1, y)) for x, y in every])
        near_row = swap(row_side, [((x, y), (x, y ^ 1)) for x, y in every])
        _, _, middle, _, seg = self.roles()
        slot = lax.broadcasted_iota(jnp.int32, (2 * self.quads, 1, 1), 0) // self.quads
        lines = jnp.where(middle & (slot != seg - 1), paired, lines)
        across = []
        for j in (1, 2, 3):
            pairs = [(spot(side, k), spot(side ^ j, k)) for side in range(4) for k in (1, 2)]
            pairs += [(corners[c], corners[c ^ j]) for c in range(4)]
            if j == 1:
                pairs += [((x, y), (x, 3 - y)) for x in (1, 2) for y in (1, 2)]
            across.append(swap(lines, pairs))
        corner, lines = lax.optimization_barrier((corner, lines))
        ends_of = jnp.broadcast_to(corner, (16,) + corner.shape[1:])
        ends_of = lax.all_to_all(ends_of, axes, 0, 0, tiled=True)
        return [lines, *across, paired, near_col, near_row, ends_of]

    def strip_cell(self, g, s, at):
        row_pos, col_pos = self.place()
        _, corner, _, side, _ = self.roles()
        slot = 2 * self.quads
        k = at // RB
        me = jnp.where(row_pos > 0, 2, 0) + jnp.where(col_pos > 0, 1, 0)
        far = jnp.where(k > 0, 1, 0)
        owner = jnp.where(s < 2, 2 * far + s, 2 * (s - 2) + far)
        at_corner = (me ^ owner) * slot + (s // 2) * self.quads
        at_middle = (side ^ s) * slot + (k - 1) * self.quads
        return (jnp.where(corner, at_corner, at_middle) + g // GROUP, (g % GROUP) * 32)

    def near_cell(self, edge, face):
        row_pos, col_pos = self.place()
        px_end, _, _, _, seg = self.roles()
        slot = 2 * self.quads
        paired = 4 * slot + (seg - 1) * self.quads
        near_col, near_row = (5 * slot, 5 * slot + self.quads)
        by_col = jnp.where(row_pos % 2 == 3 - edge, near_col, paired)
        by_row = jnp.where(col_pos % 2 == 1 - edge, near_row, jnp.where(px_end, paired, slot))
        return jnp.where(edge < 2, by_row, by_col) + face // GROUP

    def corner_cell(self, g, s, at):
        seg, hi = (at // RB, jnp.where(at % RB == 0, 0, 1))
        owner = jnp.where(s < 2, seg * 4 + 3 * s, 12 * (s - 2) + seg)
        q = jnp.where(s < 2, 2 * s + hi, s - 2 + 2 * hi)
        return (12 * self.quads + owner, g * 4 + q)

    def diagonal_cell(self, face, q, px, py):
        return (12 * self.quads + px * 4 + py, face * 4 + q)


class GatheredHalo(Place):
    counts = (1, 1, 1, 1, 2)

    def __init__(self, quads, px_count, py_count, col_len):
        self.quads = quads
        self.size = (px_count, py_count)
        self.col_len = col_len

    def chosen_sides(self):
        row_pos, col_pos = self.place()
        return [0, 1, 2, 3, jnp.where(col_pos == 0, 0, 1), jnp.where(row_pos == 0, 2, 3)]

    def exchange(self, top, bottom, left, right, lines, corner):
        px_count, py_count = self.size
        up = lambda n: [(i, i + 1) for i in range(n - 1)]
        down = lambda n: [(i + 1, i) for i in range(n - 1)]
        return [
            lax.ppermute(bottom, "py", up(py_count)),
            lax.ppermute(top, "py", down(py_count)),
            lax.ppermute(right, "px", up(px_count)),
            lax.ppermute(left, "px", down(px_count)),
            lax.all_gather(lines, ("px", "py"), axis=0, tiled=True),
            lax.all_gather(corner, ("px", "py"), axis=0, tiled=True),
        ]

    def strip_cell(self, g, s, at):
        px_count, py_count = self.size
        length = jnp.where(s < 2, RB, self.col_len)
        seg = at // length
        px = jnp.where(s < 2, seg, (s - 2) * (px_count - 1))
        py = jnp.where(s < 2, s * (py_count - 1), seg)
        tile = (4 + (px * py_count + py) * 2 + s // 2) * self.quads + g // GROUP
        return (tile, (g % GROUP) * 32 + at % length)

    def near_cell(self, edge, face):
        return edge * self.quads + face // GROUP

    def corner_cell(self, g, s, at):
        return self.strip_cell(g, s, at)

    def diagonal_cell(self, face, q, px, py):
        px_count, py_count = self.size
        base = (4 + 2 * px_count * py_count) * self.quads
        return (base + px * py_count + py, face * 4 + q)


def local(features, cotangent, weight, edge_table, corner_table):
    chan, faces = features.shape[:2]
    tile = features.shape[4]
    col_len = tile // RB
    unit = min(RB, col_len)
    units = (RB // unit, RB // unit, col_len // unit, col_len // unit)
    px_count, py_count, ch_count = [lax.axis_size(name) for name in ("px", "py", "ch")]
    ring = jnp.asarray(ring_matrix(col_len), jnp.bfloat16)
    cornsel = jnp.asarray(corner_matrix(), jnp.bfloat16)
    spread = jnp.asarray(spread_matrix(col_len), jnp.bfloat16)
    rev = jnp.asarray(reverse_matrix(unit), jnp.bfloat16)
    if px_count == py_count == 4 and col_len == RB:
        plan = SquareHalo(faces // GROUP)
    else:
        plan = GatheredHalo(faces // GROUP, px_count, py_count, col_len)

    feats = jnp.transpose(features.reshape(chan, faces, tile), (1, 0, 2))
    cot = jnp.transpose(cotangent.reshape(chan, faces, tile), (1, 0, 2))
    fields = from_others(feats, ch_count)
    parts = rings_of(feats, plan, ring, cornsel)
    table, taps, back_taps = setup(
        plan, edge_table, corner_table, weight, chan, (px_count, py_count), col_len, unit
    )
    tiles = plan.exchange(*parts)
    halo = assemble_halo(table, tiles, rev, faces, units, unit)
    halos = from_others(halo, ch_count)
    act, gated, *parts = forward(plan, fields, halos, cot, taps, spread, ring, cornsel)

    fields = from_others(gated, ch_count)
    tiles = plan.exchange(*parts)
    halo = assemble_halo(table, tiles, rev, faces, units, unit)
    halos = from_others(halo, ch_count)
    grad = backward(fields, halos, back_taps, spread)

    shape = (chan, faces, 1, 1, tile)
    return (
        jnp.transpose(act, (1, 0, 2)).reshape(shape),
        jnp.transpose(grad, (1, 0, 2)).reshape(shape),
    )


def solution(mesh):
    spec = P("ch", None, "py", "px", None)
    return jax.shard_map(
        local,
        mesh=mesh,
        in_specs=(spec, spec, P(), P(), P()),
        out_specs=(spec, spec),
        check_vma=False,
    )
```

```python
import jax
import jax.numpy as jnp
import numpy as np
from jax import lax
from jax.experimental import pallas as pl
from jax.experimental.pallas import tpu as pltpu
from jax.sharding import PartitionSpec as P

RB = 32
GROUP = 4
LANES = 128
VMEM_LIMIT = 60 * 1024 * 1024
STRIP_LANE = (96, 0, 32, 64)


def ring_matrix(col_len):
    mat = np.zeros((col_len * RB, LANES), np.float32)
    for b in range(RB):
        mat[b, b] = 1
        mat[(col_len - 1) * RB + b, 32 + b] = 1
    for a in range(col_len):
        mat[a * RB, 64 + a] = 1
        mat[a * RB + RB - 1, 96 + a] = 1
    return mat


def corner_matrix():
    mat = np.zeros((LANES, LANES), np.float32)
    for q, lane in enumerate((0, RB - 1, 32, 32 + RB - 1)):
        mat[lane, q] = 1
    return mat


def reverse_matrix(unit):
    mat = np.zeros((LANES, LANES), np.float32)
    for lane in range(LANES):
        mat[lane, (lane // unit) * unit + unit - 1 - lane % unit] = 1
    return mat


def spread_matrix(col_len):
    width = col_len * RB + LANES
    mat = np.zeros((LANES, width), np.float32)
    top, bottom = (col_len + 3) * RB, col_len * RB
    mat[0, top] = 1
    mat[1, top + RB - 1] = 1
    mat[2, bottom] = 1
    mat[3, bottom + RB - 1] = 1
    for a in range(col_len):
        mat[STRIP_LANE[2] + a, a * RB] = 1
        mat[STRIP_LANE[3] + a, a * RB + RB - 1] = 1
    return mat


def lane_iota(shape):
    return lax.broadcasted_iota(jnp.int32, shape, len(shape) - 1)


def side_tiles(fields, first_face, ring_ref, cornsel_ref):
    chan = fields[0].shape[0]
    lane = lane_iota((chan, LANES))
    rings = [
        jnp.dot(field, ring_ref[...], preferred_element_type=jnp.float32) for field in fields
    ]
    tiles = []
    for side in range(4):
        tile = jnp.zeros((chan, LANES), jnp.float32)
        for g, ring in enumerate(rings):
            moved = pltpu.roll(ring, ((g - side) * 32) % LANES, 1) if g != side else ring
            tile = jnp.where(lane // 32 == g, moved, tile)
        tiles.append(tile.astype(jnp.bfloat16))
    corners = jnp.zeros((chan, LANES), jnp.float32)
    for g, ring in enumerate(rings):
        picked = jnp.dot(
            ring.astype(jnp.bfloat16), cornsel_ref[...], preferred_element_type=jnp.float32
        )
        corners += pltpu.roll(picked, (first_face + g) * 4, 1)
    return (tiles, corners)


def hand_out(plan, steps, packs, corners, outs):
    chosen = iter(plan.chosen_sides())
    for out in outs[:-1]:
        for at in range(0, out.shape[0], steps):
            base = next(chosen) * steps
            for q in range(steps):
                out[at + q] = packs[base + q]
    packed = plan.pack_corners(corners).astype(jnp.bfloat16)
    for copy in range(outs[-1].shape[0]):
        outs[-1][copy] = packed


def ring_outs(faces, chan, plan):
    steps = faces // GROUP
    shapes = [(count * steps, chan, LANES) for count in plan.counts] + [plan.corner_shape(chan)]
    return [jax.ShapeDtypeStruct(shape, jnp.bfloat16) for shape in shapes]


def rings_kernel(steps, plan, field_ref, ring_ref, cornsel_ref, *refs):
    outs, (packs, corner_acc) = (refs[:-2], refs[-2:])
    step = pl.program_id(0)
    fields = [field_ref[g] for g in range(GROUP)]
    tiles, corners = side_tiles(fields, step * GROUP, ring_ref, cornsel_ref)
    for side, tile in enumerate(tiles):
        packs[side * steps + step] = tile

    @pl.when(step == 0)
    def _():
        corner_acc[...] = jnp.zeros_like(corner_acc)

    corner_acc[...] += corners

    @pl.when(step == steps - 1)
    def _():
        hand_out(plan, steps, packs, corner_acc[...], outs)


def whole_spec(array):
    zeros = (0,) * array.ndim
    return pl.BlockSpec(array.shape, lambda *_: zeros)


def rings_of(field, plan, ring, cornsel):
    faces, chan, tile = field.shape
    steps = faces // GROUP
    outs = ring_outs(faces, chan, plan)
    return pl.pallas_call(
        lambda *refs: rings_kernel(steps, plan, *refs),
        grid=(steps,),
        in_specs=[
            pl.BlockSpec((GROUP, chan, tile), lambda i: (i, 0, 0)),
            whole_spec(ring),
            whole_spec(cornsel),
        ],
        out_specs=[whole_spec(out) for out in outs],
        out_shape=outs,
        scratch_shapes=[
            pltpu.VMEM((4 * steps, chan, LANES), jnp.bfloat16),
            pltpu.VMEM((chan, LANES), jnp.float32),
        ],
        compiler_params=pltpu.CompilerParams(vmem_limit_bytes=VMEM_LIMIT),
        name="rings",
    )(field, ring, cornsel)


def halo_kernel(faces, units, unit, plan, *refs):
    table, tile_refs, (rev_ref, halo_ref, pool, turn_acc) = (refs[0], refs[1:-4], refs[-4:])
    chan = halo_ref.shape[1]
    lane = lane_iota((chan, LANES))
    at = 0
    for ref in tile_refs[:-1]:
        pool[at : at + ref.shape[0]] = ref[...]
        at += ref.shape[0]
    for k in range(tile_refs[-1].shape[0]):
        pool[at + k] = plan.unpack_corners(tile_refs[-1][k])
    corner_tile = jnp.zeros((chan, LANES), jnp.float32)
    most = max(units)
    rows = 4 * most
    for f in range(faces):
        tile = jnp.zeros((chan, LANES), jnp.float32)
        turned = jnp.zeros((chan, LANES), jnp.float32)
        for e in range(4):
            for un in range(units[e]):
                base = STRIP_LANE[e] + un * unit
                span = (lane >= base) & (lane < base + unit)
                entry = e * most + un
                source = pool[table[entry, f]].astype(jnp.float32)
                moved = pltpu.roll(source, table[rows + entry, f], 1)
                flip = table[2 * rows + entry, f] == 1
                tile = jnp.where(span & jnp.logical_not(flip), moved, tile)
                turned = jnp.where(span & flip, moved, turned)
        halo_ref[f] = tile.astype(jnp.bfloat16)
        turn_acc[f] = turned.astype(jnp.bfloat16)
        for c in range(4):
            source = pool[table[3 * rows + c, f]].astype(jnp.float32)
            moved = pltpu.roll(source, table[3 * rows + 4 + c, f], 1)
            corner_tile = jnp.where(lane == f * 4 + c, moved, corner_tile)
    turned = jnp.dot(
        turn_acc[...].reshape(faces * chan, LANES), rev_ref[...], preferred_element_type=jnp.float32
    ).reshape(faces, chan, LANES)
    for f in range(faces):
        halo_ref[f] += turned[f].astype(jnp.bfloat16)
    halo_ref[faces] = corner_tile.astype(jnp.bfloat16)


def assemble_halo(plan, table, tiles, rev, faces, units, unit):
    chan = tiles[0].shape[1]
    halo = jax.ShapeDtypeStruct((faces + 1, chan, LANES), jnp.bfloat16)
    vmem = pl.BlockSpec(memory_space=pltpu.VMEM)
    smem = pl.BlockSpec(memory_space=pltpu.SMEM)
    return pl.pallas_call(
        lambda *refs: halo_kernel(faces, units, unit, plan, *refs),
        in_specs=[smem] + [vmem] * (len(tiles) + 1),
        out_specs=vmem,
        out_shape=halo,
        scratch_shapes=[
            pltpu.VMEM((sum(t.shape[0] for t in tiles), chan, LANES), jnp.bfloat16),
            pltpu.VMEM((faces, chan, LANES), jnp.bfloat16),
        ],
        compiler_params=pltpu.CompilerParams(vmem_limit_bytes=VMEM_LIMIT),
        name="halo",
    )(table, *tiles, rev)


def conv_face(g, step, field_refs, halo_refs, corner_refs, taps_ref, spread_ref, stack_ref):
    chan, tile = field_refs[0].shape[1:]
    pieces = len(field_refs)
    total = chan * pieces
    width = tile + LANES
    for k in range(pieces):
        stack_ref[total + k * chan : total + (k + 1) * chan, :tile] = field_refs[k][g]
        stack_ref[total + k * chan : total + (k + 1) * chan, tile:] = halo_refs[k][g]
    halo = stack_ref[total : 2 * total, tile:].astype(jnp.float32)
    corners = jnp.concatenate([ref[0].astype(jnp.float32) for ref in corner_refs], axis=0)
    corners = pltpu.roll(corners, (LANES - (step * GROUP + g) * 4) % LANES, 1)
    lane = lane_iota((total, LANES))
    sides = jnp.where(lane < 4, corners, halo).astype(jnp.bfloat16)
    beside = jnp.dot(sides, spread_ref[...], preferred_element_type=jnp.float32)
    middle = stack_ref[total : 2 * total].astype(jnp.float32)
    col = lane_iota((total, width)) % RB
    stack_ref[:total] = jnp.where(col == 0, beside, pltpu.roll(middle, 1, 1)).astype(jnp.bfloat16)
    stack_ref[2 * total :] = jnp.where(
        col == RB - 1, beside, pltpu.roll(middle, width - 1, 1)
    ).astype(jnp.bfloat16)
    sums = jnp.dot(taps_ref[...], stack_ref[...], preferred_element_type=jnp.float32)
    above = pltpu.roll(sums[:chan], RB, 1)
    below = pltpu.roll(sums[2 * chan :], width - RB, 1)
    return (above + sums[chan : 2 * chan] + below)[:, :tile]


def split_refs(refs, *counts):
    out = []
    for count in counts:
        out.append(refs[:count])
        refs = refs[count:]
    return (*out, refs)


def forward_kernel(step, steps, pieces, plan, *refs):
    before = step
    fields, halos, corners, consts, old, refs = split_refs(
        refs, pieces, pieces, pieces, 5, 2 * before + (step > 0)
    )
    cot_ref, taps_ref, spread_ref, ring_ref, cornsel_ref = consts
    act_ref, gated_ref = refs[:2]
    made = []
    for g in range(GROUP):
        pre = conv_face(g, step, fields, halos, corners, taps_ref, spread_ref, refs[-1])
        sig = 1.0 / (1.0 + jnp.exp(-pre))
        act_ref[g] = (pre * sig).astype(jnp.bfloat16)
        gated = cot_ref[g].astype(jnp.float32) * sig * (1.0 + pre * (1.0 - sig))
        gated_ref[g] = gated.astype(jnp.bfloat16)
        made.append(gated.astype(jnp.bfloat16))
    tiles, corner = side_tiles(made, step * GROUP, ring_ref, cornsel_ref)
    if step < steps - 1:
        for side, tile in enumerate(tiles):
            refs[2][side] = tile
        refs[3][0] = corner.astype(jnp.bfloat16)
        return
    packs = refs[-2]
    for side in range(4):
        for q in range(before):
            packs[side * steps + q] = old[2 * q][side]
        packs[side * steps + step] = tiles[side]
    for q in range(before):
        corner += old[2 * q + 1][0].astype(jnp.float32)
    hand_out(plan, steps, packs, corner, refs[2:-2])


def conv_specs(fields, halos, step, own_blocks):
    _, chan, tile = fields[0].shape
    last = halos[0].shape[0] - 1
    field = 0 if own_blocks else step
    return (
        [pl.BlockSpec((GROUP, chan, tile), lambda i: (field, 0, 0)) for _ in fields]
        + [pl.BlockSpec((GROUP, chan, LANES), lambda i: (step, 0, 0)) for _ in halos]
        + [pl.BlockSpec((1, chan, LANES), lambda i: (last, 0, 0)) for _ in halos]
    )


def stack_scratch(chan, pieces, tile):
    return pltpu.VMEM((3 * chan * pieces, tile + LANES), jnp.bfloat16)


def forward(step, plan, fields, halos, cot, taps, spread, ring, cornsel, act, old):
    faces, chan, tile = fields[0].shape
    steps = faces // GROUP
    pieces = len(fields)
    if step < steps - 1:
        outs = [
            jax.ShapeDtypeStruct((4, chan, LANES), jnp.bfloat16),
            jax.ShapeDtypeStruct((1, chan, LANES), jnp.bfloat16),
        ]
        scratch = []
    else:
        outs = ring_outs(faces, chan, plan)
        scratch = [pltpu.VMEM((4 * steps, chan, LANES), jnp.bfloat16)]
    whole = jax.ShapeDtypeStruct((faces, chan, tile), jnp.bfloat16)
    chunk = jax.ShapeDtypeStruct((GROUP, chan, tile), jnp.bfloat16)
    block = pl.BlockSpec((GROUP, chan, tile), lambda i: (step, 0, 0))
    aside = [] if act is None else [act]
    args = [*fields, *halos, *halos, cot, taps, spread, ring, cornsel, *old, *aside]
    return pl.pallas_call(
        lambda *refs: forward_kernel(step, steps, pieces, plan, *refs),
        grid=(1,),
        in_specs=conv_specs(fields, halos, step, False)
        + [block, whole_spec(taps), whole_spec(spread), whole_spec(ring), whole_spec(cornsel)]
        + [whole_spec(array) for array in old]
        + [pl.BlockSpec(memory_space=pl.ANY) for _ in aside],
        out_specs=[block, whole_spec(chunk)] + [whole_spec(o) for o in outs],
        out_shape=[whole, chunk] + outs,
        input_output_aliases={len(args) - 1: 0} if aside else {},
        scratch_shapes=scratch + [stack_scratch(chan, pieces, tile)],
        compiler_params=pltpu.CompilerParams(vmem_limit_bytes=VMEM_LIMIT),
        name="forward",
    )(*args)


def backward_kernel(step, pieces, *refs):
    fields, halos, corners, consts, refs = split_refs(refs, pieces, pieces, pieces, 2)
    grad_ref, stack_ref = refs[-2:]
    for g in range(GROUP):
        total = conv_face(g, step, fields, halos, corners, *consts, stack_ref)
        grad_ref[g] = total.astype(jnp.bfloat16)


def backward(step, faces, fields, halos, taps, spread, grad):
    _, chan, tile = fields[0].shape
    pieces = len(fields)
    aside = [] if grad is None else [grad]
    args = [*fields, *halos, *halos, taps, spread, *aside]
    return pl.pallas_call(
        lambda *refs: backward_kernel(step, pieces, *refs),
        grid=(1,),
        in_specs=conv_specs(fields, halos, step, True)
        + [whole_spec(taps), whole_spec(spread)]
        + [pl.BlockSpec(memory_space=pl.ANY) for _ in aside],
        out_specs=pl.BlockSpec((GROUP, chan, tile), lambda i: (step, 0, 0)),
        out_shape=jax.ShapeDtypeStruct((faces, chan, tile), jnp.bfloat16),
        input_output_aliases={len(args) - 1: 0} if aside else {},
        scratch_shapes=[stack_scratch(chan, pieces, tile)],
        compiler_params=pltpu.CompilerParams(vmem_limit_bytes=VMEM_LIMIT),
        name="backward",
    )(*args)


def rows_of(*parts):
    return jnp.concatenate(parts, axis=0)


def halo_table(plan, edge_ref, corner_ref, px_count, py_count, col_len, unit):
    row_pos, col_pos = plan.place()
    faces = edge_ref.shape[2]
    side_len = px_count * RB
    most = RB // unit
    shape = (4 * most, faces)
    face = lane_iota(shape)
    row = lax.broadcasted_iota(jnp.int32, shape, 0)
    edge, un = (row // most, row % most)
    g, s, r = [
        rows_of(*[edge_ref[i, e : e + 1] for e in range(4) for _ in range(most)]) for i in range(3)
    ]
    border = ((edge == 0) & (col_pos == 0)) | ((edge == 1) & (col_pos == py_count - 1))
    border |= ((edge == 2) & (row_pos == 0)) | ((edge == 3) & (row_pos == px_count - 1))
    at = jnp.where(edge < 2, row_pos * RB, col_pos * col_len) + un * unit
    at = jnp.clip(at, 0, side_len - unit)
    at = jnp.where(r == 1, side_len - unit - at, at)
    line_tile, line_lane = plan.strip_cell(g, s, at)
    tile = jnp.where(border, line_tile, plan.near_cell(edge, face))
    lane = jnp.where(border, line_lane, (face % GROUP) * 32 + un * unit)
    first = jnp.where(edge == 0, STRIP_LANE[0], jnp.where(edge == 1, STRIP_LANE[1], edge * 32 - 32))
    shift = (first + un * unit - lane + LANES) % LANES
    flip = jnp.where(border & (r == 1), 1, 0)

    shape = (4, faces)
    face = lane_iota(shape)
    c = lax.broadcasted_iota(jnp.int32, shape, 0)
    down, right = (c // 2, c % 2)
    row_on = ((down == 0) & (col_pos == 0)) | ((down == 1) & (col_pos == py_count - 1))
    col_on = ((right == 0) & (row_pos == 0)) | ((right == 1) & (row_pos == px_count - 1))
    row_at = row_pos * RB + jnp.where(right == 1, RB, -1)
    col_at = col_pos * col_len + jnp.where(down == 1, col_len, -1)
    edge_of = lambda i, edges: rows_of(*[edge_ref[i, e : e + 1] for e in edges])
    g, s, r = [
        jnp.where(row_on, edge_of(i, (0, 0, 1, 1)), edge_of(i, (2, 3, 2, 3))) for i in range(3)
    ]
    at = jnp.clip(jnp.where(row_on, row_at, col_at), 0, side_len - 1)
    at = jnp.where(r == 1, side_len - 1 - at, at)
    h, q = [rows_of(*[corner_ref[k, i : i + 1] for k in range(4)]) for i in range(2)]
    both = row_on & col_on
    g = jnp.where(both, h, g)
    s = jnp.where(both, q // 2, s)
    at = jnp.where(both, (q % 2) * (side_len - 1), at)
    line_tile, line_lane = plan.corner_cell(g, s, at)
    diag_px = jnp.clip(row_pos + 2 * right - 1, 0, px_count - 1)
    diag_py = jnp.clip(col_pos + 2 * down - 1, 0, py_count - 1)
    diag_tile, diag_lane = plan.diagonal_cell(face, 3 - c, diag_px, diag_py)
    on = row_on | col_on
    corner_at = jnp.where(on, line_tile, diag_tile)
    corner_lane = jnp.where(on, line_lane, diag_lane)
    corner_shift = (face * 4 + c - corner_lane + LANES) % LANES
    return rows_of(tile, shift, flip, corner_at, corner_shift)


def setup_kernel(plan, chan, shape, edge_ref, corner_ref, weight_ref, table_ref, taps_ref, back_ref, turn):
    table_ref[...] = halo_table(plan, edge_ref, corner_ref, *shape)
    total = weight_ref.shape[2]
    own = lax.axis_index("ch") * chan
    shift = (total - own) % total
    for i in range(3):
        for j in range(3):
            turn[...] = weight_ref[i, j].astype(jnp.float32)
            rows = pltpu.roll(turn[pl.ds(pl.multiple_of(own, chan), chan)], shift, 1)
            cols = slice(j * total, (j + 1) * total)
            taps_ref[i * chan : (i + 1) * chan, cols] = rows.astype(jnp.bfloat16)
            turn[...] = turn[...].T
            rows = pltpu.roll(turn[pl.ds(pl.multiple_of(own, chan), chan)], shift, 1)
            cols = slice((2 - j) * total, (3 - j) * total)
            back_ref[(2 - i) * chan : (3 - i) * chan, cols] = rows.astype(jnp.bfloat16)


def setup(plan, edge_table, corner_table, weight, chan, counts, col_len, unit):
    edges = jnp.transpose(edge_table, (2, 1, 0))
    corners = jnp.transpose(corner_table, (1, 2, 0))
    total = weight.shape[2]
    vmem = pl.BlockSpec(memory_space=pltpu.VMEM)
    taps = jax.ShapeDtypeStruct((3 * chan, 3 * total), jnp.bfloat16)
    table = jax.ShapeDtypeStruct((12 * (RB // unit) + 8, edges.shape[2]), jnp.int32)
    return pl.pallas_call(
        lambda *refs: setup_kernel(plan, chan, (*counts, col_len, unit), *refs),
        in_specs=[vmem] * 3,
        out_specs=[vmem] * 3,
        out_shape=[table, taps, taps],
        scratch_shapes=[pltpu.VMEM((total, total), jnp.float32)],
        compiler_params=pltpu.CompilerParams(vmem_limit_bytes=VMEM_LIMIT),
        name="setup",
    )(edges, corners, weight)


def from_others(array, ch_count):
    return [array] + [
        lax.ppermute(array, "ch", [((i + k) % ch_count, i) for i in range(ch_count)])
        for k in range(1, ch_count)
    ]


class Place:
    @staticmethod
    def place():
        return (lax.axis_index("px"), lax.axis_index("py"))


class SquareHalo(Place):
    counts = (2, 1, 1, 2)

    def __init__(self, quads):
        self.quads = quads

    def corner_shape(self, chan):
        return (16, chan // 2, LANES)

    def pack_corners(self, corners):
        half = corners.shape[0] // 2
        return corners[:half] + pltpu.roll(corners[half:], LANES // 2, 1)

    def unpack_corners(self, packed):
        upper = packed.astype(jnp.float32)
        both = jnp.concatenate([upper, pltpu.roll(upper, LANES // 2, 1)], axis=0)
        return both.astype(jnp.bfloat16)

    def roles(self):
        row_pos, col_pos = self.place()
        px_end = (row_pos == 0) | (row_pos == 3)
        py_end = (col_pos == 0) | (col_pos == 3)
        side = jnp.where(
            py_end, jnp.where(col_pos == 0, 0, 1), jnp.where(row_pos == 0, 2, 3)
        )
        corner = px_end & py_end
        middle = (px_end | py_end) & jnp.logical_not(corner)
        return (px_end, corner, middle, side, jnp.where(px_end, col_pos, row_pos))

    def chosen_sides(self):
        row_pos, col_pos = self.place()
        px_end, corner, middle, side, seg = self.roles()
        row_line = jnp.where(col_pos == 0, 0, 1)
        col_line = jnp.where(row_pos == 0, 2, 3)
        to_px, to_py = (jnp.where(row_pos == 1, 3, 2), jnp.where(col_pos == 1, 1, 0))
        facing = jnp.where(px_end, to_py, to_px)
        return [
            jnp.where(seg == 1, side, facing),
            jnp.where(seg == 1, facing, side),
            jnp.where(row_pos % 2 == 0, 3, 2),
            jnp.where(col_pos % 2 == 0, 1, 0),
            jnp.where(corner, row_line, jnp.where(middle, side, to_py)),
            jnp.where(corner, col_line, side),
        ]

    def exchange(self, pair, col_side, row_side, lines, corner):
        every = [(x, y) for x in range(4) for y in range(4)]
        axes = ("px", "py")
        swap = lambda array, pairs: lax.ppermute(
            array, axes, [(a[0] * 4 + a[1], b[0] * 4 + b[1]) for a, b in pairs]
        )
        ends = (0, 3)
        corners = [(x, y) for x in ends for y in ends]
        spot = lambda side, seg: ((seg, 0), (seg, 3), (0, seg), (3, seg))[side]
        beside = [(spot(side, k), spot(side, 3 - k)) for side in range(4) for k in (1, 2)]
        beside += [((x, y), (3 - x, y)) for x in (1, 2) for y in (1, 2)]
        paired = swap(pair, beside)
        near_col = swap(col_side, [((x, y), (x ^ 1, y)) for x, y in every])
        near_row = swap(row_side, [((x, y), (x, y ^ 1)) for x, y in every])
        _, _, middle, _, seg = self.roles()
        slot = lax.broadcasted_iota(jnp.int32, (2 * self.quads, 1, 1), 0) // self.quads
        lines = jnp.where(middle & (slot != seg - 1), paired, lines)
        across = []
        for j in (1, 2, 3):
            pairs = [(spot(side, k), spot(side ^ j, k)) for side in range(4) for k in (1, 2)]
            pairs += [(corners[c], corners[c ^ j]) for c in range(4)]
            if j == 1:
                pairs += [((x, y), (x, 3 - y)) for x in (1, 2) for y in (1, 2)]
            across.append(swap(lines, pairs))
        corner, lines = lax.optimization_barrier((corner, lines))
        ends_of = lax.all_to_all(corner, axes, 0, 0, tiled=True)
        return [lines, *across, paired, near_col, near_row, ends_of]

    def strip_cell(self, g, s, at):
        row_pos, col_pos = self.place()
        _, corner, _, side, _ = self.roles()
        slot = 2 * self.quads
        k = at // RB
        me = jnp.where(row_pos > 0, 2, 0) + jnp.where(col_pos > 0, 1, 0)
        far = jnp.where(k > 0, 1, 0)
        owner = jnp.where(s < 2, 2 * far + s, 2 * (s - 2) + far)
        at_corner = (me ^ owner) * slot + (s // 2) * self.quads
        at_middle = (side ^ s) * slot + (k - 1) * self.quads
        return (jnp.where(corner, at_corner, at_middle) + g // GROUP, (g % GROUP) * 32)

    def near_cell(self, edge, face):
        row_pos, col_pos = self.place()
        px_end, _, _, _, seg = self.roles()
        slot = 2 * self.quads
        paired = 4 * slot + (seg - 1) * self.quads
        near_col, near_row = (5 * slot, 5 * slot + self.quads)
        by_col = jnp.where(row_pos % 2 == 3 - edge, near_col, paired)
        by_row = jnp.where(col_pos % 2 == 1 - edge, near_row, jnp.where(px_end, paired, slot))
        return jnp.where(edge < 2, by_row, by_col) + face // GROUP

    def corner_cell(self, g, s, at):
        seg, hi = (at // RB, jnp.where(at % RB == 0, 0, 1))
        owner = jnp.where(s < 2, seg * 4 + 3 * s, 12 * (s - 2) + seg)
        q = jnp.where(s < 2, 2 * s + hi, s - 2 + 2 * hi)
        return (12 * self.quads + owner, g * 4 + q)

    def diagonal_cell(self, face, q, px, py):
        return (12 * self.quads + px * 4 + py, face * 4 + q)


class GatheredHalo(Place):
    counts = (1, 1, 1, 1, 2)

    def corner_shape(self, chan):
        return (1, chan, LANES)

    def pack_corners(self, corners):
        return corners

    def unpack_corners(self, packed):
        return packed

    def __init__(self, quads, px_count, py_count, col_len):
        self.quads = quads
        self.size = (px_count, py_count)
        self.col_len = col_len

    def chosen_sides(self):
        row_pos, col_pos = self.place()
        return [0, 1, 2, 3, jnp.where(col_pos == 0, 0, 1), jnp.where(row_pos == 0, 2, 3)]

    def exchange(self, top, bottom, left, right, lines, corner):
        px_count, py_count = self.size
        up = lambda n: [(i, i + 1) for i in range(n - 1)]
        down = lambda n: [(i + 1, i) for i in range(n - 1)]
        return [
            lax.ppermute(bottom, "py", up(py_count)),
            lax.ppermute(top, "py", down(py_count)),
            lax.ppermute(right, "px", up(px_count)),
            lax.ppermute(left, "px", down(px_count)),
            lax.all_gather(lines, ("px", "py"), axis=0, tiled=True),
            lax.all_gather(corner, ("px", "py"), axis=0, tiled=True),
        ]

    def strip_cell(self, g, s, at):
        px_count, py_count = self.size
        length = jnp.where(s < 2, RB, self.col_len)
        seg = at // length
        px = jnp.where(s < 2, seg, (s - 2) * (px_count - 1))
        py = jnp.where(s < 2, s * (py_count - 1), seg)
        tile = (4 + (px * py_count + py) * 2 + s // 2) * self.quads + g // GROUP
        return (tile, (g % GROUP) * 32 + at % length)

    def near_cell(self, edge, face):
        return edge * self.quads + face // GROUP

    def corner_cell(self, g, s, at):
        return self.strip_cell(g, s, at)

    def diagonal_cell(self, face, q, px, py):
        px_count, py_count = self.size
        base = (4 + 2 * px_count * py_count) * self.quads
        return (base + px * py_count + py, face * 4 + q)


def local(features, cotangent, weight, edge_table, corner_table):
    chan, faces = features.shape[:2]
    tile = features.shape[4]
    col_len = tile // RB
    unit = min(RB, col_len)
    units = (RB // unit, RB // unit, col_len // unit, col_len // unit)
    px_count, py_count, ch_count = [lax.axis_size(name) for name in ("px", "py", "ch")]
    ring = jnp.asarray(ring_matrix(col_len), jnp.bfloat16)
    cornsel = jnp.asarray(corner_matrix(), jnp.bfloat16)
    spread = jnp.asarray(spread_matrix(col_len), jnp.bfloat16)
    rev = jnp.asarray(reverse_matrix(unit), jnp.bfloat16)
    if px_count == py_count == 4 and col_len == RB and chan % 32 == 0:
        plan = SquareHalo(faces // GROUP)
    else:
        plan = GatheredHalo(faces // GROUP, px_count, py_count, col_len)

    feats = jnp.transpose(features.reshape(chan, faces, tile), (1, 0, 2))
    cot = jnp.transpose(cotangent.reshape(chan, faces, tile), (1, 0, 2))
    fields = from_others(feats, ch_count)
    parts = rings_of(feats, plan, ring, cornsel)
    table, taps, back_taps = setup(
        plan, edge_table, corner_table, weight, chan, (px_count, py_count), col_len, unit
    )
    tiles = plan.exchange(*parts)
    halo = assemble_halo(plan, table, tiles, rev, faces, units, unit)
    halos = from_others(halo, ch_count)
    act, old, chunks = (None, [], [])
    for step in range(faces // GROUP):
        act, gated, *parts = forward(
            step, plan, fields, halos, cot, taps, spread, ring, cornsel, act, old
        )
        old = old + parts
        chunks.append(from_others(gated, ch_count))

    tiles = plan.exchange(*parts)
    halo = assemble_halo(plan, table, tiles, rev, faces, units, unit)
    halos = from_others(halo, ch_count)
    grad = None
    for step, fields in enumerate(chunks):
        grad = backward(step, faces, fields, halos, back_taps, spread, grad)

    shape = (chan, faces, 1, 1, tile)
    return (
        jnp.transpose(act, (1, 0, 2)).reshape(shape),
        jnp.transpose(grad, (1, 0, 2)).reshape(shape),
    )


def solution(mesh):
    spec = P("ch", None, "py", "px", None)
    return jax.shard_map(
        local,
        mesh=mesh,
        in_specs=(spec, spec, P(), P(), P()),
        out_specs=(spec, spec),
        check_vma=False,
    )
```

```python
import jax
import jax.numpy as jnp
import numpy as np
from jax import lax
from jax.experimental import pallas as pl
from jax.experimental.pallas import tpu as pltpu
from jax.sharding import PartitionSpec as P

RB = 32
GROUP = 4
LANES = 128
CALLS = (3,)
VMEM_LIMIT = 60 * 1024 * 1024
STRIP_LANE = (96, 0, 32, 64)


def ring_matrix(col_len):
    mat = np.zeros((col_len * RB, LANES), np.float32)
    for b in range(RB):
        mat[b, b] = 1
        mat[(col_len - 1) * RB + b, 32 + b] = 1
    for a in range(col_len):
        mat[a * RB, 64 + a] = 1
        mat[a * RB + RB - 1, 96 + a] = 1
    return mat


def corner_matrix():
    mat = np.zeros((LANES, LANES), np.float32)
    for q, lane in enumerate((0, RB - 1, 32, 32 + RB - 1)):
        mat[lane, q] = 1
    return mat


def reverse_matrix(unit):
    mat = np.zeros((LANES, LANES), np.float32)
    for lane in range(LANES):
        mat[lane, (lane // unit) * unit + unit - 1 - lane % unit] = 1
    return mat


def spread_matrix(col_len):
    width = col_len * RB + LANES
    mat = np.zeros((LANES, width), np.float32)
    top, bottom = (col_len + 3) * RB, col_len * RB
    mat[0, top] = 1
    mat[1, top + RB - 1] = 1
    mat[2, bottom] = 1
    mat[3, bottom + RB - 1] = 1
    for a in range(col_len):
        mat[STRIP_LANE[2] + a, a * RB] = 1
        mat[STRIP_LANE[3] + a, a * RB + RB - 1] = 1
    return mat


def lane_iota(shape):
    return lax.broadcasted_iota(jnp.int32, shape, len(shape) - 1)


def side_tiles(fields, first_face, ring_ref, cornsel_ref):
    chan = fields.shape[0] // GROUP
    lane = lane_iota((chan, LANES))
    flat = jnp.dot(fields, ring_ref[...], preferred_element_type=jnp.float32)
    picked = jnp.dot(
        flat.astype(jnp.bfloat16), cornsel_ref[...], preferred_element_type=jnp.float32
    )
    rings = [flat[g * chan : (g + 1) * chan] for g in range(GROUP)]
    tiles = []
    for side in range(4):
        tile = jnp.zeros((chan, LANES), jnp.float32)
        for g, ring in enumerate(rings):
            moved = pltpu.roll(ring, ((g - side) * 32) % LANES, 1) if g != side else ring
            tile = jnp.where(lane // 32 == g, moved, tile)
        tiles.append(tile.astype(jnp.bfloat16))
    corners = jnp.zeros((chan, LANES), jnp.float32)
    for g in range(GROUP):
        corners += pltpu.roll(picked[g * chan : (g + 1) * chan], (first_face + g) * 4, 1)
    return (tiles, corners)


def hand_out(plan, steps, packs, corners, outs):
    chosen = iter(plan.chosen_sides())
    for out in outs[:-1]:
        for at in range(0, out.shape[0], steps):
            base = next(chosen) * steps
            for q in range(steps):
                out[at + q] = packs[base + q]
    packed = plan.pack_corners(corners).astype(jnp.bfloat16)
    for copy in range(outs[-1].shape[0]):
        outs[-1][copy] = packed


def ring_outs(faces, chan, plan):
    steps = faces // GROUP
    shapes = [(count * steps, chan, LANES) for count in plan.counts] + [plan.corner_shape(chan)]
    return [jax.ShapeDtypeStruct(shape, jnp.bfloat16) for shape in shapes]


def rings_kernel(steps, plan, field_ref, ring_ref, cornsel_ref, *refs):
    outs, (packs, corner_acc) = (refs[:-2], refs[-2:])
    step = pl.program_id(0)
    fields = field_ref[...].reshape(-1, field_ref.shape[2])
    tiles, corners = side_tiles(fields, step * GROUP, ring_ref, cornsel_ref)
    for side, tile in enumerate(tiles):
        packs[side * steps + step] = tile

    @pl.when(step == 0)
    def _():
        corner_acc[...] = jnp.zeros_like(corner_acc)

    corner_acc[...] += corners

    @pl.when(step == steps - 1)
    def _():
        hand_out(plan, steps, packs, corner_acc[...], outs)


def whole_spec(array):
    zeros = (0,) * array.ndim
    return pl.BlockSpec(array.shape, lambda *_: zeros)


def rings_of(field, plan, ring, cornsel):
    faces, chan, tile = field.shape
    steps = faces // GROUP
    outs = ring_outs(faces, chan, plan)
    return pl.pallas_call(
        lambda *refs: rings_kernel(steps, plan, *refs),
        grid=(steps,),
        in_specs=[
            pl.BlockSpec((GROUP, chan, tile), lambda i: (i, 0, 0)),
            whole_spec(ring),
            whole_spec(cornsel),
        ],
        out_specs=[whole_spec(out) for out in outs],
        out_shape=outs,
        scratch_shapes=[
            pltpu.VMEM((4 * steps, chan, LANES), jnp.bfloat16),
            pltpu.VMEM((chan, LANES), jnp.float32),
        ],
        compiler_params=pltpu.CompilerParams(vmem_limit_bytes=VMEM_LIMIT),
        name="rings",
    )(field, ring, cornsel)


def halo_kernel(faces, units, unit, plan, *refs):
    table, tile_refs, (rev_ref, halo_ref, pool, turn_acc) = (refs[0], refs[1:-4], refs[-4:])
    chan = halo_ref.shape[1]
    lane = lane_iota((chan, LANES))
    at = 0
    for ref in tile_refs[:-1]:
        pool[at : at + ref.shape[0]] = ref[...]
        at += ref.shape[0]
    for k in range(tile_refs[-1].shape[0]):
        pool[at + k] = plan.unpack_corners(tile_refs[-1][k])
    corner_tile = jnp.zeros((chan, LANES), jnp.float32)
    most = max(units)
    rows = 4 * most
    for f in range(faces):
        tile = jnp.zeros((chan, LANES), jnp.float32)
        turned = jnp.zeros((chan, LANES), jnp.float32)
        for e in range(4):
            for un in range(units[e]):
                base = STRIP_LANE[e] + un * unit
                span = (lane >= base) & (lane < base + unit)
                entry = e * most + un
                source = pool[table[entry, f]].astype(jnp.float32)
                moved = pltpu.roll(source, table[rows + entry, f], 1)
                flip = table[2 * rows + entry, f] == 1
                tile = jnp.where(span & jnp.logical_not(flip), moved, tile)
                turned = jnp.where(span & flip, moved, turned)
        halo_ref[f] = tile.astype(jnp.bfloat16)
        turn_acc[f] = turned.astype(jnp.bfloat16)
        for c in range(4):
            source = pool[table[3 * rows + c, f]].astype(jnp.float32)
            moved = pltpu.roll(source, table[3 * rows + 4 + c, f], 1)
            corner_tile = jnp.where(lane == f * 4 + c, moved, corner_tile)
    turned = jnp.dot(
        turn_acc[...].reshape(faces * chan, LANES), rev_ref[...], preferred_element_type=jnp.float32
    ).reshape(faces, chan, LANES)
    for f in range(faces):
        halo_ref[f] += turned[f].astype(jnp.bfloat16)
    halo_ref[faces] = corner_tile.astype(jnp.bfloat16)


def assemble_halo(plan, table, tiles, rev, faces, units, unit):
    chan = tiles[0].shape[1]
    halo = jax.ShapeDtypeStruct((faces + 1, chan, LANES), jnp.bfloat16)
    vmem = pl.BlockSpec(memory_space=pltpu.VMEM)
    smem = pl.BlockSpec(memory_space=pltpu.SMEM)
    return pl.pallas_call(
        lambda *refs: halo_kernel(faces, units, unit, plan, *refs),
        in_specs=[smem] + [vmem] * (len(tiles) + 1),
        out_specs=vmem,
        out_shape=halo,
        scratch_shapes=[
            pltpu.VMEM((sum(t.shape[0] for t in tiles), chan, LANES), jnp.bfloat16),
            pltpu.VMEM((faces, chan, LANES), jnp.bfloat16),
        ],
        compiler_params=pltpu.CompilerParams(vmem_limit_bytes=VMEM_LIMIT),
        name="halo",
    )(table, *tiles, rev)


def sides_of(step, halo_refs, corner_refs, spread_ref, beside_ref):
    corners = jnp.concatenate([ref[0].astype(jnp.float32) for ref in corner_refs], axis=0)
    lane = lane_iota(corners.shape)
    sides = []
    for g in range(GROUP):
        halo = jnp.concatenate([ref[g].astype(jnp.float32) for ref in halo_refs], axis=0)
        moved = pltpu.roll(corners, (LANES - (step * GROUP + g) * 4) % LANES, 1)
        sides.append(jnp.where(lane < 4, moved, halo).astype(jnp.bfloat16))
    beside = jnp.dot(
        jnp.concatenate(sides, axis=0), spread_ref[...], preferred_element_type=jnp.float32
    )
    beside_ref[...] = beside.astype(jnp.bfloat16).reshape(beside_ref.shape)


def conv_face(g, field_refs, halo_refs, taps_ref, beside_ref, stack_ref):
    chan, tile = field_refs[0].shape[1:]
    total = chan * len(field_refs)
    width = tile + LANES
    for k, (field, halo) in enumerate(zip(field_refs, halo_refs)):
        stack_ref[total + k * chan : total + (k + 1) * chan, :tile] = field[g]
        stack_ref[total + k * chan : total + (k + 1) * chan, tile:] = halo[g]
    middle = stack_ref[total : 2 * total]
    beside = beside_ref[g]
    col = lane_iota((total, width)) % RB
    stack_ref[:total] = jnp.where(col == 0, beside, pltpu.roll(middle, 1, 1))
    stack_ref[2 * total :] = jnp.where(col == RB - 1, beside, pltpu.roll(middle, width - 1, 1))
    sums = jnp.dot(taps_ref[...], stack_ref[...], preferred_element_type=jnp.float32)
    above = pltpu.roll(sums[:chan], RB, 1)
    below = pltpu.roll(sums[2 * chan :], width - RB, 1)
    return (above + sums[chan : 2 * chan] + below)[:, :tile]


def split_refs(refs, *counts):
    out = []
    for count in counts:
        out.append(refs[:count])
        refs = refs[count:]
    return (*out, refs)


def forward_kernel(first, count, steps, pieces, plan, *refs):
    olds = 3 if first else 0
    fields, halos, corners, consts, old, refs = split_refs(refs, pieces, pieces, pieces, 5, olds)
    cot_ref, taps_ref, spread_ref, ring_ref, cornsel_ref = consts
    outs, (packs, corner_acc, made, beside_ref, stacks) = (refs[:-5], refs[-5:])
    act_ref, gated_ref = outs[:2]
    here = pl.program_id(0)
    step = first + here

    @pl.when(here == 0)
    def _():
        if first:
            packs[...] = old[0][...]
            corner_acc[...] = old[1][0].astype(jnp.float32)
        else:
            corner_acc[...] = jnp.zeros_like(corner_acc)

    sides_of(step, halos, corners, spread_ref, beside_ref)
    chan = act_ref.shape[1]
    for g in range(GROUP):
        pre = conv_face(g, fields, halos, taps_ref, beside_ref, stacks.at[g % 2])
        sig = 1.0 / (1.0 + jnp.exp(-pre))
        act_ref[g] = (pre * sig).astype(jnp.bfloat16)
        gated = cot_ref[g].astype(jnp.float32) * sig * (1.0 + pre * (1.0 - sig))
        gated_ref[g] = gated.astype(jnp.bfloat16)
        made[g * chan : (g + 1) * chan] = gated.astype(jnp.bfloat16)
    tiles, corner = side_tiles(made[...], step * GROUP, ring_ref, cornsel_ref)
    for side, tile in enumerate(tiles):
        packs[side * steps + step] = tile
    corner_acc[...] += corner

    @pl.when(here == count - 1)
    def _():
        if first + count == steps:
            hand_out(plan, steps, packs, corner_acc[...], outs[2:])
        else:
            outs[2][...] = packs[...]
            outs[3][0] = corner_acc[...].astype(jnp.bfloat16)


def conv_specs(fields, halos, first, field_first):
    _, chan, tile = fields[0].shape
    last = halos[0].shape[0] - 1
    return (
        [pl.BlockSpec((GROUP, chan, tile), lambda i: (field_first + i, 0, 0)) for _ in fields]
        + [pl.BlockSpec((GROUP, chan, LANES), lambda i: (first + i, 0, 0)) for _ in halos]
        + [pl.BlockSpec((1, chan, LANES), lambda i: (last, 0, 0)) for _ in halos]
    )


def conv_scratch(chan, pieces, tile):
    total = chan * pieces
    return [
        pltpu.VMEM((GROUP, total, tile + LANES), jnp.bfloat16),
        pltpu.VMEM((2, 3 * total, tile + LANES), jnp.bfloat16),
    ]


def forward(first, count, plan, fields, halos, cot, taps, spread, ring, cornsel, old):
    faces, chan, tile = fields[0].shape
    steps = faces // GROUP
    pieces = len(fields)
    if first + count < steps:
        outs = [
            jax.ShapeDtypeStruct((4 * steps, chan, LANES), jnp.bfloat16),
            jax.ShapeDtypeStruct((1, chan, LANES), jnp.bfloat16),
        ]
    else:
        outs = ring_outs(faces, chan, plan)
    whole = jax.ShapeDtypeStruct((faces, chan, tile), jnp.bfloat16)
    chunk = jax.ShapeDtypeStruct((count * GROUP, chan, tile), jnp.bfloat16)
    block = pl.BlockSpec((GROUP, chan, tile), lambda i: (first + i, 0, 0))
    args = [*fields, *halos, *halos, cot, taps, spread, ring, cornsel, *old]
    return pl.pallas_call(
        lambda *refs: forward_kernel(first, count, steps, pieces, plan, *refs),
        grid=(count,),
        in_specs=conv_specs(fields, halos, first, first)
        + [block, whole_spec(taps), whole_spec(spread), whole_spec(ring), whole_spec(cornsel)]
        + [whole_spec(array) for array in old[:2]]
        + [pl.BlockSpec(memory_space=pl.ANY) for _ in old[2:]],
        out_specs=[block, pl.BlockSpec((GROUP, chan, tile), lambda i: (i, 0, 0))]
        + [whole_spec(o) for o in outs],
        out_shape=[whole, chunk] + outs,
        input_output_aliases={len(args) - 1: 0} if old else {},
        scratch_shapes=[
            pltpu.VMEM((4 * steps, chan, LANES), jnp.bfloat16),
            pltpu.VMEM((chan, LANES), jnp.float32),
            pltpu.VMEM((GROUP * chan, tile), jnp.bfloat16),
        ]
        + conv_scratch(chan, pieces, tile),
        compiler_params=pltpu.CompilerParams(vmem_limit_bytes=VMEM_LIMIT),
        name="forward",
    )(*args)


def backward_kernel(first, pieces, *refs):
    fields, halos, corners, consts, refs = split_refs(refs, pieces, pieces, pieces, 2)
    taps_ref, spread_ref = consts
    grad_ref, beside_ref, stacks = refs[-3:]
    sides_of(first + pl.program_id(0), halos, corners, spread_ref, beside_ref)
    for g in range(GROUP):
        total = conv_face(g, fields, halos, taps_ref, beside_ref, stacks.at[g % 2])
        grad_ref[g] = total.astype(jnp.bfloat16)


def backward(first, faces, fields, halos, taps, spread, grad):
    held, chan, tile = fields[0].shape
    pieces = len(fields)
    aside = [] if grad is None else [grad]
    args = [*fields, *halos, *halos, taps, spread, *aside]
    return pl.pallas_call(
        lambda *refs: backward_kernel(first, pieces, *refs),
        grid=(held // GROUP,),
        in_specs=conv_specs(fields, halos, first, 0)
        + [whole_spec(taps), whole_spec(spread)]
        + [pl.BlockSpec(memory_space=pl.ANY) for _ in aside],
        out_specs=pl.BlockSpec((GROUP, chan, tile), lambda i: (first + i, 0, 0)),
        out_shape=jax.ShapeDtypeStruct((faces, chan, tile), jnp.bfloat16),
        input_output_aliases={len(args) - 1: 0} if aside else {},
        scratch_shapes=conv_scratch(chan, pieces, tile),
        compiler_params=pltpu.CompilerParams(vmem_limit_bytes=VMEM_LIMIT),
        name="backward",
    )(*args)


def rows_of(*parts):
    return jnp.concatenate(parts, axis=0)


def halo_table(plan, edge_ref, corner_ref, px_count, py_count, col_len, unit):
    row_pos, col_pos = plan.place()
    faces = edge_ref.shape[2]
    side_len = px_count * RB
    most = RB // unit
    shape = (4 * most, faces)
    face = lane_iota(shape)
    row = lax.broadcasted_iota(jnp.int32, shape, 0)
    edge, un = (row // most, row % most)
    g, s, r = [
        rows_of(*[edge_ref[i, e : e + 1] for e in range(4) for _ in range(most)]) for i in range(3)
    ]
    border = ((edge == 0) & (col_pos == 0)) | ((edge == 1) & (col_pos == py_count - 1))
    border |= ((edge == 2) & (row_pos == 0)) | ((edge == 3) & (row_pos == px_count - 1))
    at = jnp.where(edge < 2, row_pos * RB, col_pos * col_len) + un * unit
    at = jnp.clip(at, 0, side_len - unit)
    at = jnp.where(r == 1, side_len - unit - at, at)
    line_tile, line_lane = plan.strip_cell(g, s, at)
    tile = jnp.where(border, line_tile, plan.near_cell(edge, face))
    lane = jnp.where(border, line_lane, (face % GROUP) * 32 + un * unit)
    first = jnp.where(edge == 0, STRIP_LANE[0], jnp.where(edge == 1, STRIP_LANE[1], edge * 32 - 32))
    shift = (first + un * unit - lane + LANES) % LANES
    flip = jnp.where(border & (r == 1), 1, 0)

    shape = (4, faces)
    face = lane_iota(shape)
    c = lax.broadcasted_iota(jnp.int32, shape, 0)
    down, right = (c // 2, c % 2)
    row_on = ((down == 0) & (col_pos == 0)) | ((down == 1) & (col_pos == py_count - 1))
    col_on = ((right == 0) & (row_pos == 0)) | ((right == 1) & (row_pos == px_count - 1))
    row_at = row_pos * RB + jnp.where(right == 1, RB, -1)
    col_at = col_pos * col_len + jnp.where(down == 1, col_len, -1)
    edge_of = lambda i, edges: rows_of(*[edge_ref[i, e : e + 1] for e in edges])
    g, s, r = [
        jnp.where(row_on, edge_of(i, (0, 0, 1, 1)), edge_of(i, (2, 3, 2, 3))) for i in range(3)
    ]
    at = jnp.clip(jnp.where(row_on, row_at, col_at), 0, side_len - 1)
    at = jnp.where(r == 1, side_len - 1 - at, at)
    h, q = [rows_of(*[corner_ref[k, i : i + 1] for k in range(4)]) for i in range(2)]
    both = row_on & col_on
    g = jnp.where(both, h, g)
    s = jnp.where(both, q // 2, s)
    at = jnp.where(both, (q % 2) * (side_len - 1), at)
    line_tile, line_lane = plan.corner_cell(g, s, at)
    diag_px = jnp.clip(row_pos + 2 * right - 1, 0, px_count - 1)
    diag_py = jnp.clip(col_pos + 2 * down - 1, 0, py_count - 1)
    diag_tile, diag_lane = plan.diagonal_cell(face, 3 - c, diag_px, diag_py)
    on = row_on | col_on
    corner_at = jnp.where(on, line_tile, diag_tile)
    corner_lane = jnp.where(on, line_lane, diag_lane)
    corner_shift = (face * 4 + c - corner_lane + LANES) % LANES
    return rows_of(tile, shift, flip, corner_at, corner_shift)


def setup_kernel(plan, chan, shape, edge_ref, corner_ref, weight_ref, table_ref, taps_ref, back_ref, turn):
    table_ref[...] = halo_table(plan, edge_ref, corner_ref, *shape)
    total = weight_ref.shape[2]
    own = lax.axis_index("ch") * chan
    shift = (total - own) % total
    for i in range(3):
        for j in range(3):
            turn[...] = weight_ref[i, j].astype(jnp.float32)
            rows = pltpu.roll(turn[pl.ds(pl.multiple_of(own, chan), chan)], shift, 1)
            cols = slice(j * total, (j + 1) * total)
            taps_ref[i * chan : (i + 1) * chan, cols] = rows.astype(jnp.bfloat16)
            turn[...] = turn[...].T
            rows = pltpu.roll(turn[pl.ds(pl.multiple_of(own, chan), chan)], shift, 1)
            cols = slice((2 - j) * total, (3 - j) * total)
            back_ref[(2 - i) * chan : (3 - i) * chan, cols] = rows.astype(jnp.bfloat16)


def setup(plan, edge_table, corner_table, weight, chan, counts, col_len, unit):
    edges = jnp.transpose(edge_table, (2, 1, 0))
    corners = jnp.transpose(corner_table, (1, 2, 0))
    total = weight.shape[2]
    vmem = pl.BlockSpec(memory_space=pltpu.VMEM)
    taps = jax.ShapeDtypeStruct((3 * chan, 3 * total), jnp.bfloat16)
    table = jax.ShapeDtypeStruct((12 * (RB // unit) + 8, edges.shape[2]), jnp.int32)
    return pl.pallas_call(
        lambda *refs: setup_kernel(plan, chan, (*counts, col_len, unit), *refs),
        in_specs=[vmem] * 3,
        out_specs=[vmem] * 3,
        out_shape=[table, taps, taps],
        scratch_shapes=[pltpu.VMEM((total, total), jnp.float32)],
        compiler_params=pltpu.CompilerParams(vmem_limit_bytes=VMEM_LIMIT),
        name="setup",
    )(edges, corners, weight)


def from_others(array, ch_count):
    return [array] + [
        lax.ppermute(array, "ch", [((i + k) % ch_count, i) for i in range(ch_count)])
        for k in range(1, ch_count)
    ]


class Place:
    @staticmethod
    def place():
        return (lax.axis_index("px"), lax.axis_index("py"))


class SquareHalo(Place):
    counts = (2, 1, 1, 2)

    def __init__(self, quads):
        self.quads = quads

    def corner_shape(self, chan):
        return (16, chan // 2, LANES)

    def pack_corners(self, corners):
        half = corners.shape[0] // 2
        return corners[:half] + pltpu.roll(corners[half:], LANES // 2, 1)

    def unpack_corners(self, packed):
        upper = packed.astype(jnp.float32)
        both = jnp.concatenate([upper, pltpu.roll(upper, LANES // 2, 1)], axis=0)
        return both.astype(jnp.bfloat16)

    def roles(self):
        row_pos, col_pos = self.place()
        px_end = (row_pos == 0) | (row_pos == 3)
        py_end = (col_pos == 0) | (col_pos == 3)
        side = jnp.where(
            py_end, jnp.where(col_pos == 0, 0, 1), jnp.where(row_pos == 0, 2, 3)
        )
        corner = px_end & py_end
        middle = (px_end | py_end) & jnp.logical_not(corner)
        return (px_end, corner, middle, side, jnp.where(px_end, col_pos, row_pos))

    def chosen_sides(self):
        row_pos, col_pos = self.place()
        px_end, corner, middle, side, seg = self.roles()
        row_line = jnp.where(col_pos == 0, 0, 1)
        col_line = jnp.where(row_pos == 0, 2, 3)
        to_px, to_py = (jnp.where(row_pos == 1, 3, 2), jnp.where(col_pos == 1, 1, 0))
        facing = jnp.where(px_end, to_py, to_px)
        return [
            jnp.where(seg == 1, side, facing),
            jnp.where(seg == 1, facing, side),
            jnp.where(row_pos % 2 == 0, 3, 2),
            jnp.where(col_pos % 2 == 0, 1, 0),
            jnp.where(corner, row_line, jnp.where(middle, side, to_py)),
            jnp.where(corner, col_line, side),
        ]

    def exchange(self, pair, col_side, row_side, lines, corner):
        every = [(x, y) for x in range(4) for y in range(4)]
        axes = ("px", "py")
        swap = lambda array, pairs: lax.ppermute(
            array, axes, [(a[0] * 4 + a[1], b[0] * 4 + b[1]) for a, b in pairs]
        )
        ends = (0, 3)
        corners = [(x, y) for x in ends for y in ends]
        spot = lambda side, seg: ((seg, 0), (seg, 3), (0, seg), (3, seg))[side]
        beside = [(spot(side, k), spot(side, 3 - k)) for side in range(4) for k in (1, 2)]
        beside += [((x, y), (3 - x, y)) for x in (1, 2) for y in (1, 2)]
        paired = swap(pair, beside)
        near_col = swap(col_side, [((x, y), (x ^ 1, y)) for x, y in every])
        near_row = swap(row_side, [((x, y), (x, y ^ 1)) for x, y in every])
        _, _, middle, _, seg = self.roles()
        slot = lax.broadcasted_iota(jnp.int32, (2 * self.quads, 1, 1), 0) // self.quads
        lines = jnp.where(middle & (slot != seg - 1), paired, lines)
        across = []
        for j in (1, 2, 3):
            pairs = [(spot(side, k), spot(side ^ j, k)) for side in range(4) for k in (1, 2)]
            pairs += [(corners[c], corners[c ^ j]) for c in range(4)]
            if j == 1:
                pairs += [((x, y), (x, 3 - y)) for x in (1, 2) for y in (1, 2)]
            across.append(swap(lines, pairs))
        corner, across[0] = lax.optimization_barrier((corner, across[0]))
        ends_of = lax.all_to_all(corner, axes, 0, 0, tiled=True)
        return [lines, *across, paired, near_col, near_row, ends_of]

    def strip_cell(self, g, s, at):
        row_pos, col_pos = self.place()
        _, corner, _, side, _ = self.roles()
        slot = 2 * self.quads
        k = at // RB
        me = jnp.where(row_pos > 0, 2, 0) + jnp.where(col_pos > 0, 1, 0)
        far = jnp.where(k > 0, 1, 0)
        owner = jnp.where(s < 2, 2 * far + s, 2 * (s - 2) + far)
        at_corner = (me ^ owner) * slot + (s // 2) * self.quads
        at_middle = (side ^ s) * slot + (k - 1) * self.quads
        return (jnp.where(corner, at_corner, at_middle) + g // GROUP, (g % GROUP) * 32)

    def near_cell(self, edge, face):
        row_pos, col_pos = self.place()
        px_end, _, _, _, seg = self.roles()
        slot = 2 * self.quads
        paired = 4 * slot + (seg - 1) * self.quads
        near_col, near_row = (5 * slot, 5 * slot + self.quads)
        by_col = jnp.where(row_pos % 2 == 3 - edge, near_col, paired)
        by_row = jnp.where(col_pos % 2 == 1 - edge, near_row, jnp.where(px_end, paired, slot))
        return jnp.where(edge < 2, by_row, by_col) + face // GROUP

    def corner_cell(self, g, s, at):
        seg, hi = (at // RB, jnp.where(at % RB == 0, 0, 1))
        owner = jnp.where(s < 2, seg * 4 + 3 * s, 12 * (s - 2) + seg)
        q = jnp.where(s < 2, 2 * s + hi, s - 2 + 2 * hi)
        return (12 * self.quads + owner, g * 4 + q)

    def diagonal_cell(self, face, q, px, py):
        return (12 * self.quads + px * 4 + py, face * 4 + q)


class GatheredHalo(Place):
    counts = (1, 1, 1, 1, 2)

    def corner_shape(self, chan):
        return (1, chan, LANES)

    def pack_corners(self, corners):
        return corners

    def unpack_corners(self, packed):
        return packed

    def __init__(self, quads, px_count, py_count, col_len):
        self.quads = quads
        self.size = (px_count, py_count)
        self.col_len = col_len

    def chosen_sides(self):
        row_pos, col_pos = self.place()
        return [0, 1, 2, 3, jnp.where(col_pos == 0, 0, 1), jnp.where(row_pos == 0, 2, 3)]

    def exchange(self, top, bottom, left, right, lines, corner):
        px_count, py_count = self.size
        up = lambda n: [(i, i + 1) for i in range(n - 1)]
        down = lambda n: [(i + 1, i) for i in range(n - 1)]
        return [
            lax.ppermute(bottom, "py", up(py_count)),
            lax.ppermute(top, "py", down(py_count)),
            lax.ppermute(right, "px", up(px_count)),
            lax.ppermute(left, "px", down(px_count)),
            lax.all_gather(lines, ("px", "py"), axis=0, tiled=True),
            lax.all_gather(corner, ("px", "py"), axis=0, tiled=True),
        ]

    def strip_cell(self, g, s, at):
        px_count, py_count = self.size
        length = jnp.where(s < 2, RB, self.col_len)
        seg = at // length
        px = jnp.where(s < 2, seg, (s - 2) * (px_count - 1))
        py = jnp.where(s < 2, s * (py_count - 1), seg)
        tile = (4 + (px * py_count + py) * 2 + s // 2) * self.quads + g // GROUP
        return (tile, (g % GROUP) * 32 + at % length)

    def near_cell(self, edge, face):
        return edge * self.quads + face // GROUP

    def corner_cell(self, g, s, at):
        return self.strip_cell(g, s, at)

    def diagonal_cell(self, face, q, px, py):
        px_count, py_count = self.size
        base = (4 + 2 * px_count * py_count) * self.quads
        return (base + px * py_count + py, face * 4 + q)


def local(features, cotangent, weight, edge_table, corner_table):
    chan, faces = features.shape[:2]
    tile = features.shape[4]
    col_len = tile // RB
    unit = min(RB, col_len)
    units = (RB // unit, RB // unit, col_len // unit, col_len // unit)
    px_count, py_count, ch_count = [lax.axis_size(name) for name in ("px", "py", "ch")]
    ring = jnp.asarray(ring_matrix(col_len), jnp.bfloat16)
    cornsel = jnp.asarray(corner_matrix(), jnp.bfloat16)
    spread = jnp.asarray(spread_matrix(col_len), jnp.bfloat16)
    rev = jnp.asarray(reverse_matrix(unit), jnp.bfloat16)
    if px_count == py_count == 4 and col_len == RB and chan % 32 == 0:
        plan = SquareHalo(faces // GROUP)
    else:
        plan = GatheredHalo(faces // GROUP, px_count, py_count, col_len)

    feats = jnp.transpose(features.reshape(chan, faces, tile), (1, 0, 2))
    cot = jnp.transpose(cotangent.reshape(chan, faces, tile), (1, 0, 2))
    fields = from_others(feats, ch_count)
    parts = rings_of(feats, plan, ring, cornsel)
    table, taps, back_taps = setup(
        plan, edge_table, corner_table, weight, chan, (px_count, py_count), col_len, unit
    )
    tiles = plan.exchange(*parts)
    halo = assemble_halo(plan, table, tiles, rev, faces, units, unit)
    halos = from_others(halo, ch_count)
    old, chunks, first = ([], [], 0)
    for count in CALLS:
        act, gated, *parts = forward(
            first, count, plan, fields, halos, cot, taps, spread, ring, cornsel, old
        )
        old = [*parts, act]
        chunks.append((first, from_others(gated, ch_count)))
        first += count

    tiles = plan.exchange(*parts)
    halo = assemble_halo(plan, table, tiles, rev, faces, units, unit)
    halos = from_others(halo, ch_count)
    grad = None
    for first, fields in chunks:
        grad = backward(first, faces, fields, halos, back_taps, spread, grad)

    shape = (chan, faces, 1, 1, tile)
    return (
        jnp.transpose(act, (1, 0, 2)).reshape(shape),
        jnp.transpose(grad, (1, 0, 2)).reshape(shape),
    )


def solution(mesh):
    spec = P("ch", None, "py", "px", None)
    return jax.shard_map(
        local,
        mesh=mesh,
        in_specs=(spec, spec, P(), P(), P()),
        out_specs=(spec, spec),
        check_vma=False,
    )
```

```python
import jax
import jax.numpy as jnp
import numpy as np
from jax import lax
from jax.experimental import pallas as pl
from jax.experimental.pallas import tpu as pltpu
from jax.sharding import PartitionSpec as P

RB = 32
GROUP = 4
LANES = 128
CALLS = (3,)
VMEM_LIMIT = 60 * 1024 * 1024
STRIP_LANE = (96, 0, 32, 64)


def ring_matrix(col_len):
    mat = np.zeros((col_len * RB, LANES), np.float32)
    for b in range(RB):
        mat[b, b] = 1
        mat[(col_len - 1) * RB + b, 32 + b] = 1
    for a in range(col_len):
        mat[a * RB, 64 + a] = 1
        mat[a * RB + RB - 1, 96 + a] = 1
    return mat


def corner_matrix():
    mat = np.zeros((LANES, LANES), np.float32)
    for q, lane in enumerate((0, RB - 1, 32, 32 + RB - 1)):
        mat[lane, q] = 1
    return mat


def reverse_matrix(unit):
    mat = np.zeros((LANES, LANES), np.float32)
    for lane in range(LANES):
        mat[lane, (lane // unit) * unit + unit - 1 - lane % unit] = 1
    return mat


def spread_matrix(col_len):
    width = col_len * RB + LANES
    mat = np.zeros((LANES, width), np.float32)
    top, bottom = (col_len + 3) * RB, col_len * RB
    mat[0, top] = 1
    mat[1, top + RB - 1] = 1
    mat[2, bottom] = 1
    mat[3, bottom + RB - 1] = 1
    for a in range(col_len):
        mat[STRIP_LANE[2] + a, a * RB] = 1
        mat[STRIP_LANE[3] + a, a * RB + RB - 1] = 1
    return mat


def lane_iota(shape):
    return lax.broadcasted_iota(jnp.int32, shape, len(shape) - 1)


def side_tiles(fields, first_face, ring_ref, cornsel_ref):
    chan = fields.shape[0] // GROUP
    lane = lane_iota((chan, LANES))
    flat = jnp.dot(fields, ring_ref[...], preferred_element_type=jnp.float32)
    picked = jnp.dot(
        flat.astype(jnp.bfloat16), cornsel_ref[...], preferred_element_type=jnp.float32
    )
    rings = [flat[g * chan : (g + 1) * chan] for g in range(GROUP)]
    tiles = []
    for side in range(4):
        tile = jnp.zeros((chan, LANES), jnp.float32)
        for g, ring in enumerate(rings):
            moved = pltpu.roll(ring, ((g - side) * 32) % LANES, 1) if g != side else ring
            tile = jnp.where(lane // 32 == g, moved, tile)
        tiles.append(tile.astype(jnp.bfloat16))
    corners = jnp.zeros((chan, LANES), jnp.float32)
    for g in range(GROUP):
        corners += pltpu.roll(picked[g * chan : (g + 1) * chan], (first_face + g) * 4, 1)
    return (tiles, corners)


def hand_out(plan, steps, packs, corners, outs):
    chosen = iter(plan.chosen_sides())
    for out in outs[:-1]:
        for at in range(0, out.shape[0], steps):
            base = next(chosen) * steps
            for q in range(steps):
                out[at + q] = packs[base + q]
    packed = plan.pack_corners(corners).astype(jnp.bfloat16)
    for copy in range(outs[-1].shape[0]):
        outs[-1][copy] = packed


def ring_outs(faces, chan, plan):
    steps = faces // GROUP
    shapes = [(count * steps, chan, LANES) for count in plan.counts] + [plan.corner_shape(chan)]
    return [jax.ShapeDtypeStruct(shape, jnp.bfloat16) for shape in shapes]


def rings_kernel(steps, plan, field_ref, ring_ref, cornsel_ref, *refs):
    outs, (packs, corner_acc) = (refs[:-2], refs[-2:])
    step = pl.program_id(0)
    fields = field_ref[...].reshape(-1, field_ref.shape[2])
    tiles, corners = side_tiles(fields, step * GROUP, ring_ref, cornsel_ref)
    for side, tile in enumerate(tiles):
        packs[side * steps + step] = tile

    @pl.when(step == 0)
    def _():
        corner_acc[...] = jnp.zeros_like(corner_acc)

    corner_acc[...] += corners

    @pl.when(step == steps - 1)
    def _():
        hand_out(plan, steps, packs, corner_acc[...], outs)


def whole_spec(array):
    zeros = (0,) * array.ndim
    return pl.BlockSpec(array.shape, lambda *_: zeros)


def rings_of(field, plan, ring, cornsel):
    faces, chan, tile = field.shape
    steps = faces // GROUP
    outs = ring_outs(faces, chan, plan)
    return pl.pallas_call(
        lambda *refs: rings_kernel(steps, plan, *refs),
        grid=(steps,),
        in_specs=[
            pl.BlockSpec((GROUP, chan, tile), lambda i: (i, 0, 0)),
            whole_spec(ring),
            whole_spec(cornsel),
        ],
        out_specs=[whole_spec(out) for out in outs],
        out_shape=outs,
        scratch_shapes=[
            pltpu.VMEM((4 * steps, chan, LANES), jnp.bfloat16),
            pltpu.VMEM((chan, LANES), jnp.float32),
        ],
        compiler_params=pltpu.CompilerParams(vmem_limit_bytes=VMEM_LIMIT),
        name="rings",
    )(field, ring, cornsel)


def halo_kernel(faces, units, unit, plan, *refs):
    table, tile_refs, (rev_ref, halo_ref, pool, turn_acc) = (refs[0], refs[1:-4], refs[-4:])
    chan = halo_ref.shape[1]
    lane = lane_iota((chan, LANES))
    at = 0
    for ref in tile_refs[:-1]:
        pool[at : at + ref.shape[0]] = ref[...]
        at += ref.shape[0]
    for k in range(tile_refs[-1].shape[0]):
        pool[at + k] = plan.unpack_corners(tile_refs[-1][k])
    corner_tile = jnp.zeros((chan, LANES), jnp.float32)
    most = max(units)
    rows = 4 * most
    for f in range(faces):
        tile = jnp.zeros((chan, LANES), jnp.float32)
        turned = jnp.zeros((chan, LANES), jnp.float32)
        for e in range(4):
            for un in range(units[e]):
                base = STRIP_LANE[e] + un * unit
                span = (lane >= base) & (lane < base + unit)
                entry = e * most + un
                source = pool[table[entry, f]].astype(jnp.float32)
                moved = pltpu.roll(source, table[rows + entry, f], 1)
                flip = table[2 * rows + entry, f] == 1
                tile = jnp.where(span & jnp.logical_not(flip), moved, tile)
                turned = jnp.where(span & flip, moved, turned)
        halo_ref[f] = tile.astype(jnp.bfloat16)
        turn_acc[f] = turned.astype(jnp.bfloat16)
        for c in range(4):
            source = pool[table[3 * rows + c, f]].astype(jnp.float32)
            moved = pltpu.roll(source, table[3 * rows + 4 + c, f], 1)
            corner_tile = jnp.where(lane == f * 4 + c, moved, corner_tile)
    turned = jnp.dot(
        turn_acc[...].reshape(faces * chan, LANES), rev_ref[...], preferred_element_type=jnp.float32
    ).reshape(faces, chan, LANES)
    for f in range(faces):
        halo_ref[f] += turned[f].astype(jnp.bfloat16)
    halo_ref[faces] = corner_tile.astype(jnp.bfloat16)


def assemble_halo(plan, table, tiles, rev, faces, units, unit):
    chan = tiles[0].shape[1]
    halo = jax.ShapeDtypeStruct((faces + 1, chan, LANES), jnp.bfloat16)
    vmem = pl.BlockSpec(memory_space=pltpu.VMEM)
    smem = pl.BlockSpec(memory_space=pltpu.SMEM)
    return pl.pallas_call(
        lambda *refs: halo_kernel(faces, units, unit, plan, *refs),
        in_specs=[smem] + [vmem] * (len(tiles) + 1),
        out_specs=vmem,
        out_shape=halo,
        scratch_shapes=[
            pltpu.VMEM((sum(t.shape[0] for t in tiles), chan, LANES), jnp.bfloat16),
            pltpu.VMEM((faces, chan, LANES), jnp.bfloat16),
        ],
        compiler_params=pltpu.CompilerParams(vmem_limit_bytes=VMEM_LIMIT),
        name="halo",
    )(table, *tiles, rev)


def sides_of(step, halo_refs, corner_refs, spread_ref, beside_ref):
    corners = jnp.concatenate([ref[0].astype(jnp.float32) for ref in corner_refs], axis=0)
    lane = lane_iota(corners.shape)
    sides = []
    for g in range(GROUP):
        halo = jnp.concatenate([ref[g].astype(jnp.float32) for ref in halo_refs], axis=0)
        moved = pltpu.roll(corners, (LANES - (step * GROUP + g) * 4) % LANES, 1)
        sides.append(jnp.where(lane < 4, moved, halo).astype(jnp.bfloat16))
    beside = jnp.dot(
        jnp.concatenate(sides, axis=0), spread_ref[...], preferred_element_type=jnp.float32
    )
    beside_ref[...] = beside.astype(jnp.bfloat16).reshape(beside_ref.shape)


def conv_face(g, field_refs, halo_refs, taps_ref, beside_ref, stack_ref):
    chan, tile = field_refs[0].shape[1:]
    total = chan * len(field_refs)
    width = tile + LANES
    for k, (field, halo) in enumerate(zip(field_refs, halo_refs)):
        stack_ref[total + k * chan : total + (k + 1) * chan, :tile] = field[g]
        stack_ref[total + k * chan : total + (k + 1) * chan, tile:] = halo[g]
    middle = stack_ref[total : 2 * total]
    beside = beside_ref[g]
    col = lane_iota((total, width)) % RB
    stack_ref[:total] = jnp.where(col == 0, beside, pltpu.roll(middle, 1, 1))
    stack_ref[2 * total :] = jnp.where(col == RB - 1, beside, pltpu.roll(middle, width - 1, 1))
    sums = jnp.dot(taps_ref[...], stack_ref[...], preferred_element_type=jnp.float32)
    above = pltpu.roll(sums[:chan], RB, 1)
    below = pltpu.roll(sums[2 * chan :], width - RB, 1)
    return (above + sums[chan : 2 * chan] + below)[:, :tile]


def split_refs(refs, *counts):
    out = []
    for count in counts:
        out.append(refs[:count])
        refs = refs[count:]
    return (*out, refs)


def forward_kernel(first, count, steps, pieces, plan, *refs):
    olds = 3 if first else 0
    fields, halos, corners, consts, old, refs = split_refs(refs, pieces, pieces, pieces, 5, olds)
    cot_ref, taps_ref, spread_ref, ring_ref, cornsel_ref = consts
    outs, (packs, corner_acc, made, beside_ref, stacks) = (refs[:-5], refs[-5:])
    act_ref, gated_ref = outs[:2]
    here = pl.program_id(0)
    step = first + here

    @pl.when(here == 0)
    def _():
        if first:
            packs[...] = old[0][...]
            corner_acc[...] = old[1][0].astype(jnp.float32)
        else:
            corner_acc[...] = jnp.zeros_like(corner_acc)

    sides_of(step, halos, corners, spread_ref, beside_ref)
    chan = act_ref.shape[1]
    for g in range(GROUP):
        pre = conv_face(g, fields, halos, taps_ref, beside_ref, stacks.at[g % 2])
        sig = 1.0 / (1.0 + jnp.exp(-pre))
        act_ref[g] = (pre * sig).astype(jnp.bfloat16)
        gated = cot_ref[g].astype(jnp.float32) * sig * (1.0 + pre * (1.0 - sig))
        gated_ref[g] = gated.astype(jnp.bfloat16)
        made[g * chan : (g + 1) * chan] = gated.astype(jnp.bfloat16)
    tiles, corner = side_tiles(made[...], step * GROUP, ring_ref, cornsel_ref)
    for side, tile in enumerate(tiles):
        packs[side * steps + step] = tile
    corner_acc[...] += corner

    @pl.when(here == count - 1)
    def _():
        if first + count == steps:
            hand_out(plan, steps, packs, corner_acc[...], outs[2:])
        else:
            outs[2][...] = packs[...]
            outs[3][0] = corner_acc[...].astype(jnp.bfloat16)


def conv_specs(fields, halos, first, field_first):
    _, chan, tile = fields[0].shape
    last = halos[0].shape[0] - 1
    return (
        [pl.BlockSpec((GROUP, chan, tile), lambda i: (field_first + i, 0, 0)) for _ in fields]
        + [pl.BlockSpec((GROUP, chan, LANES), lambda i: (first + i, 0, 0)) for _ in halos]
        + [pl.BlockSpec((1, chan, LANES), lambda i: (last, 0, 0)) for _ in halos]
    )


def conv_scratch(chan, pieces, tile):
    total = chan * pieces
    return [
        pltpu.VMEM((GROUP, total, tile + LANES), jnp.bfloat16),
        pltpu.VMEM((2, 3 * total, tile + LANES), jnp.bfloat16),
    ]


def forward(first, count, plan, fields, halos, cot, taps, spread, ring, cornsel, old):
    faces, chan, tile = fields[0].shape
    steps = faces // GROUP
    pieces = len(fields)
    if first + count < steps:
        outs = [
            jax.ShapeDtypeStruct((4 * steps, chan, LANES), jnp.bfloat16),
            jax.ShapeDtypeStruct((1, chan, LANES), jnp.bfloat16),
        ]
    else:
        outs = ring_outs(faces, chan, plan)
    whole = jax.ShapeDtypeStruct((faces, chan, tile), jnp.bfloat16)
    chunk = jax.ShapeDtypeStruct((count * GROUP, chan, tile), jnp.bfloat16)
    block = pl.BlockSpec((GROUP, chan, tile), lambda i: (first + i, 0, 0))
    args = [*fields, *halos, *halos, cot, taps, spread, ring, cornsel, *old]
    return pl.pallas_call(
        lambda *refs: forward_kernel(first, count, steps, pieces, plan, *refs),
        grid=(count,),
        in_specs=conv_specs(fields, halos, first, first)
        + [block, whole_spec(taps), whole_spec(spread), whole_spec(ring), whole_spec(cornsel)]
        + [whole_spec(array) for array in old[:2]]
        + [pl.BlockSpec(memory_space=pl.ANY) for _ in old[2:]],
        out_specs=[block, pl.BlockSpec((GROUP, chan, tile), lambda i: (i, 0, 0))]
        + [whole_spec(o) for o in outs],
        out_shape=[whole, chunk] + outs,
        input_output_aliases={len(args) - 1: 0} if old else {},
        scratch_shapes=[
            pltpu.VMEM((4 * steps, chan, LANES), jnp.bfloat16),
            pltpu.VMEM((chan, LANES), jnp.float32),
            pltpu.VMEM((GROUP * chan, tile), jnp.bfloat16),
        ]
        + conv_scratch(chan, pieces, tile),
        compiler_params=pltpu.CompilerParams(vmem_limit_bytes=VMEM_LIMIT),
        name="forward",
    )(*args)


def backward_kernel(first, pieces, *refs):
    fields, halos, corners, consts, refs = split_refs(refs, pieces, pieces, pieces, 2)
    taps_ref, spread_ref = consts
    grad_ref, beside_ref, stacks = refs[-3:]
    sides_of(first + pl.program_id(0), halos, corners, spread_ref, beside_ref)
    for g in range(GROUP):
        total = conv_face(g, fields, halos, taps_ref, beside_ref, stacks.at[g % 2])
        grad_ref[g] = total.astype(jnp.bfloat16)


def backward(first, faces, fields, halos, taps, spread, grad):
    held, chan, tile = fields[0].shape
    pieces = len(fields)
    aside = [] if grad is None else [grad]
    args = [*fields, *halos, *halos, taps, spread, *aside]
    return pl.pallas_call(
        lambda *refs: backward_kernel(first, pieces, *refs),
        grid=(held // GROUP,),
        in_specs=conv_specs(fields, halos, first, 0)
        + [whole_spec(taps), whole_spec(spread)]
        + [pl.BlockSpec(memory_space=pl.ANY) for _ in aside],
        out_specs=pl.BlockSpec((GROUP, chan, tile), lambda i: (first + i, 0, 0)),
        out_shape=jax.ShapeDtypeStruct((faces, chan, tile), jnp.bfloat16),
        input_output_aliases={len(args) - 1: 0} if aside else {},
        scratch_shapes=conv_scratch(chan, pieces, tile),
        compiler_params=pltpu.CompilerParams(vmem_limit_bytes=VMEM_LIMIT),
        name="backward",
    )(*args)


def rows_of(*parts):
    return jnp.concatenate(parts, axis=0)


def halo_table(plan, edge_ref, corner_ref, px_count, py_count, col_len, unit):
    row_pos, col_pos = plan.place()
    faces = edge_ref.shape[2]
    side_len = px_count * RB
    most = RB // unit
    shape = (4 * most, faces)
    face = lane_iota(shape)
    row = lax.broadcasted_iota(jnp.int32, shape, 0)
    edge, un = (row // most, row % most)
    g, s, r = [
        rows_of(*[edge_ref[i, e : e + 1] for e in range(4) for _ in range(most)]) for i in range(3)
    ]
    border = ((edge == 0) & (col_pos == 0)) | ((edge == 1) & (col_pos == py_count - 1))
    border |= ((edge == 2) & (row_pos == 0)) | ((edge == 3) & (row_pos == px_count - 1))
    at = jnp.where(edge < 2, row_pos * RB, col_pos * col_len) + un * unit
    at = jnp.clip(at, 0, side_len - unit)
    at = jnp.where(r == 1, side_len - unit - at, at)
    line_tile, line_lane = plan.strip_cell(g, s, at)
    tile = jnp.where(border, line_tile, plan.near_cell(edge, face))
    lane = jnp.where(border, line_lane, (face % GROUP) * 32 + un * unit)
    first = jnp.where(edge == 0, STRIP_LANE[0], jnp.where(edge == 1, STRIP_LANE[1], edge * 32 - 32))
    shift = (first + un * unit - lane + LANES) % LANES
    flip = jnp.where(border & (r == 1), 1, 0)

    shape = (4, faces)
    face = lane_iota(shape)
    c = lax.broadcasted_iota(jnp.int32, shape, 0)
    down, right = (c // 2, c % 2)
    row_on = ((down == 0) & (col_pos == 0)) | ((down == 1) & (col_pos == py_count - 1))
    col_on = ((right == 0) & (row_pos == 0)) | ((right == 1) & (row_pos == px_count - 1))
    row_at = row_pos * RB + jnp.where(right == 1, RB, -1)
    col_at = col_pos * col_len + jnp.where(down == 1, col_len, -1)
    edge_of = lambda i, edges: rows_of(*[edge_ref[i, e : e + 1] for e in edges])
    g, s, r = [
        jnp.where(row_on, edge_of(i, (0, 0, 1, 1)), edge_of(i, (2, 3, 2, 3))) for i in range(3)
    ]
    at = jnp.clip(jnp.where(row_on, row_at, col_at), 0, side_len - 1)
    at = jnp.where(r == 1, side_len - 1 - at, at)
    h, q = [rows_of(*[corner_ref[k, i : i + 1] for k in range(4)]) for i in range(2)]
    both = row_on & col_on
    g = jnp.where(both, h, g)
    s = jnp.where(both, q // 2, s)
    at = jnp.where(both, (q % 2) * (side_len - 1), at)
    line_tile, line_lane = plan.corner_cell(g, s, at)
    diag_px = jnp.clip(row_pos + 2 * right - 1, 0, px_count - 1)
    diag_py = jnp.clip(col_pos + 2 * down - 1, 0, py_count - 1)
    diag_tile, diag_lane = plan.diagonal_cell(face, 3 - c, diag_px, diag_py)
    on = row_on | col_on
    corner_at = jnp.where(on, line_tile, diag_tile)
    corner_lane = jnp.where(on, line_lane, diag_lane)
    corner_shift = (face * 4 + c - corner_lane + LANES) % LANES
    return rows_of(tile, shift, flip, corner_at, corner_shift)


def setup_kernel(plan, chan, shape, edge_ref, corner_ref, weight_ref, table_ref, taps_ref, back_ref, turn):
    table_ref[...] = halo_table(plan, edge_ref, corner_ref, *shape)
    total = weight_ref.shape[2]
    own = lax.axis_index("ch") * chan
    shift = (total - own) % total
    for i in range(3):
        for j in range(3):
            turn[...] = weight_ref[i, j].astype(jnp.float32)
            rows = pltpu.roll(turn[pl.ds(pl.multiple_of(own, chan), chan)], shift, 1)
            cols = slice(j * total, (j + 1) * total)
            taps_ref[i * chan : (i + 1) * chan, cols] = rows.astype(jnp.bfloat16)
            turn[...] = turn[...].T
            rows = pltpu.roll(turn[pl.ds(pl.multiple_of(own, chan), chan)], shift, 1)
            cols = slice((2 - j) * total, (3 - j) * total)
            back_ref[(2 - i) * chan : (3 - i) * chan, cols] = rows.astype(jnp.bfloat16)


def setup(plan, edge_table, corner_table, weight, chan, counts, col_len, unit):
    edges = jnp.transpose(edge_table, (2, 1, 0))
    corners = jnp.transpose(corner_table, (1, 2, 0))
    total = weight.shape[2]
    vmem = pl.BlockSpec(memory_space=pltpu.VMEM)
    taps = jax.ShapeDtypeStruct((3 * chan, 3 * total), jnp.bfloat16)
    table = jax.ShapeDtypeStruct((12 * (RB // unit) + 8, edges.shape[2]), jnp.int32)
    return pl.pallas_call(
        lambda *refs: setup_kernel(plan, chan, (*counts, col_len, unit), *refs),
        in_specs=[vmem] * 3,
        out_specs=[vmem] * 3,
        out_shape=[table, taps, taps],
        scratch_shapes=[pltpu.VMEM((total, total), jnp.float32)],
        compiler_params=pltpu.CompilerParams(vmem_limit_bytes=VMEM_LIMIT),
        name="setup",
    )(edges, corners, weight)


def from_others(array, ch_count):
    return [array] + [
        lax.ppermute(array, "ch", [((i + k) % ch_count, i) for i in range(ch_count)])
        for k in range(1, ch_count)
    ]


class Place:
    @staticmethod
    def place():
        return (lax.axis_index("px"), lax.axis_index("py"))


class SquareHalo(Place):
    counts = (2, 1, 1, 2)

    def __init__(self, quads):
        self.quads = quads

    def corner_shape(self, chan):
        return (16, chan // 2, LANES)

    def pack_corners(self, corners):
        half = corners.shape[0] // 2
        return corners[:half] + pltpu.roll(corners[half:], LANES // 2, 1)

    def unpack_corners(self, packed):
        upper = packed.astype(jnp.float32)
        both = jnp.concatenate([upper, pltpu.roll(upper, LANES // 2, 1)], axis=0)
        return both.astype(jnp.bfloat16)

    def roles(self):
        row_pos, col_pos = self.place()
        px_end = (row_pos == 0) | (row_pos == 3)
        py_end = (col_pos == 0) | (col_pos == 3)
        side = jnp.where(
            py_end, jnp.where(col_pos == 0, 0, 1), jnp.where(row_pos == 0, 2, 3)
        )
        corner = px_end & py_end
        middle = (px_end | py_end) & jnp.logical_not(corner)
        return (px_end, corner, middle, side, jnp.where(px_end, col_pos, row_pos))

    def chosen_sides(self):
        row_pos, col_pos = self.place()
        px_end, corner, middle, side, seg = self.roles()
        row_line = jnp.where(col_pos == 0, 0, 1)
        col_line = jnp.where(row_pos == 0, 2, 3)
        to_px, to_py = (jnp.where(row_pos == 1, 3, 2), jnp.where(col_pos == 1, 1, 0))
        facing = jnp.where(px_end, to_py, to_px)
        return [
            jnp.where(seg == 1, side, facing),
            jnp.where(seg == 1, facing, side),
            jnp.where(row_pos % 2 == 0, 3, 2),
            jnp.where(col_pos % 2 == 0, 1, 0),
            jnp.where(corner, row_line, jnp.where(middle, side, to_py)),
            jnp.where(corner, col_line, side),
        ]

    def exchange(self, pair, col_side, row_side, lines, corner):
        every = [(x, y) for x in range(4) for y in range(4)]
        axes = ("px", "py")
        swap = lambda array, pairs: lax.ppermute(
            array, axes, [(a[0] * 4 + a[1], b[0] * 4 + b[1]) for a, b in pairs]
        )
        ends = (0, 3)
        corners = [(x, y) for x in ends for y in ends]
        spot = lambda side, seg: ((seg, 0), (seg, 3), (0, seg), (3, seg))[side]
        beside = [(spot(side, k), spot(side, 3 - k)) for side in range(4) for k in (1, 2)]
        beside += [((x, y), (3 - x, y)) for x in (1, 2) for y in (1, 2)]
        paired = swap(pair, beside)
        near_col = swap(col_side, [((x, y), (x ^ 1, y)) for x, y in every])
        near_row = swap(row_side, [((x, y), (x, y ^ 1)) for x, y in every])
        _, _, middle, _, seg = self.roles()
        slot = lax.broadcasted_iota(jnp.int32, (2 * self.quads, 1, 1), 0) // self.quads
        lines = jnp.where(middle & (slot != seg - 1), paired, lines)
        across = []
        for j in (1, 2, 3):
            pairs = [(spot(side, k), spot(side ^ j, k)) for side in range(4) for k in (1, 2)]
            pairs += [(corners[c], corners[c ^ j]) for c in range(4)]
            if j == 1:
                pairs += [((x, y), (x, 3 - y)) for x in (1, 2) for y in (1, 2)]
            across.append(swap(lines, pairs))
        arrived = [*across, paired, near_col, near_row]
        corner, *arrived = lax.optimization_barrier((corner, *arrived))
        ends_of = lax.all_to_all(corner, axes, 0, 0, tiled=True)
        return [lines, *arrived, ends_of]

    def strip_cell(self, g, s, at):
        row_pos, col_pos = self.place()
        _, corner, _, side, _ = self.roles()
        slot = 2 * self.quads
        k = at // RB
        me = jnp.where(row_pos > 0, 2, 0) + jnp.where(col_pos > 0, 1, 0)
        far = jnp.where(k > 0, 1, 0)
        owner = jnp.where(s < 2, 2 * far + s, 2 * (s - 2) + far)
        at_corner = (me ^ owner) * slot + (s // 2) * self.quads
        at_middle = (side ^ s) * slot + (k - 1) * self.quads
        return (jnp.where(corner, at_corner, at_middle) + g // GROUP, (g % GROUP) * 32)

    def near_cell(self, edge, face):
        row_pos, col_pos = self.place()
        px_end, _, _, _, seg = self.roles()
        slot = 2 * self.quads
        paired = 4 * slot + (seg - 1) * self.quads
        near_col, near_row = (5 * slot, 5 * slot + self.quads)
        by_col = jnp.where(row_pos % 2 == 3 - edge, near_col, paired)
        by_row = jnp.where(col_pos % 2 == 1 - edge, near_row, jnp.where(px_end, paired, slot))
        return jnp.where(edge < 2, by_row, by_col) + face // GROUP

    def corner_cell(self, g, s, at):
        seg, hi = (at // RB, jnp.where(at % RB == 0, 0, 1))
        owner = jnp.where(s < 2, seg * 4 + 3 * s, 12 * (s - 2) + seg)
        q = jnp.where(s < 2, 2 * s + hi, s - 2 + 2 * hi)
        return (12 * self.quads + owner, g * 4 + q)

    def diagonal_cell(self, face, q, px, py):
        return (12 * self.quads + px * 4 + py, face * 4 + q)


class GatheredHalo(Place):
    counts = (1, 1, 1, 1, 2)

    def corner_shape(self, chan):
        return (1, chan, LANES)

    def pack_corners(self, corners):
        return corners

    def unpack_corners(self, packed):
        return packed

    def __init__(self, quads, px_count, py_count, col_len):
        self.quads = quads
        self.size = (px_count, py_count)
        self.col_len = col_len

    def chosen_sides(self):
        row_pos, col_pos = self.place()
        return [0, 1, 2, 3, jnp.where(col_pos == 0, 0, 1), jnp.where(row_pos == 0, 2, 3)]

    def exchange(self, top, bottom, left, right, lines, corner):
        px_count, py_count = self.size
        up = lambda n: [(i, i + 1) for i in range(n - 1)]
        down = lambda n: [(i + 1, i) for i in range(n - 1)]
        return [
            lax.ppermute(bottom, "py", up(py_count)),
            lax.ppermute(top, "py", down(py_count)),
            lax.ppermute(right, "px", up(px_count)),
            lax.ppermute(left, "px", down(px_count)),
            lax.all_gather(lines, ("px", "py"), axis=0, tiled=True),
            lax.all_gather(corner, ("px", "py"), axis=0, tiled=True),
        ]

    def strip_cell(self, g, s, at):
        px_count, py_count = self.size
        length = jnp.where(s < 2, RB, self.col_len)
        seg = at // length
        px = jnp.where(s < 2, seg, (s - 2) * (px_count - 1))
        py = jnp.where(s < 2, s * (py_count - 1), seg)
        tile = (4 + (px * py_count + py) * 2 + s // 2) * self.quads + g // GROUP
        return (tile, (g % GROUP) * 32 + at % length)

    def near_cell(self, edge, face):
        return edge * self.quads + face // GROUP

    def corner_cell(self, g, s, at):
        return self.strip_cell(g, s, at)

    def diagonal_cell(self, face, q, px, py):
        px_count, py_count = self.size
        base = (4 + 2 * px_count * py_count) * self.quads
        return (base + px * py_count + py, face * 4 + q)


def local(features, cotangent, weight, edge_table, corner_table):
    chan, faces = features.shape[:2]
    tile = features.shape[4]
    col_len = tile // RB
    unit = min(RB, col_len)
    units = (RB // unit, RB // unit, col_len // unit, col_len // unit)
    px_count, py_count, ch_count = [lax.axis_size(name) for name in ("px", "py", "ch")]
    ring = jnp.asarray(ring_matrix(col_len), jnp.bfloat16)
    cornsel = jnp.asarray(corner_matrix(), jnp.bfloat16)
    spread = jnp.asarray(spread_matrix(col_len), jnp.bfloat16)
    rev = jnp.asarray(reverse_matrix(unit), jnp.bfloat16)
    if px_count == py_count == 4 and col_len == RB and chan % 32 == 0:
        plan = SquareHalo(faces // GROUP)
    else:
        plan = GatheredHalo(faces // GROUP, px_count, py_count, col_len)

    feats = jnp.transpose(features.reshape(chan, faces, tile), (1, 0, 2))
    cot = jnp.transpose(cotangent.reshape(chan, faces, tile), (1, 0, 2))
    fields = from_others(feats, ch_count)
    parts = rings_of(feats, plan, ring, cornsel)
    table, taps, back_taps = setup(
        plan, edge_table, corner_table, weight, chan, (px_count, py_count), col_len, unit
    )
    tiles = plan.exchange(*parts)
    halo = assemble_halo(plan, table, tiles, rev, faces, units, unit)
    halos = from_others(halo, ch_count)
    old, chunks, first = ([], [], 0)
    for count in CALLS:
        act, gated, *parts = forward(
            first, count, plan, fields, halos, cot, taps, spread, ring, cornsel, old
        )
        old = [*parts, act]
        chunks.append((first, from_others(gated, ch_count)))
        first += count

    tiles = plan.exchange(*parts)
    halo = assemble_halo(plan, table, tiles, rev, faces, units, unit)
    halos = from_others(halo, ch_count)
    grad = None
    for first, fields in chunks:
        grad = backward(first, faces, fields, halos, back_taps, spread, grad)

    shape = (chan, faces, 1, 1, tile)
    return (
        jnp.transpose(act, (1, 0, 2)).reshape(shape),
        jnp.transpose(grad, (1, 0, 2)).reshape(shape),
    )


def solution(mesh):
    spec = P("ch", None, "py", "px", None)
    return jax.shard_map(
        local,
        mesh=mesh,
        in_specs=(spec, spec, P(), P(), P()),
        out_specs=(spec, spec),
        check_vma=False,
    )
```

```python
import jax
import jax.numpy as jnp
import numpy as np
from jax import lax
from jax.experimental import pallas as pl
from jax.experimental.pallas import tpu as pltpu
from jax.sharding import PartitionSpec as P

RB = 32
GROUP = 4
LANES = 128
CALLS = (3,)
VMEM_LIMIT = 60 * 1024 * 1024
STRIP_LANE = (96, 0, 32, 64)
HALF = 48


def ring_matrix(col_len):
    mat = np.zeros((col_len * RB, LANES), np.float32)
    for b in range(RB):
        mat[b, b] = 1
        mat[(col_len - 1) * RB + b, 32 + b] = 1
    for a in range(col_len):
        mat[a * RB, 64 + a] = 1
        mat[a * RB + RB - 1, 96 + a] = 1
    return mat


def corner_matrix():
    mat = np.zeros((LANES, LANES), np.float32)
    for q, lane in enumerate((0, RB - 1, 32, 32 + RB - 1)):
        mat[lane, q] = 1
    return mat


def reverse_matrix(unit):
    mat = np.zeros((LANES, LANES), np.float32)
    for lane in range(LANES):
        mat[lane, (lane // unit) * unit + unit - 1 - lane % unit] = 1
    return mat


def spread_matrix(col_len):
    width = col_len * RB + LANES
    mat = np.zeros((LANES, width), np.float32)
    top, bottom = (col_len + 3) * RB, col_len * RB
    mat[0, top] = 1
    mat[1, top + RB - 1] = 1
    mat[2, bottom] = 1
    mat[3, bottom + RB - 1] = 1
    for a in range(col_len):
        mat[STRIP_LANE[2] + a, a * RB] = 1
        mat[STRIP_LANE[3] + a, a * RB + RB - 1] = 1
    return mat


def lane_iota(shape):
    return lax.broadcasted_iota(jnp.int32, shape, len(shape) - 1)


def side_tiles(fields, first_face, ring_ref, cornsel_ref):
    chan = fields.shape[0] // GROUP
    lane = lane_iota((chan, LANES))
    flat = jnp.dot(fields, ring_ref[...], preferred_element_type=jnp.float32)
    picked = jnp.dot(
        flat.astype(jnp.bfloat16), cornsel_ref[...], preferred_element_type=jnp.float32
    )
    rings = [flat[g * chan : (g + 1) * chan] for g in range(GROUP)]
    tiles = []
    for side in range(4):
        tile = jnp.zeros((chan, LANES), jnp.float32)
        for g, ring in enumerate(rings):
            moved = pltpu.roll(ring, ((g - side) * 32) % LANES, 1) if g != side else ring
            tile = jnp.where(lane // 32 == g, moved, tile)
        tiles.append(tile.astype(jnp.bfloat16))
    corners = jnp.zeros((chan, LANES), jnp.float32)
    for g in range(GROUP):
        corners += pltpu.roll(picked[g * chan : (g + 1) * chan], (first_face + g) * 4, 1)
    return (tiles, corners)


def hand_out(plan, steps, packs, corners, outs):
    chosen = iter(plan.chosen_sides())
    for out, count, extra in zip(outs, plan.counts, plan.extras):
        for at in range(count):
            base = next(chosen) * steps
            for q in range(steps):
                out[at * steps + q] = packs[base + q]
        if extra is not None:
            moved = pltpu.roll(corners, extra, 1) if extra else corners
            out[count * steps] = moved.astype(jnp.bfloat16)
    outs[-1][0] = corners.astype(jnp.bfloat16)


def ring_outs(faces, chan, plan):
    steps = faces // GROUP
    tiles = [n * steps + (extra is not None) for n, extra in zip(plan.counts, plan.extras)]
    return [jax.ShapeDtypeStruct((n, chan, LANES), jnp.bfloat16) for n in (*tiles, 1)]


def rings_kernel(steps, plan, field_ref, ring_ref, cornsel_ref, *refs):
    outs, (packs, corner_acc) = (refs[:-2], refs[-2:])
    step = pl.program_id(0)
    fields = field_ref[...].reshape(-1, field_ref.shape[2])
    tiles, corners = side_tiles(fields, step * GROUP, ring_ref, cornsel_ref)
    for side, tile in enumerate(tiles):
        packs[side * steps + step] = tile

    @pl.when(step == 0)
    def _():
        corner_acc[...] = jnp.zeros_like(corner_acc)

    corner_acc[...] += corners

    @pl.when(step == steps - 1)
    def _():
        hand_out(plan, steps, packs, corner_acc[...], outs)


def whole_spec(array):
    zeros = (0,) * array.ndim
    return pl.BlockSpec(array.shape, lambda *_: zeros)


def rings_of(field, plan, ring, cornsel):
    faces, chan, tile = field.shape
    steps = faces // GROUP
    outs = ring_outs(faces, chan, plan)
    return pl.pallas_call(
        lambda *refs: rings_kernel(steps, plan, *refs),
        grid=(steps,),
        in_specs=[
            pl.BlockSpec((GROUP, chan, tile), lambda i: (i, 0, 0)),
            whole_spec(ring),
            whole_spec(cornsel),
        ],
        out_specs=[whole_spec(out) for out in outs],
        out_shape=outs,
        scratch_shapes=[
            pltpu.VMEM((4 * steps, chan, LANES), jnp.bfloat16),
            pltpu.VMEM((chan, LANES), jnp.float32),
        ],
        compiler_params=pltpu.CompilerParams(vmem_limit_bytes=VMEM_LIMIT),
        name="rings",
    )(field, ring, cornsel)


def halo_kernel(faces, units, unit, *refs):
    table, tile_refs, (rev_ref, halo_ref, pool, turn_acc) = (refs[0], refs[1:-4], refs[-4:])
    chan = halo_ref.shape[1]
    lane = lane_iota((chan, LANES))
    at = 0
    for ref in tile_refs:
        pool[at : at + ref.shape[0]] = ref[...]
        at += ref.shape[0]
    corner_tile = jnp.zeros((chan, LANES), jnp.float32)
    most = max(units)
    rows = 4 * most
    for f in range(faces):
        tile = jnp.zeros((chan, LANES), jnp.float32)
        turned = jnp.zeros((chan, LANES), jnp.float32)
        for e in range(4):
            for un in range(units[e]):
                base = STRIP_LANE[e] + un * unit
                span = (lane >= base) & (lane < base + unit)
                entry = e * most + un
                source = pool[table[entry, f]].astype(jnp.float32)
                moved = pltpu.roll(source, table[rows + entry, f], 1)
                flip = table[2 * rows + entry, f] == 1
                tile = jnp.where(span & jnp.logical_not(flip), moved, tile)
                turned = jnp.where(span & flip, moved, turned)
        halo_ref[f] = tile.astype(jnp.bfloat16)
        turn_acc[f] = turned.astype(jnp.bfloat16)
        for c in range(4):
            source = pool[table[3 * rows + c, f]].astype(jnp.float32)
            moved = pltpu.roll(source, table[3 * rows + 4 + c, f], 1)
            corner_tile = jnp.where(lane == f * 4 + c, moved, corner_tile)
    turned = jnp.dot(
        turn_acc[...].reshape(faces * chan, LANES), rev_ref[...], preferred_element_type=jnp.float32
    ).reshape(faces, chan, LANES)
    for f in range(faces):
        halo_ref[f] += turned[f].astype(jnp.bfloat16)
    halo_ref[faces] = corner_tile.astype(jnp.bfloat16)


def assemble_halo(table, tiles, rev, faces, units, unit):
    chan = tiles[0].shape[1]
    halo = jax.ShapeDtypeStruct((faces + 1, chan, LANES), jnp.bfloat16)
    vmem = pl.BlockSpec(memory_space=pltpu.VMEM)
    smem = pl.BlockSpec(memory_space=pltpu.SMEM)
    return pl.pallas_call(
        lambda *refs: halo_kernel(faces, units, unit, *refs),
        in_specs=[smem] + [vmem] * (len(tiles) + 1),
        out_specs=vmem,
        out_shape=halo,
        scratch_shapes=[
            pltpu.VMEM((sum(t.shape[0] for t in tiles), chan, LANES), jnp.bfloat16),
            pltpu.VMEM((faces, chan, LANES), jnp.bfloat16),
        ],
        compiler_params=pltpu.CompilerParams(vmem_limit_bytes=VMEM_LIMIT),
        name="halo",
    )(table, *tiles, rev)


def sides_of(step, halo_refs, corner_refs, spread_ref, beside_ref):
    corners = jnp.concatenate([ref[0].astype(jnp.float32) for ref in corner_refs], axis=0)
    lane = lane_iota(corners.shape)
    sides = []
    for g in range(GROUP):
        halo = jnp.concatenate([ref[g].astype(jnp.float32) for ref in halo_refs], axis=0)
        moved = pltpu.roll(corners, (LANES - (step * GROUP + g) * 4) % LANES, 1)
        sides.append(jnp.where(lane < 4, moved, halo).astype(jnp.bfloat16))
    beside = jnp.dot(
        jnp.concatenate(sides, axis=0), spread_ref[...], preferred_element_type=jnp.float32
    )
    beside_ref[...] = beside.astype(jnp.bfloat16).reshape(beside_ref.shape)


def conv_face(g, field_refs, halo_refs, taps_ref, beside_ref, stack_ref):
    chan, tile = field_refs[0].shape[1:]
    total = chan * len(field_refs)
    width = tile + LANES
    for k, (field, halo) in enumerate(zip(field_refs, halo_refs)):
        stack_ref[total + k * chan : total + (k + 1) * chan, :tile] = field[g]
        stack_ref[total + k * chan : total + (k + 1) * chan, tile:] = halo[g]
    middle = stack_ref[total : 2 * total]
    beside = beside_ref[g]
    col = lane_iota((total, width)) % RB
    stack_ref[:total] = jnp.where(col == 0, beside, pltpu.roll(middle, 1, 1))
    stack_ref[2 * total :] = jnp.where(col == RB - 1, beside, pltpu.roll(middle, width - 1, 1))
    sums = jnp.dot(taps_ref[...], stack_ref[...], preferred_element_type=jnp.float32)
    above = pltpu.roll(sums[:chan], RB, 1)
    below = pltpu.roll(sums[2 * chan :], width - RB, 1)
    return (above + sums[chan : 2 * chan] + below)[:, :tile]


def split_refs(refs, *counts):
    out = []
    for count in counts:
        out.append(refs[:count])
        refs = refs[count:]
    return (*out, refs)


def forward_kernel(first, count, steps, pieces, plan, *refs):
    olds = 3 if first else 0
    fields, halos, corners, consts, old, refs = split_refs(refs, pieces, pieces, pieces, 5, olds)
    cot_ref, taps_ref, spread_ref, ring_ref, cornsel_ref = consts
    outs, (packs, corner_acc, made, beside_ref, stacks) = (refs[:-5], refs[-5:])
    act_ref, gated_ref = outs[:2]
    here = pl.program_id(0)
    step = first + here

    @pl.when(here == 0)
    def _():
        if first:
            packs[...] = old[0][...]
            corner_acc[...] = old[1][0].astype(jnp.float32)
        else:
            corner_acc[...] = jnp.zeros_like(corner_acc)

    sides_of(step, halos, corners, spread_ref, beside_ref)
    chan = act_ref.shape[1]
    for g in range(GROUP):
        pre = conv_face(g, fields, halos, taps_ref, beside_ref, stacks.at[g % 2])
        sig = 1.0 / (1.0 + jnp.exp(-pre))
        act_ref[g] = (pre * sig).astype(jnp.bfloat16)
        gated = cot_ref[g].astype(jnp.float32) * sig * (1.0 + pre * (1.0 - sig))
        gated_ref[g] = gated.astype(jnp.bfloat16)
        made[g * chan : (g + 1) * chan] = gated.astype(jnp.bfloat16)
    tiles, corner = side_tiles(made[...], step * GROUP, ring_ref, cornsel_ref)
    for side, tile in enumerate(tiles):
        packs[side * steps + step] = tile
    corner_acc[...] += corner

    @pl.when(here == count - 1)
    def _():
        if first + count == steps:
            hand_out(plan, steps, packs, corner_acc[...], outs[2:])
        else:
            outs[2][...] = packs[...]
            outs[3][0] = corner_acc[...].astype(jnp.bfloat16)


def conv_specs(fields, halos, first, field_first):
    _, chan, tile = fields[0].shape
    last = halos[0].shape[0] - 1
    return (
        [pl.BlockSpec((GROUP, chan, tile), lambda i: (field_first + i, 0, 0)) for _ in fields]
        + [pl.BlockSpec((GROUP, chan, LANES), lambda i: (first + i, 0, 0)) for _ in halos]
        + [pl.BlockSpec((1, chan, LANES), lambda i: (last, 0, 0)) for _ in halos]
    )


def conv_scratch(chan, pieces, tile):
    total = chan * pieces
    return [
        pltpu.VMEM((GROUP, total, tile + LANES), jnp.bfloat16),
        pltpu.VMEM((2, 3 * total, tile + LANES), jnp.bfloat16),
    ]


def forward(first, count, plan, fields, halos, cot, taps, spread, ring, cornsel, old):
    faces, chan, tile = fields[0].shape
    steps = faces // GROUP
    pieces = len(fields)
    if first + count < steps:
        outs = [
            jax.ShapeDtypeStruct((4 * steps, chan, LANES), jnp.bfloat16),
            jax.ShapeDtypeStruct((1, chan, LANES), jnp.bfloat16),
        ]
    else:
        outs = ring_outs(faces, chan, plan)
    whole = jax.ShapeDtypeStruct((faces, chan, tile), jnp.bfloat16)
    chunk = jax.ShapeDtypeStruct((count * GROUP, chan, tile), jnp.bfloat16)
    block = pl.BlockSpec((GROUP, chan, tile), lambda i: (first + i, 0, 0))
    args = [*fields, *halos, *halos, cot, taps, spread, ring, cornsel, *old]
    return pl.pallas_call(
        lambda *refs: forward_kernel(first, count, steps, pieces, plan, *refs),
        grid=(count,),
        in_specs=conv_specs(fields, halos, first, first)
        + [block, whole_spec(taps), whole_spec(spread), whole_spec(ring), whole_spec(cornsel)]
        + [whole_spec(array) for array in old[:2]]
        + [pl.BlockSpec(memory_space=pl.ANY) for _ in old[2:]],
        out_specs=[block, pl.BlockSpec((GROUP, chan, tile), lambda i: (i, 0, 0))]
        + [whole_spec(o) for o in outs],
        out_shape=[whole, chunk] + outs,
        input_output_aliases={len(args) - 1: 0} if old else {},
        scratch_shapes=[
            pltpu.VMEM((4 * steps, chan, LANES), jnp.bfloat16),
            pltpu.VMEM((chan, LANES), jnp.float32),
            pltpu.VMEM((GROUP * chan, tile), jnp.bfloat16),
        ]
        + conv_scratch(chan, pieces, tile),
        compiler_params=pltpu.CompilerParams(vmem_limit_bytes=VMEM_LIMIT),
        name="forward",
    )(*args)


def backward_kernel(first, pieces, *refs):
    fields, halos, corners, consts, refs = split_refs(refs, pieces, pieces, pieces, 2)
    taps_ref, spread_ref = consts
    grad_ref, beside_ref, stacks = refs[-3:]
    sides_of(first + pl.program_id(0), halos, corners, spread_ref, beside_ref)
    for g in range(GROUP):
        total = conv_face(g, fields, halos, taps_ref, beside_ref, stacks.at[g % 2])
        grad_ref[g] = total.astype(jnp.bfloat16)


def backward(first, faces, fields, halos, taps, spread, grad):
    held, chan, tile = fields[0].shape
    pieces = len(fields)
    aside = [] if grad is None else [grad]
    args = [*fields, *halos, *halos, taps, spread, *aside]
    return pl.pallas_call(
        lambda *refs: backward_kernel(first, pieces, *refs),
        grid=(held // GROUP,),
        in_specs=conv_specs(fields, halos, first, 0)
        + [whole_spec(taps), whole_spec(spread)]
        + [pl.BlockSpec(memory_space=pl.ANY) for _ in aside],
        out_specs=pl.BlockSpec((GROUP, chan, tile), lambda i: (first + i, 0, 0)),
        out_shape=jax.ShapeDtypeStruct((faces, chan, tile), jnp.bfloat16),
        input_output_aliases={len(args) - 1: 0} if aside else {},
        scratch_shapes=conv_scratch(chan, pieces, tile),
        compiler_params=pltpu.CompilerParams(vmem_limit_bytes=VMEM_LIMIT),
        name="backward",
    )(*args)


def rows_of(*parts):
    return jnp.concatenate(parts, axis=0)


def halo_table(plan, edge_ref, corner_ref, px_count, py_count, col_len, unit):
    row_pos, col_pos = plan.place()
    faces = edge_ref.shape[2]
    side_len = px_count * RB
    most = RB // unit
    shape = (4 * most, faces)
    face = lane_iota(shape)
    row = lax.broadcasted_iota(jnp.int32, shape, 0)
    edge, un = (row // most, row % most)
    g, s, r = [
        rows_of(*[edge_ref[i, e : e + 1] for e in range(4) for _ in range(most)]) for i in range(3)
    ]
    border = ((edge == 0) & (col_pos == 0)) | ((edge == 1) & (col_pos == py_count - 1))
    border |= ((edge == 2) & (row_pos == 0)) | ((edge == 3) & (row_pos == px_count - 1))
    at = jnp.where(edge < 2, row_pos * RB, col_pos * col_len) + un * unit
    at = jnp.clip(at, 0, side_len - unit)
    at = jnp.where(r == 1, side_len - unit - at, at)
    line_tile, line_lane = plan.strip_cell(g, s, at)
    tile = jnp.where(border, line_tile, plan.near_cell(edge, face))
    lane = jnp.where(border, line_lane, (face % GROUP) * 32 + un * unit)
    first = jnp.where(edge == 0, STRIP_LANE[0], jnp.where(edge == 1, STRIP_LANE[1], edge * 32 - 32))
    shift = (first + un * unit - lane + LANES) % LANES
    flip = jnp.where(border & (r == 1), 1, 0)

    shape = (4, faces)
    face = lane_iota(shape)
    c = lax.broadcasted_iota(jnp.int32, shape, 0)
    down, right = (c // 2, c % 2)
    row_on = ((down == 0) & (col_pos == 0)) | ((down == 1) & (col_pos == py_count - 1))
    col_on = ((right == 0) & (row_pos == 0)) | ((right == 1) & (row_pos == px_count - 1))
    row_at = row_pos * RB + jnp.where(right == 1, RB, -1)
    col_at = col_pos * col_len + jnp.where(down == 1, col_len, -1)
    edge_of = lambda i, edges: rows_of(*[edge_ref[i, e : e + 1] for e in edges])
    g, s, r = [
        jnp.where(row_on, edge_of(i, (0, 0, 1, 1)), edge_of(i, (2, 3, 2, 3))) for i in range(3)
    ]
    at = jnp.clip(jnp.where(row_on, row_at, col_at), 0, side_len - 1)
    at = jnp.where(r == 1, side_len - 1 - at, at)
    h, q = [rows_of(*[corner_ref[k, i : i + 1] for k in range(4)]) for i in range(2)]
    both = row_on & col_on
    g = jnp.where(both, h, g)
    s = jnp.where(both, q // 2, s)
    at = jnp.where(both, (q % 2) * (side_len - 1), at)
    line_tile, line_lane = plan.corner_cell(g, s, at)
    diag_px = jnp.clip(row_pos + 2 * right - 1, 0, px_count - 1)
    diag_py = jnp.clip(col_pos + 2 * down - 1, 0, py_count - 1)
    diag_tile, diag_lane = plan.diagonal_cell(face, 3 - c, diag_px, diag_py)
    on = row_on | col_on
    corner_at = jnp.where(on, line_tile, diag_tile)
    corner_lane = jnp.where(on, line_lane, diag_lane)
    corner_shift = (face * 4 + c - corner_lane + LANES) % LANES
    return rows_of(tile, shift, flip, corner_at, corner_shift)


def setup_kernel(plan, chan, shape, edge_ref, corner_ref, weight_ref, table_ref, taps_ref, back_ref, turn):
    table_ref[...] = halo_table(plan, edge_ref, corner_ref, *shape)
    total = weight_ref.shape[2]
    own = lax.axis_index("ch") * chan
    shift = (total - own) % total
    for i in range(3):
        for j in range(3):
            turn[...] = weight_ref[i, j].astype(jnp.float32)
            rows = pltpu.roll(turn[pl.ds(pl.multiple_of(own, chan), chan)], shift, 1)
            cols = slice(j * total, (j + 1) * total)
            taps_ref[i * chan : (i + 1) * chan, cols] = rows.astype(jnp.bfloat16)
            turn[...] = turn[...].T
            rows = pltpu.roll(turn[pl.ds(pl.multiple_of(own, chan), chan)], shift, 1)
            cols = slice((2 - j) * total, (3 - j) * total)
            back_ref[(2 - i) * chan : (3 - i) * chan, cols] = rows.astype(jnp.bfloat16)


def setup(plan, edge_table, corner_table, weight, chan, counts, col_len, unit):
    edges = jnp.transpose(edge_table, (2, 1, 0))
    corners = jnp.transpose(corner_table, (1, 2, 0))
    total = weight.shape[2]
    vmem = pl.BlockSpec(memory_space=pltpu.VMEM)
    taps = jax.ShapeDtypeStruct((3 * chan, 3 * total), jnp.bfloat16)
    table = jax.ShapeDtypeStruct((12 * (RB // unit) + 8, edges.shape[2]), jnp.int32)
    return pl.pallas_call(
        lambda *refs: setup_kernel(plan, chan, (*counts, col_len, unit), *refs),
        in_specs=[vmem] * 3,
        out_specs=[vmem] * 3,
        out_shape=[table, taps, taps],
        scratch_shapes=[pltpu.VMEM((total, total), jnp.float32)],
        compiler_params=pltpu.CompilerParams(vmem_limit_bytes=VMEM_LIMIT),
        name="setup",
    )(edges, corners, weight)


def from_others(array, ch_count):
    return [array] + [
        lax.ppermute(array, "ch", [((i + k) % ch_count, i) for i in range(ch_count)])
        for k in range(1, ch_count)
    ]


class Place:
    @staticmethod
    def place():
        return (lax.axis_index("px"), lax.axis_index("py"))


class SquareHalo(Place):
    counts = (2, 1, 1, 2)
    extras = (None, 0, HALF, None)

    def __init__(self, quads):
        self.quads = quads
        self.span = 2 * quads + 1

    def roles(self):
        row_pos, col_pos = self.place()
        px_end = (row_pos == 0) | (row_pos == 3)
        py_end = (col_pos == 0) | (col_pos == 3)
        side = jnp.where(
            py_end, jnp.where(col_pos == 0, 0, 1), jnp.where(row_pos == 0, 2, 3)
        )
        corner = px_end & py_end
        middle = (px_end | py_end) & jnp.logical_not(corner)
        return (px_end, corner, middle, side, jnp.where(px_end, col_pos, row_pos))

    def chosen_sides(self):
        row_pos, col_pos = self.place()
        px_end, corner, middle, side, seg = self.roles()
        row_line = jnp.where(col_pos == 0, 0, 1)
        col_line = jnp.where(row_pos == 0, 2, 3)
        to_px, to_py = (jnp.where(row_pos == 1, 3, 2), jnp.where(col_pos == 1, 1, 0))
        facing = jnp.where(px_end, to_py, to_px)
        return [
            jnp.where(seg == 1, side, facing),
            jnp.where(seg == 1, facing, side),
            jnp.where(row_pos % 2 == 0, 3, 2),
            jnp.where(col_pos % 2 == 0, 1, 0),
            jnp.where(corner, row_line, jnp.where(middle, side, to_py)),
            jnp.where(corner, col_line, side),
        ]

    def exchange(self, pair, col_side, row_side, lines, corner):
        every = [(x, y) for x in range(4) for y in range(4)]
        axes = ("px", "py")
        swap = lambda array, pairs: lax.ppermute(
            array, axes, [(a[0] * 4 + a[1], b[0] * 4 + b[1]) for a, b in pairs]
        )
        ends = (0, 3)
        corners = [(x, y) for x in ends for y in ends]
        spot = lambda side, seg: ((seg, 0), (seg, 3), (0, seg), (3, seg))[side]
        beside = [(spot(side, k), spot(side, 3 - k)) for side in range(4) for k in (1, 2)]
        beside += [((x, y), (3 - x, y)) for x in (1, 2) for y in (1, 2)]
        paired = swap(pair, beside)
        near_col = swap(col_side, [((x, y), (x ^ 1, y)) for x, y in every])
        near_row = swap(row_side, [((x, y), (x, y ^ 1)) for x, y in every])
        small = lambda pairs: swap(corner, pairs)
        diagonal = [
            small([((x, y), (x ^ 1, y ^ 1)) for x, y in every]),
            small([((x, y), (3 - x, y ^ 1)) for x, y in every if x in (1, 2)]),
            small([((x, y), (x ^ 1, 3 - y)) for x, y in every if y in (1, 2)]),
            small([((x, y), (3 - x, 3 - y)) for x, y in every if x in (1, 2) and y in (1, 2)]),
        ]
        lines = self.line_message(lines, paired, near_col, near_row)
        across = []
        for j in (1, 2, 3):
            pairs = [
                (spot(side, k), spot(side ^ j, k if j == 3 else 3 - k))
                for side in range(4)
                for k in (1, 2)
            ]
            pairs += [(corners[c], corners[c ^ j]) for c in range(4)]
            if j == 1:
                pairs += [((x, y), (x, 3 - y)) for x in (1, 2) for y in (1, 2)]
            across.append(swap(lines, pairs))
        return [lines, *across, paired, near_col, near_row, *diagonal]

    def line_message(self, *parts):
        vmem = pl.BlockSpec(memory_space=pltpu.VMEM)

        def kernel(lines_ref, paired_ref, col_ref, row_ref, out_ref):
            _, _, middle, _, seg = self.roles()
            for at in range(2 * self.quads):
                theirs = middle & (seg - 1 != at // self.quads)
                out_ref[at] = jnp.where(theirs, paired_ref[at], lines_ref[at])
            out_ref[2 * self.quads] = col_ref[self.quads] + row_ref[self.quads]

        return pl.pallas_call(
            kernel,
            in_specs=[vmem] * 4,
            out_specs=vmem,
            out_shape=jax.ShapeDtypeStruct((self.span, *parts[0].shape[1:]), jnp.bfloat16),
            compiler_params=pltpu.CompilerParams(vmem_limit_bytes=VMEM_LIMIT),
            name="lines",
        )(*parts)

    def owner(self, s, k):
        far = jnp.where(k >= 2, 1, 0)
        return jnp.where(s < 2, 2 * far + s, 2 * (s - 2) + far)

    def me(self):
        row_pos, col_pos = self.place()
        return jnp.where(row_pos > 0, 2, 0) + jnp.where(col_pos > 0, 1, 0)

    def strip_cell(self, g, s, at):
        _, corner, _, side, _ = self.roles()
        k = at // RB
        at_corner = (self.me() ^ self.owner(s, k)) * self.span + (s // 2) * self.quads
        at_middle = (side ^ s) * self.span + (k - 1) * self.quads
        return (jnp.where(corner, at_corner, at_middle) + g // GROUP, (g % GROUP) * 32)

    def near_cell(self, edge, face):
        row_pos, col_pos = self.place()
        px_end, _, _, _, seg = self.roles()
        paired = 4 * self.span + (seg - 1) * self.quads
        near_col = 4 * self.span + 2 * self.quads
        near_row = near_col + self.quads + 1
        by_col = jnp.where(row_pos % 2 == 3 - edge, near_col, paired)
        rest = jnp.where(px_end, paired, self.span)
        by_row = jnp.where(col_pos % 2 == 1 - edge, near_row, rest)
        return jnp.where(edge < 2, by_row, by_col) + face // GROUP

    def corner_cell(self, g, s, at):
        _, corner, _, side, seg = self.roles()
        k, hi = (at // RB, jnp.where(at % RB == 0, 0, 1))
        end = (k == 0) | (k == 3)
        line_tile, line_lane = self.strip_cell(g, s, at)
        owner = self.owner(s, k)
        source = self.me() ^ owner
        half = jnp.where(s < 2, 0, HALF)
        for j in range(4):
            their_side = side ^ j
            their_seg = seg if j in (0, 3) else 3 - seg
            hit = jnp.logical_not(corner) & (self.owner(their_side, their_seg) == owner)
            source = jnp.where(hit, j, source)
            half = jnp.where(hit, jnp.where(their_side < 2, 0, HALF), half)
        q = jnp.where(s < 2, 2 * s + hi, s - 2 + 2 * hi)
        in_line = (corner & end) | jnp.logical_not(corner | end)
        tile = jnp.where(in_line, line_tile, source * self.span + 2 * self.quads)
        return (tile, jnp.where(in_line, line_lane + at % RB, half + g * 4 + q))

    def diagonal_cell(self, face, q, px, py):
        row_pos, col_pos = self.place()
        far = jnp.where(px == (row_pos ^ 1), 0, 1) + jnp.where(py == (col_pos ^ 1), 0, 2)
        return (4 * self.span + 4 * self.quads + 2 + far, face * 4 + q)


class GatheredHalo(Place):
    counts = (1, 1, 1, 1, 2)

    extras = (None,) * 5

    def __init__(self, quads, px_count, py_count, col_len):
        self.quads = quads
        self.size = (px_count, py_count)
        self.col_len = col_len

    def chosen_sides(self):
        row_pos, col_pos = self.place()
        return [0, 1, 2, 3, jnp.where(col_pos == 0, 0, 1), jnp.where(row_pos == 0, 2, 3)]

    def exchange(self, top, bottom, left, right, lines, corner):
        px_count, py_count = self.size
        up = lambda n: [(i, i + 1) for i in range(n - 1)]
        down = lambda n: [(i + 1, i) for i in range(n - 1)]
        return [
            lax.ppermute(bottom, "py", up(py_count)),
            lax.ppermute(top, "py", down(py_count)),
            lax.ppermute(right, "px", up(px_count)),
            lax.ppermute(left, "px", down(px_count)),
            lax.all_gather(lines, ("px", "py"), axis=0, tiled=True),
            lax.all_gather(corner, ("px", "py"), axis=0, tiled=True),
        ]

    def strip_cell(self, g, s, at):
        px_count, py_count = self.size
        length = jnp.where(s < 2, RB, self.col_len)
        seg = at // length
        px = jnp.where(s < 2, seg, (s - 2) * (px_count - 1))
        py = jnp.where(s < 2, s * (py_count - 1), seg)
        tile = (4 + (px * py_count + py) * 2 + s // 2) * self.quads + g // GROUP
        return (tile, (g % GROUP) * 32 + at % length)

    def near_cell(self, edge, face):
        return edge * self.quads + face // GROUP

    def corner_cell(self, g, s, at):
        return self.strip_cell(g, s, at)

    def diagonal_cell(self, face, q, px, py):
        px_count, py_count = self.size
        base = (4 + 2 * px_count * py_count) * self.quads
        return (base + px * py_count + py, face * 4 + q)


def local(features, cotangent, weight, edge_table, corner_table):
    chan, faces = features.shape[:2]
    tile = features.shape[4]
    col_len = tile // RB
    unit = min(RB, col_len)
    units = (RB // unit, RB // unit, col_len // unit, col_len // unit)
    px_count, py_count, ch_count = [lax.axis_size(name) for name in ("px", "py", "ch")]
    ring = jnp.asarray(ring_matrix(col_len), jnp.bfloat16)
    cornsel = jnp.asarray(corner_matrix(), jnp.bfloat16)
    spread = jnp.asarray(spread_matrix(col_len), jnp.bfloat16)
    rev = jnp.asarray(reverse_matrix(unit), jnp.bfloat16)
    if px_count == py_count == 4 and col_len == RB and 4 * faces <= HALF:
        plan = SquareHalo(faces // GROUP)
    else:
        plan = GatheredHalo(faces // GROUP, px_count, py_count, col_len)

    feats = jnp.transpose(features.reshape(chan, faces, tile), (1, 0, 2))
    cot = jnp.transpose(cotangent.reshape(chan, faces, tile), (1, 0, 2))
    fields = from_others(feats, ch_count)
    parts = rings_of(feats, plan, ring, cornsel)
    table, taps, back_taps = setup(
        plan, edge_table, corner_table, weight, chan, (px_count, py_count), col_len, unit
    )
    tiles = plan.exchange(*parts)
    halo = assemble_halo(table, tiles, rev, faces, units, unit)
    halos = from_others(halo, ch_count)
    old, chunks, first = ([], [], 0)
    for count in CALLS:
        act, gated, *parts = forward(
            first, count, plan, fields, halos, cot, taps, spread, ring, cornsel, old
        )
        old = [*parts, act]
        chunks.append((first, from_others(gated, ch_count)))
        first += count

    tiles = plan.exchange(*parts)
    halo = assemble_halo(table, tiles, rev, faces, units, unit)
    halos = from_others(halo, ch_count)
    grad = None
    for first, fields in chunks:
        grad = backward(first, faces, fields, halos, back_taps, spread, grad)

    shape = (chan, faces, 1, 1, tile)
    return (
        jnp.transpose(act, (1, 0, 2)).reshape(shape),
        jnp.transpose(grad, (1, 0, 2)).reshape(shape),
    )


def solution(mesh):
    spec = P("ch", None, "py", "px", None)
    return jax.shard_map(
        local,
        mesh=mesh,
        in_specs=(spec, spec, P(), P(), P()),
        out_specs=(spec, spec),
        check_vma=False,
    )
```

```python
import jax
import jax.numpy as jnp
import numpy as np
from jax import lax
from jax.experimental import pallas as pl
from jax.experimental.pallas import tpu as pltpu
from jax.sharding import PartitionSpec as P

RB = 32
GROUP = 4
LANES = 128
CALLS = (3,)
VMEM_LIMIT = 60 * 1024 * 1024
STRIP_LANE = (96, 0, 32, 64)
HALF = 48


def ring_matrix(col_len):
    mat = np.zeros((col_len * RB, LANES), np.float32)
    for b in range(RB):
        mat[b, b] = 1
        mat[(col_len - 1) * RB + b, 32 + b] = 1
    for a in range(col_len):
        mat[a * RB, 64 + a] = 1
        mat[a * RB + RB - 1, 96 + a] = 1
    return mat


def corner_matrix():
    mat = np.zeros((LANES, LANES), np.float32)
    for q, lane in enumerate((0, RB - 1, 32, 32 + RB - 1)):
        mat[lane, q] = 1
    return mat


def reverse_matrix(unit):
    mat = np.zeros((LANES, LANES), np.float32)
    for lane in range(LANES):
        mat[lane, (lane // unit) * unit + unit - 1 - lane % unit] = 1
    return mat


def spread_matrix(col_len):
    width = col_len * RB + LANES
    mat = np.zeros((LANES, width), np.float32)
    top, bottom = (col_len + 3) * RB, col_len * RB
    mat[0, top] = 1
    mat[1, top + RB - 1] = 1
    mat[2, bottom] = 1
    mat[3, bottom + RB - 1] = 1
    for a in range(col_len):
        mat[STRIP_LANE[2] + a, a * RB] = 1
        mat[STRIP_LANE[3] + a, a * RB + RB - 1] = 1
    return mat


def lane_iota(shape):
    return lax.broadcasted_iota(jnp.int32, shape, len(shape) - 1)


def side_tiles(fields, first_face, ring_ref, cornsel_ref):
    chan = fields.shape[0] // GROUP
    lane = lane_iota((chan, LANES))
    flat = jnp.dot(fields, ring_ref[...], preferred_element_type=jnp.float32)
    picked = jnp.dot(
        flat.astype(jnp.bfloat16), cornsel_ref[...], preferred_element_type=jnp.float32
    )
    rings = [flat[g * chan : (g + 1) * chan] for g in range(GROUP)]
    tiles = []
    for side in range(4):
        tile = jnp.zeros((chan, LANES), jnp.float32)
        for g, ring in enumerate(rings):
            moved = pltpu.roll(ring, ((g - side) * 32) % LANES, 1) if g != side else ring
            tile = jnp.where(lane // 32 == g, moved, tile)
        tiles.append(tile.astype(jnp.bfloat16))
    corners = jnp.zeros((chan, LANES), jnp.float32)
    for g in range(GROUP):
        corners += pltpu.roll(picked[g * chan : (g + 1) * chan], (first_face + g) * 4, 1)
    return (tiles, corners)


def hand_out(plan, steps, packs, corners, outs):
    chosen = iter(plan.chosen_sides())
    for out, count, extra in zip(outs, plan.counts, plan.extras):
        for at in range(count):
            base = next(chosen) * steps
            for q in range(steps):
                out[at * steps + q] = packs[base + q]
        if extra is not None:
            moved = pltpu.roll(corners, extra, 1) if extra else corners
            out[count * steps] = moved.astype(jnp.bfloat16)
    outs[-1][0] = corners.astype(jnp.bfloat16)


def ring_outs(faces, chan, plan):
    steps = faces // GROUP
    tiles = [n * steps + (extra is not None) for n, extra in zip(plan.counts, plan.extras)]
    return [jax.ShapeDtypeStruct((n, chan, LANES), jnp.bfloat16) for n in (*tiles, 1)]


def rings_kernel(steps, plan, field_ref, ring_ref, cornsel_ref, *refs):
    outs, (packs, corner_acc) = (refs[:-2], refs[-2:])
    step = pl.program_id(0)
    fields = field_ref[...].reshape(-1, field_ref.shape[2])
    tiles, corners = side_tiles(fields, step * GROUP, ring_ref, cornsel_ref)
    for side, tile in enumerate(tiles):
        packs[side * steps + step] = tile

    @pl.when(step == 0)
    def _():
        corner_acc[...] = jnp.zeros_like(corner_acc)

    corner_acc[...] += corners

    @pl.when(step == steps - 1)
    def _():
        hand_out(plan, steps, packs, corner_acc[...], outs)


def whole_spec(array):
    zeros = (0,) * array.ndim
    return pl.BlockSpec(array.shape, lambda *_: zeros)


def rings_of(field, plan, ring, cornsel):
    faces, chan, tile = field.shape
    steps = faces // GROUP
    outs = ring_outs(faces, chan, plan)
    return pl.pallas_call(
        lambda *refs: rings_kernel(steps, plan, *refs),
        grid=(steps,),
        in_specs=[
            pl.BlockSpec((GROUP, chan, tile), lambda i: (i, 0, 0)),
            whole_spec(ring),
            whole_spec(cornsel),
        ],
        out_specs=[whole_spec(out) for out in outs],
        out_shape=outs,
        scratch_shapes=[
            pltpu.VMEM((4 * steps, chan, LANES), jnp.bfloat16),
            pltpu.VMEM((chan, LANES), jnp.float32),
        ],
        compiler_params=pltpu.CompilerParams(vmem_limit_bytes=VMEM_LIMIT),
        name="rings",
    )(field, ring, cornsel)


def halo_kernel(faces, units, unit, *refs):
    table, tile_refs, (rev_ref, halo_ref, pool, turn_acc) = (refs[0], refs[1:-4], refs[-4:])
    chan = halo_ref.shape[1]
    lane = lane_iota((chan, LANES))
    at = 0
    for ref in tile_refs:
        pool[at : at + ref.shape[0]] = ref[...]
        at += ref.shape[0]
    corner_tile = jnp.zeros((chan, LANES), jnp.float32)
    most = max(units)
    rows = 4 * most
    for f in range(faces):
        tile = jnp.zeros((chan, LANES), jnp.float32)
        turned = jnp.zeros((chan, LANES), jnp.float32)
        for e in range(4):
            for un in range(units[e]):
                base = STRIP_LANE[e] + un * unit
                span = (lane >= base) & (lane < base + unit)
                entry = e * most + un
                source = pool[table[entry, f]].astype(jnp.float32)
                moved = pltpu.roll(source, table[rows + entry, f], 1)
                flip = table[2 * rows + entry, f] == 1
                tile = jnp.where(span & jnp.logical_not(flip), moved, tile)
                turned = jnp.where(span & flip, moved, turned)
        halo_ref[f] = tile.astype(jnp.bfloat16)
        turn_acc[f] = turned.astype(jnp.bfloat16)
        for c in range(4):
            source = pool[table[3 * rows + c, f]].astype(jnp.float32)
            moved = pltpu.roll(source, table[3 * rows + 4 + c, f], 1)
            corner_tile = jnp.where(lane == f * 4 + c, moved, corner_tile)
    turned = jnp.dot(
        turn_acc[...].reshape(faces * chan, LANES), rev_ref[...], preferred_element_type=jnp.float32
    ).reshape(faces, chan, LANES)
    for f in range(faces):
        halo_ref[f] += turned[f].astype(jnp.bfloat16)
    halo_ref[faces] = corner_tile.astype(jnp.bfloat16)


def assemble_halo(table, tiles, rev, faces, units, unit):
    chan = tiles[0].shape[1]
    halo = jax.ShapeDtypeStruct((faces + 1, chan, LANES), jnp.bfloat16)
    vmem = pl.BlockSpec(memory_space=pltpu.VMEM)
    smem = pl.BlockSpec(memory_space=pltpu.SMEM)
    return pl.pallas_call(
        lambda *refs: halo_kernel(faces, units, unit, *refs),
        in_specs=[smem] + [vmem] * (len(tiles) + 1),
        out_specs=vmem,
        out_shape=halo,
        scratch_shapes=[
            pltpu.VMEM((sum(t.shape[0] for t in tiles), chan, LANES), jnp.bfloat16),
            pltpu.VMEM((faces, chan, LANES), jnp.bfloat16),
        ],
        compiler_params=pltpu.CompilerParams(vmem_limit_bytes=VMEM_LIMIT),
        name="halo",
    )(table, *tiles, rev)


def sides_of(step, halo_refs, corner_refs, spread_ref, beside_ref):
    corners = jnp.concatenate([ref[0].astype(jnp.float32) for ref in corner_refs], axis=0)
    lane = lane_iota(corners.shape)
    sides = []
    for g in range(GROUP):
        halo = jnp.concatenate([ref[g].astype(jnp.float32) for ref in halo_refs], axis=0)
        moved = pltpu.roll(corners, (LANES - (step * GROUP + g) * 4) % LANES, 1)
        sides.append(jnp.where(lane < 4, moved, halo).astype(jnp.bfloat16))
    beside = jnp.dot(
        jnp.concatenate(sides, axis=0), spread_ref[...], preferred_element_type=jnp.float32
    )
    beside_ref[...] = beside.astype(jnp.bfloat16).reshape(beside_ref.shape)


def conv_face(g, field_refs, halo_refs, taps_ref, beside_ref, stack_ref):
    chan, tile = field_refs[0].shape[1:]
    total = chan * len(field_refs)
    width = tile + LANES
    for k, (field, halo) in enumerate(zip(field_refs, halo_refs)):
        stack_ref[total + k * chan : total + (k + 1) * chan, :tile] = field[g]
        stack_ref[total + k * chan : total + (k + 1) * chan, tile:] = halo[g]
    middle = stack_ref[total : 2 * total]
    beside = beside_ref[g]
    col = lane_iota((total, width)) % RB
    stack_ref[:total] = jnp.where(col == 0, beside, pltpu.roll(middle, 1, 1))
    stack_ref[2 * total :] = jnp.where(col == RB - 1, beside, pltpu.roll(middle, width - 1, 1))
    sums = jnp.dot(taps_ref[...], stack_ref[...], preferred_element_type=jnp.float32)
    above = pltpu.roll(sums[:chan], RB, 1)
    below = pltpu.roll(sums[2 * chan :], width - RB, 1)
    return (above + sums[chan : 2 * chan] + below)[:, :tile]


def split_refs(refs, *counts):
    out = []
    for count in counts:
        out.append(refs[:count])
        refs = refs[count:]
    return (*out, refs)


def forward_kernel(first, count, steps, pieces, plan, *refs):
    olds = 3 if first else 0
    fields, halos, corners, consts, old, refs = split_refs(refs, pieces, pieces, pieces, 5, olds)
    cot_ref, taps_ref, spread_ref, ring_ref, cornsel_ref = consts
    outs, (packs, corner_acc, made, beside_ref, stacks) = (refs[:-5], refs[-5:])
    act_ref, gated_ref = outs[:2]
    here = pl.program_id(0)
    step = first + here

    @pl.when(here == 0)
    def _():
        if first:
            packs[...] = old[0][...]
            corner_acc[...] = old[1][0].astype(jnp.float32)
        else:
            corner_acc[...] = jnp.zeros_like(corner_acc)

    sides_of(step, halos, corners, spread_ref, beside_ref)
    chan = act_ref.shape[1]
    for g in range(GROUP):
        pre = conv_face(g, fields, halos, taps_ref, beside_ref, stacks.at[g % 2])
        sig = 1.0 / (1.0 + jnp.exp(-pre))
        act_ref[g] = (pre * sig).astype(jnp.bfloat16)
        gated = cot_ref[g].astype(jnp.float32) * sig * (1.0 + pre * (1.0 - sig))
        gated_ref[g] = gated.astype(jnp.bfloat16)
        made[g * chan : (g + 1) * chan] = gated.astype(jnp.bfloat16)
    tiles, corner = side_tiles(made[...], step * GROUP, ring_ref, cornsel_ref)
    for side, tile in enumerate(tiles):
        packs[side * steps + step] = tile
    corner_acc[...] += corner

    @pl.when(here == count - 1)
    def _():
        if first + count == steps:
            hand_out(plan, steps, packs, corner_acc[...], outs[2:])
        else:
            outs[2][...] = packs[...]
            outs[3][0] = corner_acc[...].astype(jnp.bfloat16)


def conv_specs(fields, halos, first, field_first):
    _, chan, tile = fields[0].shape
    last = halos[0].shape[0] - 1
    return (
        [pl.BlockSpec((GROUP, chan, tile), lambda i: (field_first + i, 0, 0)) for _ in fields]
        + [pl.BlockSpec((GROUP, chan, LANES), lambda i: (first + i, 0, 0)) for _ in halos]
        + [pl.BlockSpec((1, chan, LANES), lambda i: (last, 0, 0)) for _ in halos]
    )


def conv_scratch(chan, pieces, tile):
    total = chan * pieces
    return [
        pltpu.VMEM((GROUP, total, tile + LANES), jnp.bfloat16),
        pltpu.VMEM((2, 3 * total, tile + LANES), jnp.bfloat16),
    ]


def forward(first, count, plan, fields, halos, cot, taps, spread, ring, cornsel, old):
    faces, chan, tile = fields[0].shape
    steps = faces // GROUP
    pieces = len(fields)
    if first + count < steps:
        outs = [
            jax.ShapeDtypeStruct((4 * steps, chan, LANES), jnp.bfloat16),
            jax.ShapeDtypeStruct((1, chan, LANES), jnp.bfloat16),
        ]
    else:
        outs = ring_outs(faces, chan, plan)
    whole = jax.ShapeDtypeStruct((faces, chan, tile), jnp.bfloat16)
    chunk = jax.ShapeDtypeStruct((count * GROUP, chan, tile), jnp.bfloat16)
    block = pl.BlockSpec((GROUP, chan, tile), lambda i: (first + i, 0, 0))
    args = [*fields, *halos, *halos, cot, taps, spread, ring, cornsel, *old]
    return pl.pallas_call(
        lambda *refs: forward_kernel(first, count, steps, pieces, plan, *refs),
        grid=(count,),
        in_specs=conv_specs(fields, halos, first, first)
        + [block, whole_spec(taps), whole_spec(spread), whole_spec(ring), whole_spec(cornsel)]
        + [whole_spec(array) for array in old[:2]]
        + [pl.BlockSpec(memory_space=pl.ANY) for _ in old[2:]],
        out_specs=[block, pl.BlockSpec((GROUP, chan, tile), lambda i: (i, 0, 0))]
        + [whole_spec(o) for o in outs],
        out_shape=[whole, chunk] + outs,
        input_output_aliases={len(args) - 1: 0} if old else {},
        scratch_shapes=[
            pltpu.VMEM((4 * steps, chan, LANES), jnp.bfloat16),
            pltpu.VMEM((chan, LANES), jnp.float32),
            pltpu.VMEM((GROUP * chan, tile), jnp.bfloat16),
        ]
        + conv_scratch(chan, pieces, tile),
        compiler_params=pltpu.CompilerParams(vmem_limit_bytes=VMEM_LIMIT),
        name="forward",
    )(*args)


def backward_kernel(first, pieces, *refs):
    fields, halos, corners, consts, refs = split_refs(refs, pieces, pieces, pieces, 2)
    taps_ref, spread_ref = consts
    grad_ref, beside_ref, stacks = refs[-3:]
    sides_of(first + pl.program_id(0), halos, corners, spread_ref, beside_ref)
    for g in range(GROUP):
        total = conv_face(g, fields, halos, taps_ref, beside_ref, stacks.at[g % 2])
        grad_ref[g] = total.astype(jnp.bfloat16)


def backward(first, faces, fields, halos, taps, spread, grad):
    held, chan, tile = fields[0].shape
    pieces = len(fields)
    aside = [] if grad is None else [grad]
    args = [*fields, *halos, *halos, taps, spread, *aside]
    return pl.pallas_call(
        lambda *refs: backward_kernel(first, pieces, *refs),
        grid=(held // GROUP,),
        in_specs=conv_specs(fields, halos, first, 0)
        + [whole_spec(taps), whole_spec(spread)]
        + [pl.BlockSpec(memory_space=pl.ANY) for _ in aside],
        out_specs=pl.BlockSpec((GROUP, chan, tile), lambda i: (first + i, 0, 0)),
        out_shape=jax.ShapeDtypeStruct((faces, chan, tile), jnp.bfloat16),
        input_output_aliases={len(args) - 1: 0} if aside else {},
        scratch_shapes=conv_scratch(chan, pieces, tile),
        compiler_params=pltpu.CompilerParams(vmem_limit_bytes=VMEM_LIMIT),
        name="backward",
    )(*args)


def rows_of(*parts):
    return jnp.concatenate(parts, axis=0)


def halo_table(plan, edge_ref, corner_ref, px_count, py_count, col_len, unit):
    row_pos, col_pos = plan.place()
    faces = edge_ref.shape[2]
    side_len = px_count * RB
    most = RB // unit
    shape = (4 * most, faces)
    face = lane_iota(shape)
    row = lax.broadcasted_iota(jnp.int32, shape, 0)
    edge, un = (row // most, row % most)
    g, s, r = [
        rows_of(*[edge_ref[i, e : e + 1] for e in range(4) for _ in range(most)]) for i in range(3)
    ]
    border = ((edge == 0) & (col_pos == 0)) | ((edge == 1) & (col_pos == py_count - 1))
    border |= ((edge == 2) & (row_pos == 0)) | ((edge == 3) & (row_pos == px_count - 1))
    at = jnp.where(edge < 2, row_pos * RB, col_pos * col_len) + un * unit
    at = jnp.clip(at, 0, side_len - unit)
    at = jnp.where(r == 1, side_len - unit - at, at)
    line_tile, line_lane = plan.strip_cell(g, s, at)
    tile = jnp.where(border, line_tile, plan.near_cell(edge, face))
    lane = jnp.where(border, line_lane, (face % GROUP) * 32 + un * unit)
    first = jnp.where(edge == 0, STRIP_LANE[0], jnp.where(edge == 1, STRIP_LANE[1], edge * 32 - 32))
    shift = (first + un * unit - lane + LANES) % LANES
    flip = jnp.where(border & (r == 1), 1, 0)

    shape = (4, faces)
    face = lane_iota(shape)
    c = lax.broadcasted_iota(jnp.int32, shape, 0)
    down, right = (c // 2, c % 2)
    row_on = ((down == 0) & (col_pos == 0)) | ((down == 1) & (col_pos == py_count - 1))
    col_on = ((right == 0) & (row_pos == 0)) | ((right == 1) & (row_pos == px_count - 1))
    row_at = row_pos * RB + jnp.where(right == 1, RB, -1)
    col_at = col_pos * col_len + jnp.where(down == 1, col_len, -1)
    edge_of = lambda i, edges: rows_of(*[edge_ref[i, e : e + 1] for e in edges])
    g, s, r = [
        jnp.where(row_on, edge_of(i, (0, 0, 1, 1)), edge_of(i, (2, 3, 2, 3))) for i in range(3)
    ]
    at = jnp.clip(jnp.where(row_on, row_at, col_at), 0, side_len - 1)
    at = jnp.where(r == 1, side_len - 1 - at, at)
    h, q = [rows_of(*[corner_ref[k, i : i + 1] for k in range(4)]) for i in range(2)]
    both = row_on & col_on
    g = jnp.where(both, h, g)
    s = jnp.where(both, q // 2, s)
    at = jnp.where(both, (q % 2) * (side_len - 1), at)
    line_tile, line_lane = plan.corner_cell(g, s, at)
    diag_px = jnp.clip(row_pos + 2 * right - 1, 0, px_count - 1)
    diag_py = jnp.clip(col_pos + 2 * down - 1, 0, py_count - 1)
    diag_tile, diag_lane = plan.diagonal_cell(face, 3 - c, diag_px, diag_py)
    on = row_on | col_on
    corner_at = jnp.where(on, line_tile, diag_tile)
    corner_lane = jnp.where(on, line_lane, diag_lane)
    corner_shift = (face * 4 + c - corner_lane + LANES) % LANES
    return rows_of(tile, shift, flip, corner_at, corner_shift)


def setup_kernel(plan, chan, shape, edge_ref, corner_ref, weight_ref, table_ref, taps_ref, back_ref, turn):
    table_ref[...] = halo_table(plan, edge_ref, corner_ref, *shape)
    total = weight_ref.shape[2]
    own = lax.axis_index("ch") * chan
    shift = (total - own) % total
    for i in range(3):
        for j in range(3):
            turn[...] = weight_ref[i, j].astype(jnp.float32)
            rows = pltpu.roll(turn[pl.ds(pl.multiple_of(own, chan), chan)], shift, 1)
            cols = slice(j * total, (j + 1) * total)
            taps_ref[i * chan : (i + 1) * chan, cols] = rows.astype(jnp.bfloat16)
            turn[...] = turn[...].T
            rows = pltpu.roll(turn[pl.ds(pl.multiple_of(own, chan), chan)], shift, 1)
            cols = slice((2 - j) * total, (3 - j) * total)
            back_ref[(2 - i) * chan : (3 - i) * chan, cols] = rows.astype(jnp.bfloat16)


def setup(plan, edge_table, corner_table, weight, chan, counts, col_len, unit):
    edges = jnp.transpose(edge_table, (2, 1, 0))
    corners = jnp.transpose(corner_table, (1, 2, 0))
    total = weight.shape[2]
    vmem = pl.BlockSpec(memory_space=pltpu.VMEM)
    taps = jax.ShapeDtypeStruct((3 * chan, 3 * total), jnp.bfloat16)
    table = jax.ShapeDtypeStruct((12 * (RB // unit) + 8, edges.shape[2]), jnp.int32)
    return pl.pallas_call(
        lambda *refs: setup_kernel(plan, chan, (*counts, col_len, unit), *refs),
        in_specs=[vmem] * 3,
        out_specs=[vmem] * 3,
        out_shape=[table, taps, taps],
        scratch_shapes=[pltpu.VMEM((total, total), jnp.float32)],
        compiler_params=pltpu.CompilerParams(vmem_limit_bytes=VMEM_LIMIT),
        name="setup",
    )(edges, corners, weight)


def from_others(array, ch_count):
    return [array] + [
        lax.ppermute(array, "ch", [((i + k) % ch_count, i) for i in range(ch_count)])
        for k in range(1, ch_count)
    ]


class Place:
    @staticmethod
    def place():
        return (lax.axis_index("px"), lax.axis_index("py"))


class SquareHalo(Place):
    counts = (2, 1, 1, 2)
    extras = (None, 0, HALF, None)

    def __init__(self, quads):
        self.quads = quads
        self.span = 2 * quads + 1

    def roles(self):
        row_pos, col_pos = self.place()
        px_end = (row_pos == 0) | (row_pos == 3)
        py_end = (col_pos == 0) | (col_pos == 3)
        side = jnp.where(
            py_end, jnp.where(col_pos == 0, 0, 1), jnp.where(row_pos == 0, 2, 3)
        )
        corner = px_end & py_end
        middle = (px_end | py_end) & jnp.logical_not(corner)
        return (px_end, corner, middle, side, jnp.where(px_end, col_pos, row_pos))

    def chosen_sides(self):
        row_pos, col_pos = self.place()
        px_end, corner, middle, side, seg = self.roles()
        row_line = jnp.where(col_pos == 0, 0, 1)
        col_line = jnp.where(row_pos == 0, 2, 3)
        to_px, to_py = (jnp.where(row_pos == 1, 3, 2), jnp.where(col_pos == 1, 1, 0))
        facing = jnp.where(px_end, to_py, to_px)
        return [
            jnp.where(seg == 1, side, facing),
            jnp.where(seg == 1, facing, side),
            jnp.where(row_pos % 2 == 0, 3, 2),
            jnp.where(col_pos % 2 == 0, 1, 0),
            jnp.where(corner, row_line, jnp.where(middle, side, to_py)),
            jnp.where(corner, col_line, side),
        ]

    def exchange(self, table, pair, col_side, row_side, lines, corner):
        every = [(x, y) for x in range(4) for y in range(4)]
        axes = ("px", "py")
        swap = lambda array, pairs: lax.ppermute(
            array, axes, [(a[0] * 4 + a[1], b[0] * 4 + b[1]) for a, b in pairs]
        )
        ends = (0, 3)
        corners = [(x, y) for x in ends for y in ends]
        spot = lambda side, seg: ((seg, 0), (seg, 3), (0, seg), (3, seg))[side]
        beside = [(spot(side, k), spot(side, 3 - k)) for side in range(4) for k in (1, 2)]
        beside += [((x, y), (3 - x, y)) for x in (1, 2) for y in (1, 2)]
        small = lambda pairs: swap(corner, pairs)
        diagonal = [
            small([((x, y), (x ^ 1, y ^ 1)) for x, y in every]),
            small([((x, y), (3 - x, y ^ 1)) for x, y in every if x in (1, 2)]),
            small([((x, y), (x ^ 1, 3 - y)) for x, y in every if y in (1, 2)]),
            small([((x, y), (3 - x, 3 - y)) for x, y in every if x in (1, 2) and y in (1, 2)]),
        ]
        pair, col_side, row_side, _, *diagonal = lax.optimization_barrier(
            (pair, col_side, row_side, table, *diagonal)
        )
        paired = swap(pair, beside)
        near_col = swap(col_side, [((x, y), (x ^ 1, y)) for x, y in every])
        near_row = swap(row_side, [((x, y), (x, y ^ 1)) for x, y in every])
        lines = self.line_message(lines, paired, near_col, near_row)
        across = []
        for j in (1, 2, 3):
            pairs = [
                (spot(side, k), spot(side ^ j, k if j == 3 else 3 - k))
                for side in range(4)
                for k in (1, 2)
            ]
            pairs += [(corners[c], corners[c ^ j]) for c in range(4)]
            if j == 1:
                pairs += [((x, y), (x, 3 - y)) for x in (1, 2) for y in (1, 2)]
            across.append(swap(lines, pairs))
        return [lines, *across, paired, near_col, near_row, *diagonal]

    def line_message(self, *parts):
        vmem = pl.BlockSpec(memory_space=pltpu.VMEM)

        def kernel(lines_ref, paired_ref, col_ref, row_ref, out_ref):
            _, _, middle, _, seg = self.roles()
            for at in range(2 * self.quads):
                theirs = middle & (seg - 1 != at // self.quads)
                out_ref[at] = jnp.where(theirs, paired_ref[at], lines_ref[at])
            out_ref[2 * self.quads] = col_ref[self.quads] + row_ref[self.quads]

        return pl.pallas_call(
            kernel,
            in_specs=[vmem] * 4,
            out_specs=vmem,
            out_shape=jax.ShapeDtypeStruct((self.span, *parts[0].shape[1:]), jnp.bfloat16),
            compiler_params=pltpu.CompilerParams(vmem_limit_bytes=VMEM_LIMIT),
            name="lines",
        )(*parts)

    def owner(self, s, k):
        far = jnp.where(k >= 2, 1, 0)
        return jnp.where(s < 2, 2 * far + s, 2 * (s - 2) + far)

    def me(self):
        row_pos, col_pos = self.place()
        return jnp.where(row_pos > 0, 2, 0) + jnp.where(col_pos > 0, 1, 0)

    def strip_cell(self, g, s, at):
        _, corner, _, side, _ = self.roles()
        k = at // RB
        at_corner = (self.me() ^ self.owner(s, k)) * self.span + (s // 2) * self.quads
        at_middle = (side ^ s) * self.span + (k - 1) * self.quads
        return (jnp.where(corner, at_corner, at_middle) + g // GROUP, (g % GROUP) * 32)

    def near_cell(self, edge, face):
        row_pos, col_pos = self.place()
        px_end, _, _, _, seg = self.roles()
        paired = 4 * self.span + (seg - 1) * self.quads
        near_col = 4 * self.span + 2 * self.quads
        near_row = near_col + self.quads + 1
        by_col = jnp.where(row_pos % 2 == 3 - edge, near_col, paired)
        rest = jnp.where(px_end, paired, self.span)
        by_row = jnp.where(col_pos % 2 == 1 - edge, near_row, rest)
        return jnp.where(edge < 2, by_row, by_col) + face // GROUP

    def corner_cell(self, g, s, at):
        _, corner, _, side, seg = self.roles()
        k, hi = (at // RB, jnp.where(at % RB == 0, 0, 1))
        end = (k == 0) | (k == 3)
        line_tile, line_lane = self.strip_cell(g, s, at)
        owner = self.owner(s, k)
        source = self.me() ^ owner
        half = jnp.where(s < 2, 0, HALF)
        for j in range(4):
            their_side = side ^ j
            their_seg = seg if j in (0, 3) else 3 - seg
            hit = jnp.logical_not(corner) & (self.owner(their_side, their_seg) == owner)
            source = jnp.where(hit, j, source)
            half = jnp.where(hit, jnp.where(their_side < 2, 0, HALF), half)
        q = jnp.where(s < 2, 2 * s + hi, s - 2 + 2 * hi)
        in_line = (corner & end) | jnp.logical_not(corner | end)
        tile = jnp.where(in_line, line_tile, source * self.span + 2 * self.quads)
        return (tile, jnp.where(in_line, line_lane + at % RB, half + g * 4 + q))

    def diagonal_cell(self, face, q, px, py):
        row_pos, col_pos = self.place()
        far = jnp.where(px == (row_pos ^ 1), 0, 1) + jnp.where(py == (col_pos ^ 1), 0, 2)
        return (4 * self.span + 4 * self.quads + 2 + far, face * 4 + q)


class GatheredHalo(Place):
    counts = (1, 1, 1, 1, 2)

    extras = (None,) * 5

    def __init__(self, quads, px_count, py_count, col_len):
        self.quads = quads
        self.size = (px_count, py_count)
        self.col_len = col_len

    def chosen_sides(self):
        row_pos, col_pos = self.place()
        return [0, 1, 2, 3, jnp.where(col_pos == 0, 0, 1), jnp.where(row_pos == 0, 2, 3)]

    def exchange(self, table, top, bottom, left, right, lines, corner):
        px_count, py_count = self.size
        up = lambda n: [(i, i + 1) for i in range(n - 1)]
        down = lambda n: [(i + 1, i) for i in range(n - 1)]
        return [
            lax.ppermute(bottom, "py", up(py_count)),
            lax.ppermute(top, "py", down(py_count)),
            lax.ppermute(right, "px", up(px_count)),
            lax.ppermute(left, "px", down(px_count)),
            lax.all_gather(lines, ("px", "py"), axis=0, tiled=True),
            lax.all_gather(corner, ("px", "py"), axis=0, tiled=True),
        ]

    def strip_cell(self, g, s, at):
        px_count, py_count = self.size
        length = jnp.where(s < 2, RB, self.col_len)
        seg = at // length
        px = jnp.where(s < 2, seg, (s - 2) * (px_count - 1))
        py = jnp.where(s < 2, s * (py_count - 1), seg)
        tile = (4 + (px * py_count + py) * 2 + s // 2) * self.quads + g // GROUP
        return (tile, (g % GROUP) * 32 + at % length)

    def near_cell(self, edge, face):
        return edge * self.quads + face // GROUP

    def corner_cell(self, g, s, at):
        return self.strip_cell(g, s, at)

    def diagonal_cell(self, face, q, px, py):
        px_count, py_count = self.size
        base = (4 + 2 * px_count * py_count) * self.quads
        return (base + px * py_count + py, face * 4 + q)


def local(features, cotangent, weight, edge_table, corner_table):
    chan, faces = features.shape[:2]
    tile = features.shape[4]
    col_len = tile // RB
    unit = min(RB, col_len)
    units = (RB // unit, RB // unit, col_len // unit, col_len // unit)
    px_count, py_count, ch_count = [lax.axis_size(name) for name in ("px", "py", "ch")]
    ring = jnp.asarray(ring_matrix(col_len), jnp.bfloat16)
    cornsel = jnp.asarray(corner_matrix(), jnp.bfloat16)
    spread = jnp.asarray(spread_matrix(col_len), jnp.bfloat16)
    rev = jnp.asarray(reverse_matrix(unit), jnp.bfloat16)
    if px_count == py_count == 4 and col_len == RB and 4 * faces <= HALF:
        plan = SquareHalo(faces // GROUP)
    else:
        plan = GatheredHalo(faces // GROUP, px_count, py_count, col_len)

    feats = jnp.transpose(features.reshape(chan, faces, tile), (1, 0, 2))
    cot = jnp.transpose(cotangent.reshape(chan, faces, tile), (1, 0, 2))
    fields = from_others(feats, ch_count)
    parts = rings_of(feats, plan, ring, cornsel)
    table, taps, back_taps = setup(
        plan, edge_table, corner_table, weight, chan, (px_count, py_count), col_len, unit
    )
    tiles = plan.exchange(table, *parts)
    halo = assemble_halo(table, tiles, rev, faces, units, unit)
    halos = from_others(halo, ch_count)
    old, chunks, first = ([], [], 0)
    for count in CALLS:
        act, gated, *parts = forward(
            first, count, plan, fields, halos, cot, taps, spread, ring, cornsel, old
        )
        old = [*parts, act]
        chunks.append((first, from_others(gated, ch_count)))
        first += count

    tiles = plan.exchange(table, *parts)
    halo = assemble_halo(table, tiles, rev, faces, units, unit)
    halos = from_others(halo, ch_count)
    grad = None
    for first, fields in chunks:
        grad = backward(first, faces, fields, halos, back_taps, spread, grad)

    shape = (chan, faces, 1, 1, tile)
    return (
        jnp.transpose(act, (1, 0, 2)).reshape(shape),
        jnp.transpose(grad, (1, 0, 2)).reshape(shape),
    )


def solution(mesh):
    spec = P("ch", None, "py", "px", None)
    return jax.shard_map(
        local,
        mesh=mesh,
        in_specs=(spec, spec, P(), P(), P()),
        out_specs=(spec, spec),
        check_vma=False,
    )
```

```python
import jax
import jax.numpy as jnp
import numpy as np
from jax import lax
from jax.experimental import pallas as pl
from jax.experimental.pallas import tpu as pltpu
from jax.sharding import PartitionSpec as P

RB = 32
GROUP = 4
LANES = 128
CALLS = (3,)
VMEM_LIMIT = 60 * 1024 * 1024
STRIP_LANE = (96, 0, 32, 64)


def ring_matrix(col_len):
    mat = np.zeros((col_len * RB, LANES), np.float32)
    for b in range(RB):
        mat[b, b] = 1
        mat[(col_len - 1) * RB + b, 32 + b] = 1
    for a in range(col_len):
        mat[a * RB, 64 + a] = 1
        mat[a * RB + RB - 1, 96 + a] = 1
    return mat


def corner_matrix():
    mat = np.zeros((LANES, LANES), np.float32)
    for q, lane in enumerate((0, RB - 1, 32, 32 + RB - 1)):
        mat[lane, q] = 1
    return mat


def reverse_matrix(unit):
    mat = np.zeros((LANES, LANES), np.float32)
    for lane in range(LANES):
        mat[lane, (lane // unit) * unit + unit - 1 - lane % unit] = 1
    return mat


def spread_matrix(col_len):
    width = col_len * RB + LANES
    mat = np.zeros((LANES, width), np.float32)
    top, bottom = (col_len + 3) * RB, col_len * RB
    mat[0, top] = 1
    mat[1, top + RB - 1] = 1
    mat[2, bottom] = 1
    mat[3, bottom + RB - 1] = 1
    for a in range(col_len):
        mat[STRIP_LANE[2] + a, a * RB] = 1
        mat[STRIP_LANE[3] + a, a * RB + RB - 1] = 1
    return mat


def lane_iota(shape):
    return lax.broadcasted_iota(jnp.int32, shape, len(shape) - 1)


def side_tiles(fields, first_face, ring_ref, cornsel_ref):
    chan = fields.shape[0] // GROUP
    lane = lane_iota((chan, LANES))
    flat = jnp.dot(fields, ring_ref[...], preferred_element_type=jnp.float32)
    picked = jnp.dot(
        flat.astype(jnp.bfloat16), cornsel_ref[...], preferred_element_type=jnp.float32
    )
    rings = [flat[g * chan : (g + 1) * chan] for g in range(GROUP)]
    tiles = []
    for side in range(4):
        tile = jnp.zeros((chan, LANES), jnp.float32)
        for g, ring in enumerate(rings):
            moved = pltpu.roll(ring, ((g - side) * 32) % LANES, 1) if g != side else ring
            tile = jnp.where(lane // 32 == g, moved, tile)
        tiles.append(tile.astype(jnp.bfloat16))
    corners = jnp.zeros((chan, LANES), jnp.float32)
    for g in range(GROUP):
        corners += pltpu.roll(picked[g * chan : (g + 1) * chan], (first_face + g) * 4, 1)
    return (tiles, corners)


def hand_out(plan, steps, packs, corners, outs):
    chosen = iter(plan.chosen_sides())
    for out in outs[:-1]:
        for at in range(0, out.shape[0], steps):
            base = next(chosen) * steps
            for q in range(steps):
                out[at + q] = packs[base + q]
    packed = plan.pack_corners(corners).astype(jnp.bfloat16)
    for copy in range(outs[-1].shape[0]):
        outs[-1][copy] = packed


def ring_outs(faces, chan, plan):
    steps = faces // GROUP
    shapes = [(count * steps, chan, LANES) for count in plan.counts] + [plan.corner_shape(chan)]
    return [jax.ShapeDtypeStruct(shape, jnp.bfloat16) for shape in shapes]


def rings_kernel(steps, plan, field_ref, ring_ref, cornsel_ref, *refs):
    outs, (packs, corner_acc) = (refs[:-2], refs[-2:])
    step = pl.program_id(0)
    fields = field_ref[...].reshape(-1, field_ref.shape[2])
    tiles, corners = side_tiles(fields, step * GROUP, ring_ref, cornsel_ref)
    for side, tile in enumerate(tiles):
        packs[side * steps + step] = tile

    @pl.when(step == 0)
    def _():
        corner_acc[...] = jnp.zeros_like(corner_acc)

    corner_acc[...] += corners

    @pl.when(step == steps - 1)
    def _():
        hand_out(plan, steps, packs, corner_acc[...], outs)


def whole_spec(array):
    zeros = (0,) * array.ndim
    return pl.BlockSpec(array.shape, lambda *_: zeros)


def rings_of(field, plan, ring, cornsel):
    faces, chan, tile = field.shape
    steps = faces // GROUP
    outs = ring_outs(faces, chan, plan)
    return pl.pallas_call(
        lambda *refs: rings_kernel(steps, plan, *refs),
        grid=(steps,),
        in_specs=[
            pl.BlockSpec((GROUP, chan, tile), lambda i: (i, 0, 0)),
            whole_spec(ring),
            whole_spec(cornsel),
        ],
        out_specs=[whole_spec(out) for out in outs],
        out_shape=outs,
        scratch_shapes=[
            pltpu.VMEM((4 * steps, chan, LANES), jnp.bfloat16),
            pltpu.VMEM((chan, LANES), jnp.float32),
        ],
        compiler_params=pltpu.CompilerParams(vmem_limit_bytes=VMEM_LIMIT),
        name="rings",
    )(field, ring, cornsel)


def halo_kernel(faces, units, unit, plan, *refs):
    table, tile_refs, (rev_ref, halo_ref, pool, turn_acc) = (refs[0], refs[1:-4], refs[-4:])
    chan = halo_ref.shape[1]
    lane = lane_iota((chan, LANES))
    at = 0
    for ref in tile_refs[:-1]:
        pool[at : at + ref.shape[0]] = ref[...]
        at += ref.shape[0]
    for k in range(tile_refs[-1].shape[0]):
        pool[at + k] = plan.unpack_corners(tile_refs[-1][k])
    corner_tile = jnp.zeros((chan, LANES), jnp.float32)
    most = max(units)
    rows = 4 * most
    for f in range(faces):
        tile = jnp.zeros((chan, LANES), jnp.float32)
        turned = jnp.zeros((chan, LANES), jnp.float32)
        for e in range(4):
            for un in range(units[e]):
                base = STRIP_LANE[e] + un * unit
                span = (lane >= base) & (lane < base + unit)
                entry = e * most + un
                source = pool[table[entry, f]].astype(jnp.float32)
                moved = pltpu.roll(source, table[rows + entry, f], 1)
                flip = table[2 * rows + entry, f] == 1
                tile = jnp.where(span & jnp.logical_not(flip), moved, tile)
                turned = jnp.where(span & flip, moved, turned)
        halo_ref[f] = tile.astype(jnp.bfloat16)
        turn_acc[f] = turned.astype(jnp.bfloat16)
        for c in range(4):
            source = pool[table[3 * rows + c, f]].astype(jnp.float32)
            moved = pltpu.roll(source, table[3 * rows + 4 + c, f], 1)
            corner_tile = jnp.where(lane == f * 4 + c, moved, corner_tile)
    turned = jnp.dot(
        turn_acc[...].reshape(faces * chan, LANES), rev_ref[...], preferred_element_type=jnp.float32
    ).reshape(faces, chan, LANES)
    for f in range(faces):
        halo_ref[f] += turned[f].astype(jnp.bfloat16)
    halo_ref[faces] = corner_tile.astype(jnp.bfloat16)


def assemble_halo(plan, table, tiles, rev, faces, units, unit):
    chan = tiles[0].shape[1]
    halo = jax.ShapeDtypeStruct((faces + 1, chan, LANES), jnp.bfloat16)
    vmem = pl.BlockSpec(memory_space=pltpu.VMEM)
    smem = pl.BlockSpec(memory_space=pltpu.SMEM)
    return pl.pallas_call(
        lambda *refs: halo_kernel(faces, units, unit, plan, *refs),
        in_specs=[smem] + [vmem] * (len(tiles) + 1),
        out_specs=vmem,
        out_shape=halo,
        scratch_shapes=[
            pltpu.VMEM((sum(t.shape[0] for t in tiles), chan, LANES), jnp.bfloat16),
            pltpu.VMEM((faces, chan, LANES), jnp.bfloat16),
        ],
        compiler_params=pltpu.CompilerParams(vmem_limit_bytes=VMEM_LIMIT),
        name="halo",
    )(table, *tiles, rev)


def sides_of(step, halo_refs, corner_refs, spread_ref, beside_ref):
    corners = jnp.concatenate([ref[0].astype(jnp.float32) for ref in corner_refs], axis=0)
    lane = lane_iota(corners.shape)
    sides = []
    for g in range(GROUP):
        halo = jnp.concatenate([ref[g].astype(jnp.float32) for ref in halo_refs], axis=0)
        moved = pltpu.roll(corners, (LANES - (step * GROUP + g) * 4) % LANES, 1)
        sides.append(jnp.where(lane < 4, moved, halo).astype(jnp.bfloat16))
    beside = jnp.dot(
        jnp.concatenate(sides, axis=0), spread_ref[...], preferred_element_type=jnp.float32
    )
    beside_ref[...] = beside.astype(jnp.bfloat16).reshape(beside_ref.shape)


def conv_face(g, field_refs, halo_refs, taps_ref, beside_ref, stack_ref):
    chan, tile = field_refs[0].shape[1:]
    total = chan * len(field_refs)
    width = tile + LANES
    for k, (field, halo) in enumerate(zip(field_refs, halo_refs)):
        stack_ref[total + k * chan : total + (k + 1) * chan, :tile] = field[g]
        stack_ref[total + k * chan : total + (k + 1) * chan, tile:] = halo[g]
    middle = stack_ref[total : 2 * total]
    beside = beside_ref[g]
    col = lane_iota((total, width)) % RB
    stack_ref[:total] = jnp.where(col == 0, beside, pltpu.roll(middle, 1, 1))
    stack_ref[2 * total :] = jnp.where(col == RB - 1, beside, pltpu.roll(middle, width - 1, 1))
    sums = jnp.dot(taps_ref[...], stack_ref[...], preferred_element_type=jnp.float32)
    above = pltpu.roll(sums[:chan], RB, 1)
    below = pltpu.roll(sums[2 * chan :], width - RB, 1)
    return (above + sums[chan : 2 * chan] + below)[:, :tile]


def split_refs(refs, *counts):
    out = []
    for count in counts:
        out.append(refs[:count])
        refs = refs[count:]
    return (*out, refs)


def forward_kernel(first, count, steps, pieces, plan, *refs):
    olds = 3 if first else 0
    fields, halos, corners, consts, old, refs = split_refs(refs, pieces, pieces, pieces, 5, olds)
    cot_ref, taps_ref, spread_ref, ring_ref, cornsel_ref = consts
    outs, (packs, corner_acc, made, beside_ref, stacks) = (refs[:-5], refs[-5:])
    act_ref, gated_ref = outs[:2]
    here = pl.program_id(0)
    step = first + here

    @pl.when(here == 0)
    def _():
        if first:
            packs[...] = old[0][...]
            corner_acc[...] = old[1][0].astype(jnp.float32)
        else:
            corner_acc[...] = jnp.zeros_like(corner_acc)

    sides_of(step, halos, corners, spread_ref, beside_ref)
    chan = act_ref.shape[1]
    for g in range(GROUP):
        pre = conv_face(g, fields, halos, taps_ref, beside_ref, stacks.at[g % 2])
        sig = 1.0 / (1.0 + jnp.exp(-pre))
        act_ref[g] = (pre * sig).astype(jnp.bfloat16)
        gated = cot_ref[g].astype(jnp.float32) * sig * (1.0 + pre * (1.0 - sig))
        gated_ref[g] = gated.astype(jnp.bfloat16)
        made[g * chan : (g + 1) * chan] = gated.astype(jnp.bfloat16)
    tiles, corner = side_tiles(made[...], step * GROUP, ring_ref, cornsel_ref)
    for side, tile in enumerate(tiles):
        packs[side * steps + step] = tile
    corner_acc[...] += corner

    @pl.when(here == count - 1)
    def _():
        if first + count == steps:
            hand_out(plan, steps, packs, corner_acc[...], outs[2:])
        else:
            outs[2][...] = packs[...]
            outs[3][0] = corner_acc[...].astype(jnp.bfloat16)


def conv_specs(fields, halos, first, field_first):
    _, chan, tile = fields[0].shape
    last = halos[0].shape[0] - 1
    return (
        [pl.BlockSpec((GROUP, chan, tile), lambda i: (field_first + i, 0, 0)) for _ in fields]
        + [pl.BlockSpec((GROUP, chan, LANES), lambda i: (first + i, 0, 0)) for _ in halos]
        + [pl.BlockSpec((1, chan, LANES), lambda i: (last, 0, 0)) for _ in halos]
    )


def conv_scratch(chan, pieces, tile):
    total = chan * pieces
    return [
        pltpu.VMEM((GROUP, total, tile + LANES), jnp.bfloat16),
        pltpu.VMEM((2, 3 * total, tile + LANES), jnp.bfloat16),
    ]


def forward(first, count, plan, fields, halos, cot, taps, spread, ring, cornsel, old):
    faces, chan, tile = fields[0].shape
    steps = faces // GROUP
    pieces = len(fields)
    if first + count < steps:
        outs = [
            jax.ShapeDtypeStruct((4 * steps, chan, LANES), jnp.bfloat16),
            jax.ShapeDtypeStruct((1, chan, LANES), jnp.bfloat16),
        ]
    else:
        outs = ring_outs(faces, chan, plan)
    whole = jax.ShapeDtypeStruct((faces, chan, tile), jnp.bfloat16)
    chunk = jax.ShapeDtypeStruct((count * GROUP, chan, tile), jnp.bfloat16)
    block = pl.BlockSpec((GROUP, chan, tile), lambda i: (first + i, 0, 0))
    args = [*fields, *halos, *halos, cot, taps, spread, ring, cornsel, *old]
    return pl.pallas_call(
        lambda *refs: forward_kernel(first, count, steps, pieces, plan, *refs),
        grid=(count,),
        in_specs=conv_specs(fields, halos, first, first)
        + [block, whole_spec(taps), whole_spec(spread), whole_spec(ring), whole_spec(cornsel)]
        + [whole_spec(array) for array in old[:2]]
        + [pl.BlockSpec(memory_space=pl.ANY) for _ in old[2:]],
        out_specs=[block, pl.BlockSpec((GROUP, chan, tile), lambda i: (i, 0, 0))]
        + [whole_spec(o) for o in outs],
        out_shape=[whole, chunk] + outs,
        input_output_aliases={len(args) - 1: 0} if old else {},
        scratch_shapes=[
            pltpu.VMEM((4 * steps, chan, LANES), jnp.bfloat16),
            pltpu.VMEM((chan, LANES), jnp.float32),
            pltpu.VMEM((GROUP * chan, tile), jnp.bfloat16),
        ]
        + conv_scratch(chan, pieces, tile),
        compiler_params=pltpu.CompilerParams(vmem_limit_bytes=VMEM_LIMIT),
        name="forward",
    )(*args)


def backward_kernel(first, pieces, *refs):
    fields, halos, corners, consts, refs = split_refs(refs, pieces, pieces, pieces, 2)
    taps_ref, spread_ref = consts
    grad_ref, beside_ref, stacks = refs[-3:]
    sides_of(first + pl.program_id(0), halos, corners, spread_ref, beside_ref)
    for g in range(GROUP):
        total = conv_face(g, fields, halos, taps_ref, beside_ref, stacks.at[g % 2])
        grad_ref[g] = total.astype(jnp.bfloat16)


def backward(first, faces, fields, halos, taps, spread, grad):
    held, chan, tile = fields[0].shape
    pieces = len(fields)
    aside = [] if grad is None else [grad]
    args = [*fields, *halos, *halos, taps, spread, *aside]
    return pl.pallas_call(
        lambda *refs: backward_kernel(first, pieces, *refs),
        grid=(held // GROUP,),
        in_specs=conv_specs(fields, halos, first, 0)
        + [whole_spec(taps), whole_spec(spread)]
        + [pl.BlockSpec(memory_space=pl.ANY) for _ in aside],
        out_specs=pl.BlockSpec((GROUP, chan, tile), lambda i: (first + i, 0, 0)),
        out_shape=jax.ShapeDtypeStruct((faces, chan, tile), jnp.bfloat16),
        input_output_aliases={len(args) - 1: 0} if aside else {},
        scratch_shapes=conv_scratch(chan, pieces, tile),
        compiler_params=pltpu.CompilerParams(vmem_limit_bytes=VMEM_LIMIT),
        name="backward",
    )(*args)


def rows_of(*parts):
    return jnp.concatenate(parts, axis=0)


def halo_table(plan, edge_ref, corner_ref, px_count, py_count, col_len, unit):
    row_pos, col_pos = plan.place()
    faces = edge_ref.shape[2]
    side_len = px_count * RB
    most = RB // unit
    shape = (4 * most, faces)
    face = lane_iota(shape)
    row = lax.broadcasted_iota(jnp.int32, shape, 0)
    edge, un = (row // most, row % most)
    g, s, r = [
        rows_of(*[edge_ref[i, e : e + 1] for e in range(4) for _ in range(most)]) for i in range(3)
    ]
    border = ((edge == 0) & (col_pos == 0)) | ((edge == 1) & (col_pos == py_count - 1))
    border |= ((edge == 2) & (row_pos == 0)) | ((edge == 3) & (row_pos == px_count - 1))
    at = jnp.where(edge < 2, row_pos * RB, col_pos * col_len) + un * unit
    at = jnp.clip(at, 0, side_len - unit)
    at = jnp.where(r == 1, side_len - unit - at, at)
    line_tile, line_lane = plan.strip_cell(g, s, at)
    tile = jnp.where(border, line_tile, plan.near_cell(edge, face))
    lane = jnp.where(border, line_lane, (face % GROUP) * 32 + un * unit)
    first = jnp.where(edge == 0, STRIP_LANE[0], jnp.where(edge == 1, STRIP_LANE[1], edge * 32 - 32))
    shift = (first + un * unit - lane + LANES) % LANES
    flip = jnp.where(border & (r == 1), 1, 0)

    shape = (4, faces)
    face = lane_iota(shape)
    c = lax.broadcasted_iota(jnp.int32, shape, 0)
    down, right = (c // 2, c % 2)
    row_on = ((down == 0) & (col_pos == 0)) | ((down == 1) & (col_pos == py_count - 1))
    col_on = ((right == 0) & (row_pos == 0)) | ((right == 1) & (row_pos == px_count - 1))
    row_at = row_pos * RB + jnp.where(right == 1, RB, -1)
    col_at = col_pos * col_len + jnp.where(down == 1, col_len, -1)
    edge_of = lambda i, edges: rows_of(*[edge_ref[i, e : e + 1] for e in edges])
    g, s, r = [
        jnp.where(row_on, edge_of(i, (0, 0, 1, 1)), edge_of(i, (2, 3, 2, 3))) for i in range(3)
    ]
    at = jnp.clip(jnp.where(row_on, row_at, col_at), 0, side_len - 1)
    at = jnp.where(r == 1, side_len - 1 - at, at)
    h, q = [rows_of(*[corner_ref[k, i : i + 1] for k in range(4)]) for i in range(2)]
    both = row_on & col_on
    g = jnp.where(both, h, g)
    s = jnp.where(both, q // 2, s)
    at = jnp.where(both, (q % 2) * (side_len - 1), at)
    line_tile, line_lane = plan.corner_cell(g, s, at)
    diag_px = jnp.clip(row_pos + 2 * right - 1, 0, px_count - 1)
    diag_py = jnp.clip(col_pos + 2 * down - 1, 0, py_count - 1)
    diag_tile, diag_lane = plan.diagonal_cell(face, 3 - c, diag_px, diag_py)
    on = row_on | col_on
    corner_at = jnp.where(on, line_tile, diag_tile)
    corner_lane = jnp.where(on, line_lane, diag_lane)
    corner_shift = (face * 4 + c - corner_lane + LANES) % LANES
    return rows_of(tile, shift, flip, corner_at, corner_shift)


def setup_kernel(plan, chan, shape, edge_ref, corner_ref, weight_ref, table_ref, taps_ref, back_ref, turn):
    table_ref[...] = halo_table(plan, edge_ref, corner_ref, *shape)
    total = weight_ref.shape[2]
    own = lax.axis_index("ch") * chan
    shift = (total - own) % total
    for i in range(3):
        for j in range(3):
            turn[...] = weight_ref[i, j].astype(jnp.float32)
            rows = pltpu.roll(turn[pl.ds(pl.multiple_of(own, chan), chan)], shift, 1)
            cols = slice(j * total, (j + 1) * total)
            taps_ref[i * chan : (i + 1) * chan, cols] = rows.astype(jnp.bfloat16)
            turn[...] = turn[...].T
            rows = pltpu.roll(turn[pl.ds(pl.multiple_of(own, chan), chan)], shift, 1)
            cols = slice((2 - j) * total, (3 - j) * total)
            back_ref[(2 - i) * chan : (3 - i) * chan, cols] = rows.astype(jnp.bfloat16)


def setup(plan, edge_table, corner_table, weight, chan, counts, col_len, unit):
    edges = jnp.transpose(edge_table, (2, 1, 0))
    corners = jnp.transpose(corner_table, (1, 2, 0))
    total = weight.shape[2]
    vmem = pl.BlockSpec(memory_space=pltpu.VMEM)
    taps = jax.ShapeDtypeStruct((3 * chan, 3 * total), jnp.bfloat16)
    table = jax.ShapeDtypeStruct((12 * (RB // unit) + 8, edges.shape[2]), jnp.int32)
    return pl.pallas_call(
        lambda *refs: setup_kernel(plan, chan, (*counts, col_len, unit), *refs),
        in_specs=[vmem] * 3,
        out_specs=[vmem] * 3,
        out_shape=[table, taps, taps],
        scratch_shapes=[pltpu.VMEM((total, total), jnp.float32)],
        compiler_params=pltpu.CompilerParams(vmem_limit_bytes=VMEM_LIMIT),
        name="setup",
    )(edges, corners, weight)


def from_others(array, ch_count):
    return [array] + [
        lax.ppermute(array, "ch", [((i + k) % ch_count, i) for i in range(ch_count)])
        for k in range(1, ch_count)
    ]


class Place:
    @staticmethod
    def place():
        return (lax.axis_index("px"), lax.axis_index("py"))


class SquareHalo(Place):
    counts = (2, 1, 1, 2)

    def __init__(self, quads):
        self.quads = quads

    def corner_shape(self, chan):
        return (16, chan // 2, LANES)

    def pack_corners(self, corners):
        half = corners.shape[0] // 2
        return corners[:half] + pltpu.roll(corners[half:], LANES // 2, 1)

    def unpack_corners(self, packed):
        upper = packed.astype(jnp.float32)
        both = jnp.concatenate([upper, pltpu.roll(upper, LANES // 2, 1)], axis=0)
        return both.astype(jnp.bfloat16)

    def roles(self):
        row_pos, col_pos = self.place()
        px_end = (row_pos == 0) | (row_pos == 3)
        py_end = (col_pos == 0) | (col_pos == 3)
        side = jnp.where(
            py_end, jnp.where(col_pos == 0, 0, 1), jnp.where(row_pos == 0, 2, 3)
        )
        corner = px_end & py_end
        middle = (px_end | py_end) & jnp.logical_not(corner)
        return (px_end, corner, middle, side, jnp.where(px_end, col_pos, row_pos))

    def chosen_sides(self):
        row_pos, col_pos = self.place()
        px_end, corner, middle, side, seg = self.roles()
        row_line = jnp.where(col_pos == 0, 0, 1)
        col_line = jnp.where(row_pos == 0, 2, 3)
        to_px, to_py = (jnp.where(row_pos == 1, 3, 2), jnp.where(col_pos == 1, 1, 0))
        facing = jnp.where(px_end, to_py, to_px)
        return [
            jnp.where(seg == 1, side, facing),
            jnp.where(seg == 1, facing, side),
            jnp.where(row_pos % 2 == 0, 3, 2),
            jnp.where(col_pos % 2 == 0, 1, 0),
            jnp.where(corner, row_line, jnp.where(middle, side, to_py)),
            jnp.where(corner, col_line, side),
        ]

    def exchange(self, pair, col_side, row_side, lines, corner):
        every = [(x, y) for x in range(4) for y in range(4)]
        axes = ("px", "py")
        swap = lambda array, pairs: lax.ppermute(
            array, axes, [(a[0] * 4 + a[1], b[0] * 4 + b[1]) for a, b in pairs]
        )
        ends = (0, 3)
        corners = [(x, y) for x in ends for y in ends]
        spot = lambda side, seg: ((seg, 0), (seg, 3), (0, seg), (3, seg))[side]
        beside = [(spot(side, k), spot(side, 3 - k)) for side in range(4) for k in (1, 2)]
        beside += [((x, y), (3 - x, y)) for x in (1, 2) for y in (1, 2)]
        paired = swap(pair, beside)
        near_col = swap(col_side, [((x, y), (x ^ 1, y)) for x, y in every])
        near_row = swap(row_side, [((x, y), (x, y ^ 1)) for x, y in every])
        _, _, middle, _, seg = self.roles()
        slot = lax.broadcasted_iota(jnp.int32, (2 * self.quads, 1, 1), 0) // self.quads
        lines = jnp.where(middle & (slot != seg - 1), paired, lines)
        across = []
        for j in (1, 2, 3):
            pairs = [(spot(side, k), spot(side ^ j, k)) for side in range(4) for k in (1, 2)]
            pairs += [(corners[c], corners[c ^ j]) for c in range(4)]
            if j == 1:
                pairs += [((x, y), (x, 3 - y)) for x in (1, 2) for y in (1, 2)]
            across.append(swap(lines, pairs))
        ends_of = lax.all_to_all(corner, axes, 0, 0, tiled=True)
        return [lines, *across, paired, near_col, near_row, ends_of]

    def strip_cell(self, g, s, at):
        row_pos, col_pos = self.place()
        _, corner, _, side, _ = self.roles()
        slot = 2 * self.quads
        k = at // RB
        me = jnp.where(row_pos > 0, 2, 0) + jnp.where(col_pos > 0, 1, 0)
        far = jnp.where(k > 0, 1, 0)
        owner = jnp.where(s < 2, 2 * far + s, 2 * (s - 2) + far)
        at_corner = (me ^ owner) * slot + (s // 2) * self.quads
        at_middle = (side ^ s) * slot + (k - 1) * self.quads
        return (jnp.where(corner, at_corner, at_middle) + g // GROUP, (g % GROUP) * 32)

    def near_cell(self, edge, face):
        row_pos, col_pos = self.place()
        px_end, _, _, _, seg = self.roles()
        slot = 2 * self.quads
        paired = 4 * slot + (seg - 1) * self.quads
        near_col, near_row = (5 * slot, 5 * slot + self.quads)
        by_col = jnp.where(row_pos % 2 == 3 - edge, near_col, paired)
        by_row = jnp.where(col_pos % 2 == 1 - edge, near_row, jnp.where(px_end, paired, slot))
        return jnp.where(edge < 2, by_row, by_col) + face // GROUP

    def corner_cell(self, g, s, at):
        seg, hi = (at // RB, jnp.where(at % RB == 0, 0, 1))
        owner = jnp.where(s < 2, seg * 4 + 3 * s, 12 * (s - 2) + seg)
        q = jnp.where(s < 2, 2 * s + hi, s - 2 + 2 * hi)
        return (12 * self.quads + owner, g * 4 + q)

    def diagonal_cell(self, face, q, px, py):
        return (12 * self.quads + px * 4 + py, face * 4 + q)


class GatheredHalo(Place):
    counts = (1, 1, 1, 1, 2)

    def corner_shape(self, chan):
        return (1, chan, LANES)

    def pack_corners(self, corners):
        return corners

    def unpack_corners(self, packed):
        return packed

    def __init__(self, quads, px_count, py_count, col_len):
        self.quads = quads
        self.size = (px_count, py_count)
        self.col_len = col_len

    def chosen_sides(self):
        row_pos, col_pos = self.place()
        return [0, 1, 2, 3, jnp.where(col_pos == 0, 0, 1), jnp.where(row_pos == 0, 2, 3)]

    def exchange(self, top, bottom, left, right, lines, corner):
        px_count, py_count = self.size
        up = lambda n: [(i, i + 1) for i in range(n - 1)]
        down = lambda n: [(i + 1, i) for i in range(n - 1)]
        return [
            lax.ppermute(bottom, "py", up(py_count)),
            lax.ppermute(top, "py", down(py_count)),
            lax.ppermute(right, "px", up(px_count)),
            lax.ppermute(left, "px", down(px_count)),
            lax.all_gather(lines, ("px", "py"), axis=0, tiled=True),
            lax.all_gather(corner, ("px", "py"), axis=0, tiled=True),
        ]

    def strip_cell(self, g, s, at):
        px_count, py_count = self.size
        length = jnp.where(s < 2, RB, self.col_len)
        seg = at // length
        px = jnp.where(s < 2, seg, (s - 2) * (px_count - 1))
        py = jnp.where(s < 2, s * (py_count - 1), seg)
        tile = (4 + (px * py_count + py) * 2 + s // 2) * self.quads + g // GROUP
        return (tile, (g % GROUP) * 32 + at % length)

    def near_cell(self, edge, face):
        return edge * self.quads + face // GROUP

    def corner_cell(self, g, s, at):
        return self.strip_cell(g, s, at)

    def diagonal_cell(self, face, q, px, py):
        px_count, py_count = self.size
        base = (4 + 2 * px_count * py_count) * self.quads
        return (base + px * py_count + py, face * 4 + q)


def local(features, cotangent, weight, edge_table, corner_table):
    chan, faces = features.shape[:2]
    tile = features.shape[4]
    col_len = tile // RB
    unit = min(RB, col_len)
    units = (RB // unit, RB // unit, col_len // unit, col_len // unit)
    px_count, py_count, ch_count = [lax.axis_size(name) for name in ("px", "py", "ch")]
    ring = jnp.asarray(ring_matrix(col_len), jnp.bfloat16)
    cornsel = jnp.asarray(corner_matrix(), jnp.bfloat16)
    spread = jnp.asarray(spread_matrix(col_len), jnp.bfloat16)
    rev = jnp.asarray(reverse_matrix(unit), jnp.bfloat16)
    if px_count == py_count == 4 and col_len == RB and chan % 32 == 0:
        plan = SquareHalo(faces // GROUP)
    else:
        plan = GatheredHalo(faces // GROUP, px_count, py_count, col_len)

    feats = jnp.transpose(features.reshape(chan, faces, tile), (1, 0, 2))
    cot = jnp.transpose(cotangent.reshape(chan, faces, tile), (1, 0, 2))
    fields = from_others(feats, ch_count)
    parts = rings_of(feats, plan, ring, cornsel)
    table, taps, back_taps = setup(
        plan, edge_table, corner_table, weight, chan, (px_count, py_count), col_len, unit
    )
    tiles = plan.exchange(*parts)
    halo = assemble_halo(plan, table, tiles, rev, faces, units, unit)
    halos = from_others(halo, ch_count)
    old, chunks, first = ([], [], 0)
    for count in CALLS:
        act, gated, *parts = forward(
            first, count, plan, fields, halos, cot, taps, spread, ring, cornsel, old
        )
        old = [*parts, act]
        chunks.append((first, from_others(gated, ch_count)))
        first += count

    tiles = plan.exchange(*parts)
    halo = assemble_halo(plan, table, tiles, rev, faces, units, unit)
    halos = from_others(halo, ch_count)
    grad = None
    for first, fields in chunks:
        grad = backward(first, faces, fields, halos, back_taps, spread, grad)

    shape = (chan, faces, 1, 1, tile)
    return (
        jnp.transpose(act, (1, 0, 2)).reshape(shape),
        jnp.transpose(grad, (1, 0, 2)).reshape(shape),
    )


def solution(mesh):
    spec = P("ch", None, "py", "px", None)
    return jax.shard_map(
        local,
        mesh=mesh,
        in_specs=(spec, spec, P(), P(), P()),
        out_specs=(spec, spec),
        check_vma=False,
    )
```

```python
import jax
import jax.numpy as jnp
import numpy as np
from jax import lax
from jax.experimental import pallas as pl
from jax.experimental.pallas import tpu as pltpu
from jax.sharding import PartitionSpec as P

RB = 32
GROUP = 4
LANES = 128
CALLS = (2, 1)
VMEM_LIMIT = 60 * 1024 * 1024
STRIP_LANE = (96, 0, 32, 64)


def ring_matrix(col_len):
    mat = np.zeros((col_len * RB, LANES), np.float32)
    for b in range(RB):
        mat[b, b] = 1
        mat[(col_len - 1) * RB + b, 32 + b] = 1
    for a in range(col_len):
        mat[a * RB, 64 + a] = 1
        mat[a * RB + RB - 1, 96 + a] = 1
    return mat


def corner_matrix():
    mat = np.zeros((LANES, LANES), np.float32)
    for q, lane in enumerate((0, RB - 1, 32, 32 + RB - 1)):
        mat[lane, q] = 1
    return mat


def reverse_matrix(unit):
    mat = np.zeros((LANES, LANES), np.float32)
    for lane in range(LANES):
        mat[lane, (lane // unit) * unit + unit - 1 - lane % unit] = 1
    return mat


def spread_matrix(col_len):
    width = col_len * RB + LANES
    mat = np.zeros((LANES, width), np.float32)
    top, bottom = (col_len + 3) * RB, col_len * RB
    mat[0, top] = 1
    mat[1, top + RB - 1] = 1
    mat[2, bottom] = 1
    mat[3, bottom + RB - 1] = 1
    for a in range(col_len):
        mat[STRIP_LANE[2] + a, a * RB] = 1
        mat[STRIP_LANE[3] + a, a * RB + RB - 1] = 1
    return mat


def lane_iota(shape):
    return lax.broadcasted_iota(jnp.int32, shape, len(shape) - 1)


def side_tiles(fields, first_face, ring_ref, cornsel_ref):
    chan = fields.shape[0] // GROUP
    lane = lane_iota((chan, LANES))
    flat = jnp.dot(fields, ring_ref[...], preferred_element_type=jnp.float32)
    picked = jnp.dot(
        flat.astype(jnp.bfloat16), cornsel_ref[...], preferred_element_type=jnp.float32
    )
    rings = [flat[g * chan : (g + 1) * chan] for g in range(GROUP)]
    tiles = []
    for side in range(4):
        tile = jnp.zeros((chan, LANES), jnp.float32)
        for g, ring in enumerate(rings):
            moved = pltpu.roll(ring, ((g - side) * 32) % LANES, 1) if g != side else ring
            tile = jnp.where(lane // 32 == g, moved, tile)
        tiles.append(tile.astype(jnp.bfloat16))
    corners = jnp.zeros((chan, LANES), jnp.float32)
    for g in range(GROUP):
        corners += pltpu.roll(picked[g * chan : (g + 1) * chan], (first_face + g) * 4, 1)
    return (tiles, corners)


def hand_out(plan, steps, packs, corners, outs):
    chosen = iter(plan.chosen_sides())
    for out in outs[:-1]:
        for at in range(0, out.shape[0], steps):
            base = next(chosen) * steps
            for q in range(steps):
                out[at + q] = packs[base + q]
    packed = plan.pack_corners(corners).astype(jnp.bfloat16)
    for copy in range(outs[-1].shape[0]):
        outs[-1][copy] = packed


def ring_outs(faces, chan, plan):
    steps = faces // GROUP
    shapes = [(count * steps, chan, LANES) for count in plan.counts] + [plan.corner_shape(chan)]
    return [jax.ShapeDtypeStruct(shape, jnp.bfloat16) for shape in shapes]


def rings_kernel(steps, plan, field_ref, ring_ref, cornsel_ref, *refs):
    outs, (packs, corner_acc) = (refs[:-2], refs[-2:])
    step = pl.program_id(0)
    fields = field_ref[...].reshape(-1, field_ref.shape[2])
    tiles, corners = side_tiles(fields, step * GROUP, ring_ref, cornsel_ref)
    for side, tile in enumerate(tiles):
        packs[side * steps + step] = tile

    @pl.when(step == 0)
    def _():
        corner_acc[...] = jnp.zeros_like(corner_acc)

    corner_acc[...] += corners

    @pl.when(step == steps - 1)
    def _():
        hand_out(plan, steps, packs, corner_acc[...], outs)


def whole_spec(array):
    zeros = (0,) * array.ndim
    return pl.BlockSpec(array.shape, lambda *_: zeros)


def rings_of(field, plan, ring, cornsel):
    faces, chan, tile = field.shape
    steps = faces // GROUP
    outs = ring_outs(faces, chan, plan)
    return pl.pallas_call(
        lambda *refs: rings_kernel(steps, plan, *refs),
        grid=(steps,),
        in_specs=[
            pl.BlockSpec((GROUP, chan, tile), lambda i: (i, 0, 0)),
            whole_spec(ring),
            whole_spec(cornsel),
        ],
        out_specs=[whole_spec(out) for out in outs],
        out_shape=outs,
        scratch_shapes=[
            pltpu.VMEM((4 * steps, chan, LANES), jnp.bfloat16),
            pltpu.VMEM((chan, LANES), jnp.float32),
        ],
        compiler_params=pltpu.CompilerParams(vmem_limit_bytes=VMEM_LIMIT),
        name="rings",
    )(field, ring, cornsel)


def halo_kernel(faces, units, unit, plan, *refs):
    table, tile_refs, (rev_ref, halo_ref, pool, turn_acc) = (refs[0], refs[1:-4], refs[-4:])
    chan = halo_ref.shape[1]
    lane = lane_iota((chan, LANES))
    at = 0
    for ref in tile_refs[:-1]:
        pool[at : at + ref.shape[0]] = ref[...]
        at += ref.shape[0]
    for k in range(tile_refs[-1].shape[0]):
        pool[at + k] = plan.unpack_corners(tile_refs[-1][k])
    corner_tile = jnp.zeros((chan, LANES), jnp.float32)
    most = max(units)
    rows = 4 * most
    for f in range(faces):
        tile = jnp.zeros((chan, LANES), jnp.float32)
        turned = jnp.zeros((chan, LANES), jnp.float32)
        for e in range(4):
            for un in range(units[e]):
                base = STRIP_LANE[e] + un * unit
                span = (lane >= base) & (lane < base + unit)
                entry = e * most + un
                source = pool[table[entry, f]].astype(jnp.float32)
                moved = pltpu.roll(source, table[rows + entry, f], 1)
                flip = table[2 * rows + entry, f] == 1
                tile = jnp.where(span & jnp.logical_not(flip), moved, tile)
                turned = jnp.where(span & flip, moved, turned)
        halo_ref[f] = tile.astype(jnp.bfloat16)
        turn_acc[f] = turned.astype(jnp.bfloat16)
        for c in range(4):
            source = pool[table[3 * rows + c, f]].astype(jnp.float32)
            moved = pltpu.roll(source, table[3 * rows + 4 + c, f], 1)
            corner_tile = jnp.where(lane == f * 4 + c, moved, corner_tile)
    turned = jnp.dot(
        turn_acc[...].reshape(faces * chan, LANES), rev_ref[...], preferred_element_type=jnp.float32
    ).reshape(faces, chan, LANES)
    for f in range(faces):
        halo_ref[f] += turned[f].astype(jnp.bfloat16)
    halo_ref[faces] = corner_tile.astype(jnp.bfloat16)


def assemble_halo(plan, table, tiles, rev, faces, units, unit):
    chan = tiles[0].shape[1]
    halo = jax.ShapeDtypeStruct((faces + 1, chan, LANES), jnp.bfloat16)
    vmem = pl.BlockSpec(memory_space=pltpu.VMEM)
    smem = pl.BlockSpec(memory_space=pltpu.SMEM)
    return pl.pallas_call(
        lambda *refs: halo_kernel(faces, units, unit, plan, *refs),
        in_specs=[smem] + [vmem] * (len(tiles) + 1),
        out_specs=vmem,
        out_shape=halo,
        scratch_shapes=[
            pltpu.VMEM((sum(t.shape[0] for t in tiles), chan, LANES), jnp.bfloat16),
            pltpu.VMEM((faces, chan, LANES), jnp.bfloat16),
        ],
        compiler_params=pltpu.CompilerParams(vmem_limit_bytes=VMEM_LIMIT),
        name="halo",
    )(table, *tiles, rev)


def sides_of(step, halo_refs, corner_refs, spread_ref, beside_ref):
    corners = jnp.concatenate([ref[0].astype(jnp.float32) for ref in corner_refs], axis=0)
    lane = lane_iota(corners.shape)
    sides = []
    for g in range(GROUP):
        halo = jnp.concatenate([ref[g].astype(jnp.float32) for ref in halo_refs], axis=0)
        moved = pltpu.roll(corners, (LANES - (step * GROUP + g) * 4) % LANES, 1)
        sides.append(jnp.where(lane < 4, moved, halo).astype(jnp.bfloat16))
    beside = jnp.dot(
        jnp.concatenate(sides, axis=0), spread_ref[...], preferred_element_type=jnp.float32
    )
    beside_ref[...] = beside.astype(jnp.bfloat16).reshape(beside_ref.shape)


def conv_face(g, field_refs, halo_refs, taps_ref, beside_ref, stack_ref):
    chan, tile = field_refs[0].shape[1:]
    total = chan * len(field_refs)
    width = tile + LANES
    for k, (field, halo) in enumerate(zip(field_refs, halo_refs)):
        stack_ref[total + k * chan : total + (k + 1) * chan, :tile] = field[g]
        stack_ref[total + k * chan : total + (k + 1) * chan, tile:] = halo[g]
    middle = stack_ref[total : 2 * total]
    beside = beside_ref[g]
    col = lane_iota((total, width)) % RB
    stack_ref[:total] = jnp.where(col == 0, beside, pltpu.roll(middle, 1, 1))
    stack_ref[2 * total :] = jnp.where(col == RB - 1, beside, pltpu.roll(middle, width - 1, 1))
    sums = jnp.dot(taps_ref[...], stack_ref[...], preferred_element_type=jnp.float32)
    above = pltpu.roll(sums[:chan], RB, 1)
    below = pltpu.roll(sums[2 * chan :], width - RB, 1)
    return (above + sums[chan : 2 * chan] + below)[:, :tile]


def split_refs(refs, *counts):
    out = []
    for count in counts:
        out.append(refs[:count])
        refs = refs[count:]
    return (*out, refs)


def forward_kernel(first, count, steps, pieces, plan, *refs):
    olds = 3 if first else 0
    fields, halos, corners, consts, old, refs = split_refs(refs, pieces, pieces, pieces, 5, olds)
    cot_ref, taps_ref, spread_ref, ring_ref, cornsel_ref = consts
    outs, (packs, corner_acc, made, beside_ref, stacks) = (refs[:-5], refs[-5:])
    act_ref, gated_ref = outs[:2]
    here = pl.program_id(0)
    step = first + here

    @pl.when(here == 0)
    def _():
        if first:
            packs[...] = old[0][...]
            corner_acc[...] = old[1][0].astype(jnp.float32)
        else:
            corner_acc[...] = jnp.zeros_like(corner_acc)

    sides_of(step, halos, corners, spread_ref, beside_ref)
    chan = act_ref.shape[1]
    for g in range(GROUP):
        pre = conv_face(g, fields, halos, taps_ref, beside_ref, stacks.at[g % 2])
        sig = 1.0 / (1.0 + jnp.exp(-pre))
        act_ref[g] = (pre * sig).astype(jnp.bfloat16)
        gated = cot_ref[g].astype(jnp.float32) * sig * (1.0 + pre * (1.0 - sig))
        gated_ref[g] = gated.astype(jnp.bfloat16)
        made[g * chan : (g + 1) * chan] = gated.astype(jnp.bfloat16)
    tiles, corner = side_tiles(made[...], step * GROUP, ring_ref, cornsel_ref)
    for side, tile in enumerate(tiles):
        packs[side * steps + step] = tile
    corner_acc[...] += corner

    @pl.when(here == count - 1)
    def _():
        if first + count == steps:
            hand_out(plan, steps, packs, corner_acc[...], outs[2:])
        else:
            outs[2][...] = packs[...]
            outs[3][0] = corner_acc[...].astype(jnp.bfloat16)


def conv_specs(fields, halos, first, field_first):
    _, chan, tile = fields[0].shape
    last = halos[0].shape[0] - 1
    return (
        [pl.BlockSpec((GROUP, chan, tile), lambda i: (field_first + i, 0, 0)) for _ in fields]
        + [pl.BlockSpec((GROUP, chan, LANES), lambda i: (first + i, 0, 0)) for _ in halos]
        + [pl.BlockSpec((1, chan, LANES), lambda i: (last, 0, 0)) for _ in halos]
    )


def conv_scratch(chan, pieces, tile):
    total = chan * pieces
    return [
        pltpu.VMEM((GROUP, total, tile + LANES), jnp.bfloat16),
        pltpu.VMEM((2, 3 * total, tile + LANES), jnp.bfloat16),
    ]


def forward(first, count, plan, fields, halos, cot, taps, spread, ring, cornsel, old):
    faces, chan, tile = fields[0].shape
    steps = faces // GROUP
    pieces = len(fields)
    if first + count < steps:
        outs = [
            jax.ShapeDtypeStruct((4 * steps, chan, LANES), jnp.bfloat16),
            jax.ShapeDtypeStruct((1, chan, LANES), jnp.bfloat16),
        ]
    else:
        outs = ring_outs(faces, chan, plan)
    whole = jax.ShapeDtypeStruct((faces, chan, tile), jnp.bfloat16)
    chunk = jax.ShapeDtypeStruct((count * GROUP, chan, tile), jnp.bfloat16)
    block = pl.BlockSpec((GROUP, chan, tile), lambda i: (first + i, 0, 0))
    args = [*fields, *halos, *halos, cot, taps, spread, ring, cornsel, *old]
    return pl.pallas_call(
        lambda *refs: forward_kernel(first, count, steps, pieces, plan, *refs),
        grid=(count,),
        in_specs=conv_specs(fields, halos, first, first)
        + [block, whole_spec(taps), whole_spec(spread), whole_spec(ring), whole_spec(cornsel)]
        + [whole_spec(array) for array in old[:2]]
        + [pl.BlockSpec(memory_space=pl.ANY) for _ in old[2:]],
        out_specs=[block, pl.BlockSpec((GROUP, chan, tile), lambda i: (i, 0, 0))]
        + [whole_spec(o) for o in outs],
        out_shape=[whole, chunk] + outs,
        input_output_aliases={len(args) - 1: 0} if old else {},
        scratch_shapes=[
            pltpu.VMEM((4 * steps, chan, LANES), jnp.bfloat16),
            pltpu.VMEM((chan, LANES), jnp.float32),
            pltpu.VMEM((GROUP * chan, tile), jnp.bfloat16),
        ]
        + conv_scratch(chan, pieces, tile),
        compiler_params=pltpu.CompilerParams(vmem_limit_bytes=VMEM_LIMIT),
        name="forward",
    )(*args)


def backward_kernel(first, pieces, *refs):
    fields, halos, corners, consts, refs = split_refs(refs, pieces, pieces, pieces, 2)
    taps_ref, spread_ref = consts
    grad_ref, beside_ref, stacks = refs[-3:]
    sides_of(first + pl.program_id(0), halos, corners, spread_ref, beside_ref)
    for g in range(GROUP):
        total = conv_face(g, fields, halos, taps_ref, beside_ref, stacks.at[g % 2])
        grad_ref[g] = total.astype(jnp.bfloat16)


def backward(first, faces, fields, halos, taps, spread, grad):
    held, chan, tile = fields[0].shape
    pieces = len(fields)
    aside = [] if grad is None else [grad]
    args = [*fields, *halos, *halos, taps, spread, *aside]
    return pl.pallas_call(
        lambda *refs: backward_kernel(first, pieces, *refs),
        grid=(held // GROUP,),
        in_specs=conv_specs(fields, halos, first, 0)
        + [whole_spec(taps), whole_spec(spread)]
        + [pl.BlockSpec(memory_space=pl.ANY) for _ in aside],
        out_specs=pl.BlockSpec((GROUP, chan, tile), lambda i: (first + i, 0, 0)),
        out_shape=jax.ShapeDtypeStruct((faces, chan, tile), jnp.bfloat16),
        input_output_aliases={len(args) - 1: 0} if aside else {},
        scratch_shapes=conv_scratch(chan, pieces, tile),
        compiler_params=pltpu.CompilerParams(vmem_limit_bytes=VMEM_LIMIT),
        name="backward",
    )(*args)


def rows_of(*parts):
    return jnp.concatenate(parts, axis=0)


def halo_table(plan, edge_ref, corner_ref, px_count, py_count, col_len, unit):
    row_pos, col_pos = plan.place()
    faces = edge_ref.shape[2]
    side_len = px_count * RB
    most = RB // unit
    shape = (4 * most, faces)
    face = lane_iota(shape)
    row = lax.broadcasted_iota(jnp.int32, shape, 0)
    edge, un = (row // most, row % most)
    g, s, r = [
        rows_of(*[edge_ref[i, e : e + 1] for e in range(4) for _ in range(most)]) for i in range(3)
    ]
    border = ((edge == 0) & (col_pos == 0)) | ((edge == 1) & (col_pos == py_count - 1))
    border |= ((edge == 2) & (row_pos == 0)) | ((edge == 3) & (row_pos == px_count - 1))
    at = jnp.where(edge < 2, row_pos * RB, col_pos * col_len) + un * unit
    at = jnp.clip(at, 0, side_len - unit)
    at = jnp.where(r == 1, side_len - unit - at, at)
    line_tile, line_lane = plan.strip_cell(g, s, at)
    tile = jnp.where(border, line_tile, plan.near_cell(edge, face))
    lane = jnp.where(border, line_lane, (face % GROUP) * 32 + un * unit)
    first = jnp.where(edge == 0, STRIP_LANE[0], jnp.where(edge == 1, STRIP_LANE[1], edge * 32 - 32))
    shift = (first + un * unit - lane + LANES) % LANES
    flip = jnp.where(border & (r == 1), 1, 0)

    shape = (4, faces)
    face = lane_iota(shape)
    c = lax.broadcasted_iota(jnp.int32, shape, 0)
    down, right = (c // 2, c % 2)
    row_on = ((down == 0) & (col_pos == 0)) | ((down == 1) & (col_pos == py_count - 1))
    col_on = ((right == 0) & (row_pos == 0)) | ((right == 1) & (row_pos == px_count - 1))
    row_at = row_pos * RB + jnp.where(right == 1, RB, -1)
    col_at = col_pos * col_len + jnp.where(down == 1, col_len, -1)
    edge_of = lambda i, edges: rows_of(*[edge_ref[i, e : e + 1] for e in edges])
    g, s, r = [
        jnp.where(row_on, edge_of(i, (0, 0, 1, 1)), edge_of(i, (2, 3, 2, 3))) for i in range(3)
    ]
    at = jnp.clip(jnp.where(row_on, row_at, col_at), 0, side_len - 1)
    at = jnp.where(r == 1, side_len - 1 - at, at)
    h, q = [rows_of(*[corner_ref[k, i : i + 1] for k in range(4)]) for i in range(2)]
    both = row_on & col_on
    g = jnp.where(both, h, g)
    s = jnp.where(both, q // 2, s)
    at = jnp.where(both, (q % 2) * (side_len - 1), at)
    line_tile, line_lane = plan.corner_cell(g, s, at)
    diag_px = jnp.clip(row_pos + 2 * right - 1, 0, px_count - 1)
    diag_py = jnp.clip(col_pos + 2 * down - 1, 0, py_count - 1)
    diag_tile, diag_lane = plan.diagonal_cell(face, 3 - c, diag_px, diag_py)
    on = row_on | col_on
    corner_at = jnp.where(on, line_tile, diag_tile)
    corner_lane = jnp.where(on, line_lane, diag_lane)
    corner_shift = (face * 4 + c - corner_lane + LANES) % LANES
    return rows_of(tile, shift, flip, corner_at, corner_shift)


def setup_kernel(plan, chan, shape, edge_ref, corner_ref, weight_ref, table_ref, taps_ref, back_ref, turn):
    table_ref[...] = halo_table(plan, edge_ref, corner_ref, *shape)
    total = weight_ref.shape[2]
    own = lax.axis_index("ch") * chan
    shift = (total - own) % total
    for i in range(3):
        for j in range(3):
            turn[...] = weight_ref[i, j].astype(jnp.float32)
            rows = pltpu.roll(turn[pl.ds(pl.multiple_of(own, chan), chan)], shift, 1)
            cols = slice(j * total, (j + 1) * total)
            taps_ref[i * chan : (i + 1) * chan, cols] = rows.astype(jnp.bfloat16)
            turn[...] = turn[...].T
            rows = pltpu.roll(turn[pl.ds(pl.multiple_of(own, chan), chan)], shift, 1)
            cols = slice((2 - j) * total, (3 - j) * total)
            back_ref[(2 - i) * chan : (3 - i) * chan, cols] = rows.astype(jnp.bfloat16)


def setup(plan, edge_table, corner_table, weight, chan, counts, col_len, unit):
    edges = jnp.transpose(edge_table, (2, 1, 0))
    corners = jnp.transpose(corner_table, (1, 2, 0))
    total = weight.shape[2]
    vmem = pl.BlockSpec(memory_space=pltpu.VMEM)
    taps = jax.ShapeDtypeStruct((3 * chan, 3 * total), jnp.bfloat16)
    table = jax.ShapeDtypeStruct((12 * (RB // unit) + 8, edges.shape[2]), jnp.int32)
    return pl.pallas_call(
        lambda *refs: setup_kernel(plan, chan, (*counts, col_len, unit), *refs),
        in_specs=[vmem] * 3,
        out_specs=[vmem] * 3,
        out_shape=[table, taps, taps],
        scratch_shapes=[pltpu.VMEM((total, total), jnp.float32)],
        compiler_params=pltpu.CompilerParams(vmem_limit_bytes=VMEM_LIMIT),
        name="setup",
    )(edges, corners, weight)


def from_others(array, ch_count):
    return [array] + [
        lax.ppermute(array, "ch", [((i + k) % ch_count, i) for i in range(ch_count)])
        for k in range(1, ch_count)
    ]


class Place:
    @staticmethod
    def place():
        return (lax.axis_index("px"), lax.axis_index("py"))


class SquareHalo(Place):
    counts = (2, 1, 1, 2)

    def __init__(self, quads):
        self.quads = quads

    def corner_shape(self, chan):
        return (16, chan // 2, LANES)

    def pack_corners(self, corners):
        half = corners.shape[0] // 2
        return corners[:half] + pltpu.roll(corners[half:], LANES // 2, 1)

    def unpack_corners(self, packed):
        upper = packed.astype(jnp.float32)
        both = jnp.concatenate([upper, pltpu.roll(upper, LANES // 2, 1)], axis=0)
        return both.astype(jnp.bfloat16)

    def roles(self):
        row_pos, col_pos = self.place()
        px_end = (row_pos == 0) | (row_pos == 3)
        py_end = (col_pos == 0) | (col_pos == 3)
        side = jnp.where(
            py_end, jnp.where(col_pos == 0, 0, 1), jnp.where(row_pos == 0, 2, 3)
        )
        corner = px_end & py_end
        middle = (px_end | py_end) & jnp.logical_not(corner)
        return (px_end, corner, middle, side, jnp.where(px_end, col_pos, row_pos))

    def chosen_sides(self):
        row_pos, col_pos = self.place()
        px_end, corner, middle, side, seg = self.roles()
        row_line = jnp.where(col_pos == 0, 0, 1)
        col_line = jnp.where(row_pos == 0, 2, 3)
        to_px, to_py = (jnp.where(row_pos == 1, 3, 2), jnp.where(col_pos == 1, 1, 0))
        facing = jnp.where(px_end, to_py, to_px)
        return [
            jnp.where(seg == 1, side, facing),
            jnp.where(seg == 1, facing, side),
            jnp.where(row_pos % 2 == 0, 3, 2),
            jnp.where(col_pos % 2 == 0, 1, 0),
            jnp.where(corner, row_line, jnp.where(middle, side, to_py)),
            jnp.where(corner, col_line, side),
        ]

    def exchange(self, pair, col_side, row_side, lines, corner):
        every = [(x, y) for x in range(4) for y in range(4)]
        axes = ("px", "py")
        swap = lambda array, pairs: lax.ppermute(
            array, axes, [(a[0] * 4 + a[1], b[0] * 4 + b[1]) for a, b in pairs]
        )
        ends = (0, 3)
        corners = [(x, y) for x in ends for y in ends]
        spot = lambda side, seg: ((seg, 0), (seg, 3), (0, seg), (3, seg))[side]
        beside = [(spot(side, k), spot(side, 3 - k)) for side in range(4) for k in (1, 2)]
        beside += [((x, y), (3 - x, y)) for x in (1, 2) for y in (1, 2)]
        paired = swap(pair, beside)
        near_col = swap(col_side, [((x, y), (x ^ 1, y)) for x, y in every])
        near_row = swap(row_side, [((x, y), (x, y ^ 1)) for x, y in every])
        _, _, middle, _, seg = self.roles()
        slot = lax.broadcasted_iota(jnp.int32, (2 * self.quads, 1, 1), 0) // self.quads
        lines = jnp.where(middle & (slot != seg - 1), paired, lines)
        across = []
        for j in (1, 2, 3):
            pairs = [(spot(side, k), spot(side ^ j, k)) for side in range(4) for k in (1, 2)]
            pairs += [(corners[c], corners[c ^ j]) for c in range(4)]
            if j == 1:
                pairs += [((x, y), (x, 3 - y)) for x in (1, 2) for y in (1, 2)]
            across.append(swap(lines, pairs))
        ends_of = lax.all_to_all(corner, axes, 0, 0, tiled=True)
        return [lines, *across, paired, near_col, near_row, ends_of]

    def strip_cell(self, g, s, at):
        row_pos, col_pos = self.place()
        _, corner, _, side, _ = self.roles()
        slot = 2 * self.quads
        k = at // RB
        me = jnp.where(row_pos > 0, 2, 0) + jnp.where(col_pos > 0, 1, 0)
        far = jnp.where(k > 0, 1, 0)
        owner = jnp.where(s < 2, 2 * far + s, 2 * (s - 2) + far)
        at_corner = (me ^ owner) * slot + (s // 2) * self.quads
        at_middle = (side ^ s) * slot + (k - 1) * self.quads
        return (jnp.where(corner, at_corner, at_middle) + g // GROUP, (g % GROUP) * 32)

    def near_cell(self, edge, face):
        row_pos, col_pos = self.place()
        px_end, _, _, _, seg = self.roles()
        slot = 2 * self.quads
        paired = 4 * slot + (seg - 1) * self.quads
        near_col, near_row = (5 * slot, 5 * slot + self.quads)
        by_col = jnp.where(row_pos % 2 == 3 - edge, near_col, paired)
        by_row = jnp.where(col_pos % 2 == 1 - edge, near_row, jnp.where(px_end, paired, slot))
        return jnp.where(edge < 2, by_row, by_col) + face // GROUP

    def corner_cell(self, g, s, at):
        seg, hi = (at // RB, jnp.where(at % RB == 0, 0, 1))
        owner = jnp.where(s < 2, seg * 4 + 3 * s, 12 * (s - 2) + seg)
        q = jnp.where(s < 2, 2 * s + hi, s - 2 + 2 * hi)
        return (12 * self.quads + owner, g * 4 + q)

    def diagonal_cell(self, face, q, px, py):
        return (12 * self.quads + px * 4 + py, face * 4 + q)


class GatheredHalo(Place):
    counts = (1, 1, 1, 1, 2)

    def corner_shape(self, chan):
        return (1, chan, LANES)

    def pack_corners(self, corners):
        return corners

    def unpack_corners(self, packed):
        return packed

    def __init__(self, quads, px_count, py_count, col_len):
        self.quads = quads
        self.size = (px_count, py_count)
        self.col_len = col_len

    def chosen_sides(self):
        row_pos, col_pos = self.place()
        return [0, 1, 2, 3, jnp.where(col_pos == 0, 0, 1), jnp.where(row_pos == 0, 2, 3)]

    def exchange(self, top, bottom, left, right, lines, corner):
        px_count, py_count = self.size
        up = lambda n: [(i, i + 1) for i in range(n - 1)]
        down = lambda n: [(i + 1, i) for i in range(n - 1)]
        return [
            lax.ppermute(bottom, "py", up(py_count)),
            lax.ppermute(top, "py", down(py_count)),
            lax.ppermute(right, "px", up(px_count)),
            lax.ppermute(left, "px", down(px_count)),
            lax.all_gather(lines, ("px", "py"), axis=0, tiled=True),
            lax.all_gather(corner, ("px", "py"), axis=0, tiled=True),
        ]

    def strip_cell(self, g, s, at):
        px_count, py_count = self.size
        length = jnp.where(s < 2, RB, self.col_len)
        seg = at // length
        px = jnp.where(s < 2, seg, (s - 2) * (px_count - 1))
        py = jnp.where(s < 2, s * (py_count - 1), seg)
        tile = (4 + (px * py_count + py) * 2 + s // 2) * self.quads + g // GROUP
        return (tile, (g % GROUP) * 32 + at % length)

    def near_cell(self, edge, face):
        return edge * self.quads + face // GROUP

    def corner_cell(self, g, s, at):
        return self.strip_cell(g, s, at)

    def diagonal_cell(self, face, q, px, py):
        px_count, py_count = self.size
        base = (4 + 2 * px_count * py_count) * self.quads
        return (base + px * py_count + py, face * 4 + q)


def local(features, cotangent, weight, edge_table, corner_table):
    chan, faces = features.shape[:2]
    tile = features.shape[4]
    col_len = tile // RB
    unit = min(RB, col_len)
    units = (RB // unit, RB // unit, col_len // unit, col_len // unit)
    px_count, py_count, ch_count = [lax.axis_size(name) for name in ("px", "py", "ch")]
    ring = jnp.asarray(ring_matrix(col_len), jnp.bfloat16)
    cornsel = jnp.asarray(corner_matrix(), jnp.bfloat16)
    spread = jnp.asarray(spread_matrix(col_len), jnp.bfloat16)
    rev = jnp.asarray(reverse_matrix(unit), jnp.bfloat16)
    if px_count == py_count == 4 and col_len == RB and chan % 32 == 0:
        plan = SquareHalo(faces // GROUP)
    else:
        plan = GatheredHalo(faces // GROUP, px_count, py_count, col_len)

    feats = jnp.transpose(features.reshape(chan, faces, tile), (1, 0, 2))
    cot = jnp.transpose(cotangent.reshape(chan, faces, tile), (1, 0, 2))
    fields = from_others(feats, ch_count)
    parts = rings_of(feats, plan, ring, cornsel)
    table, taps, back_taps = setup(
        plan, edge_table, corner_table, weight, chan, (px_count, py_count), col_len, unit
    )
    tiles = plan.exchange(*parts)
    halo = assemble_halo(plan, table, tiles, rev, faces, units, unit)
    halos = from_others(halo, ch_count)
    old, chunks, first = ([], [], 0)
    for count in CALLS:
        act, gated, *parts = forward(
            first, count, plan, fields, halos, cot, taps, spread, ring, cornsel, old
        )
        old = [*parts, act]
        chunks.append((first, from_others(gated, ch_count)))
        first += count

    tiles = plan.exchange(*parts)
    halo = assemble_halo(plan, table, tiles, rev, faces, units, unit)
    halos = from_others(halo, ch_count)
    grad = None
    for first, fields in chunks:
        grad = backward(first, faces, fields, halos, back_taps, spread, grad)

    shape = (chan, faces, 1, 1, tile)
    return (
        jnp.transpose(act, (1, 0, 2)).reshape(shape),
        jnp.transpose(grad, (1, 0, 2)).reshape(shape),
    )


def solution(mesh):
    spec = P("ch", None, "py", "px", None)
    return jax.shard_map(
        local,
        mesh=mesh,
        in_specs=(spec, spec, P(), P(), P()),
        out_specs=(spec, spec),
        check_vma=False,
    )
```
